32 devices in a mesh: group: 4 (over y, x), resp: 8 (over z, core).
Axes of the slice: x: 2, y: 2, z: 4, core: 2. Of those that a mesh axis runs over, the one named last changes fastest.
Arguments:
- prompt_hidden: bfloat16 [4, 512, 5120], P('group', 'resp'), may hold values from -48 to 48
- key_matrix: bfloat16 [5120, 512], P('group'), may hold values from -0.078125 to 0.078125
- key_gain: float32 [128], replicated, may hold values from 0.25 to 1.75
- prompt_token_value: bfloat16 [4, 512, 512], P('group', 'resp'), may hold values from -6 to 6
- resp_query: bfloat16 [4, 8, 256, 4096], P('group', 'resp'), may hold values from -120 to 120
- resp_key: bfloat16 [4, 8, 256, 512], P('group', 'resp'), may hold values from -4 to 4
- response_value: bfloat16 [4, 8, 256, 512], P('group', 'resp'), may hold values from -6 to 6
- grad_out: bfloat16 [4, 8, 256, 4096], P('group', 'resp'), may hold values from -48 to 48
- resp_length: int32 [4, 8], P('group', 'resp'), may hold values from 64 to 256, as said below
Outputs:
- grad_prompt_hidden: bfloat16 [4, 512, 5120], P('group', 'resp')
- grad_key_weight: float32 [5120, 512], P(('group', 'resp'))
- grad_prompt_value: bfloat16 [4, 512, 512], P('group', 'resp')
- grad_resp_query: bfloat16 [4, 8, 256, 4096], P('group', 'resp')
- grad_resp_key: bfloat16 [4, 8, 256, 512], P('group', 'resp')
- grad_resp_value: bfloat16 [4, 8, 256, 512], P('group', 'resp')
The draws below stay inside these ranges and needn't reach their ends.
Inputs may be any that keep to these rules, and one draw needn't show every extreme that they name: Rows from resp_length to 256 of a response are padding.
All inputs are finite; a program needn't handle non-finite values.
Results may differ from the reference program's by a relative error of at most 0.0067.
Values may be sent and summed in bfloat16 or wider, within the bound.
No kernel may reach another device: no remote copies, remote signals or barrier semaphores. Data moves between devices by JAX's collectives and lax.ppermute only.
A program may use at most 128 MiB of HBM per device.

```python
import math
import jax
import jax.numpy as jnp
from jax import lax

MODEL_WIDTH = 5120
QUERY_HEADS = 32
KEY_VALUE_HEADS = 4
HEAD_SIZE = 128
RESPONSE_ROWS = 256
PROMPT_GROUPS = 4
GROUP_RESPONSES = 8
PROMPT_TOKENS = 512


def key_base(key):
    return jnp.clip(jax.random.normal(key, (PROMPT_GROUPS, GROUP_RESPONSES, RESPONSE_ROWS, KEY_VALUE_HEADS, HEAD_SIZE), jnp.float32), -4.0, 4.0)


def draw_resp_key(key, part):
    key_row_block = key_base(key)
    return key_row_block.reshape(PROMPT_GROUPS, GROUP_RESPONSES, RESPONSE_ROWS, KEY_VALUE_HEADS * HEAD_SIZE).astype(jnp.bfloat16)


def draw_resp_query(key, part):
    key = jax.random.fold_in(key, 7)
    query_rows = jnp.clip(jax.random.normal(key, (PROMPT_GROUPS, GROUP_RESPONSES, RESPONSE_ROWS, QUERY_HEADS, HEAD_SIZE), jnp.float32), -4.0, 4.0)
    return query_rows.reshape(PROMPT_GROUPS, GROUP_RESPONSES, RESPONSE_ROWS, QUERY_HEADS * HEAD_SIZE).astype(jnp.bfloat16)


def draw_prompt_hidden(key, part):
    key = jax.random.fold_in(key, 3)
    first, second = jax.random.split(key, 2)
    full_shape = (PROMPT_GROUPS, PROMPT_TOKENS, MODEL_WIDTH)
    values = jnp.clip(jax.random.normal(first, full_shape, jnp.float32), -4.0, 4.0)
    scales = jnp.exp(jax.random.uniform(second, (PROMPT_GROUPS, PROMPT_TOKENS, 1), jnp.float32, 0.0, math.log(10.0)))
    result = values * scales
    return result.astype(jnp.bfloat16)


def draw_resp_length(key, part):
    key = jax.random.fold_in(key, 9)
    first, second = jax.random.split(key, 2)
    lengths = jax.random.randint(first, (PROMPT_GROUPS * GROUP_RESPONSES,), RESPONSE_ROWS // 4, RESPONSE_ROWS + 1, jnp.int32)
    chosen = jax.random.randint(second, (), 0, PROMPT_GROUPS * GROUP_RESPONSES, jnp.int32)
    lengths = jnp.where(jnp.arange(PROMPT_GROUPS * GROUP_RESPONSES, dtype=jnp.int32) == chosen, RESPONSE_ROWS, lengths)
    return lengths.reshape(PROMPT_GROUPS, GROUP_RESPONSES).astype(jnp.int32)


def levels(own_key, dims, cuts, smallest, largest):
    factor_of, own = 1.0, jax.random.fold_in(own_key, 6)
    for axis_at, shards_of in cuts:
        draws = jnp.exp(jax.random.uniform(jax.random.fold_in(own, axis_at), (shards_of,), jnp.float32, smallest / len(cuts), largest / len(cuts)))
        factor_of = factor_of * jnp.repeat(draws, dims[axis_at] // shards_of).reshape([-1 if axis == axis_at else 1 for axis in range(len(dims))])
    return factor_of


def centred(key, shape, spread, limit, pieces=(), held_as=jnp.bfloat16):
    array = spread * jax.random.normal(key, shape, jnp.float32)
    if pieces:
        array = array * levels(key, shape, pieces, -0.22, 0.18)
    return jnp.clip(array, -limit, limit).astype(held_as)


def setup_inputs(seed: int = 0) -> dict:
    arg_keys = jax.random.split(jax.random.key(seed), 10)
    return {
        "prompt_hidden": draw_prompt_hidden(jax.random.fold_in(arg_keys[9], 71), 0),
        "key_matrix": centred(arg_keys[1], (MODEL_WIDTH, KEY_VALUE_HEADS * HEAD_SIZE), MODEL_WIDTH ** -0.5, 0.078125, ((0, 4),)),
        "key_gain": jnp.clip(1.0 + 0.15 * jax.random.normal(arg_keys[2], (HEAD_SIZE,), jnp.float32), 0.25, 1.75),
        "prompt_token_value": centred(arg_keys[3], (PROMPT_GROUPS, PROMPT_TOKENS, KEY_VALUE_HEADS * HEAD_SIZE), 1.0, 6.0, ((0, 4), (1, 8))),
        "resp_query": draw_resp_query(jax.random.fold_in(arg_keys[9], 71), 0),
        "resp_key": draw_resp_key(jax.random.fold_in(arg_keys[9], 71), 0),
        "response_value": centred(arg_keys[6], (PROMPT_GROUPS, GROUP_RESPONSES, RESPONSE_ROWS, KEY_VALUE_HEADS * HEAD_SIZE), 1.0, 6.0, ((0, 4), (1, 8))),
        "grad_out": centred(arg_keys[7], (PROMPT_GROUPS, GROUP_RESPONSES, RESPONSE_ROWS, QUERY_HEADS * HEAD_SIZE), 8.0, 48.0, ((0, 4), (1, 8))),
        "resp_length": draw_resp_length(jax.random.fold_in(arg_keys[9], 71), 0),
    }


def rms_keys(key_pre, key_gain):
    shaped = key_pre.reshape(key_pre.shape[:-1] + (-1, key_gain.shape[0]))
    inverse = lax.rsqrt(lax.optimization_barrier(jnp.mean(shaped * shaped, axis=-1, keepdims=True)) + 1e-06)
    return (shaped * inverse * key_gain).reshape(key_pre.shape)

def barrier_round(values):
    return lax.optimization_barrier(values.astype(jnp.bfloat16)).astype(jnp.float32)

def attend(query_rows, keys_combined, values_combined, incoming_gradient, length):
    response_rows = query_rows.shape[0]
    key_row_block = keys_combined.shape[0]
    heads_per_group = QUERY_HEADS // KEY_VALUE_HEADS
    queries_float = query_rows.astype(jnp.float32).reshape(response_rows, KEY_VALUE_HEADS, heads_per_group, HEAD_SIZE)
    incoming_float = incoming_gradient.astype(jnp.float32).reshape(response_rows, KEY_VALUE_HEADS, heads_per_group, HEAD_SIZE)
    keys_float = keys_combined.astype(jnp.float32).reshape(key_row_block, KEY_VALUE_HEADS, HEAD_SIZE)
    values_float = values_combined.astype(jnp.float32).reshape(key_row_block, KEY_VALUE_HEADS, HEAD_SIZE)
    scores = jnp.einsum('ikrd,jkd->kirj', queries_float, keys_float) * HEAD_SIZE ** (-0.5)
    index_of_row = jnp.arange(response_rows, dtype=jnp.int32)
    key_index = jnp.arange(key_row_block, dtype=jnp.int32)
    visible = (key_index[None, :] < PROMPT_TOKENS) | (key_index[None, :] - PROMPT_TOKENS <= index_of_row[:, None])
    visible = visible[None, :, None, :]
    masked = jnp.where(visible, scores, -jnp.inf)
    row_max = lax.optimization_barrier(jnp.max(masked, axis=-1, keepdims=True))
    exponent = jnp.where(visible, jnp.exp(masked - row_max), 0.0)
    attn_weights = exponent / lax.optimization_barrier(jnp.sum(exponent, axis=-1, keepdims=True))
    live = (index_of_row < length)[None, :, None, None]
    attn_weights = jnp.where(live, attn_weights, 0.0)
    dprob = jnp.einsum('ikrd,jkd->kirj', incoming_float, values_float)
    row_delta = lax.optimization_barrier(jnp.sum(attn_weights * dprob, axis=-1, keepdims=True))
    dscore = barrier_round(attn_weights * (dprob - row_delta) * HEAD_SIZE ** (-0.5))
    weights_b = barrier_round(attn_weights)
    query_grad = jnp.einsum('kirj,jkd->ikrd', dscore, keys_float).reshape(response_rows, -1)
    key_grad = jnp.einsum('kirj,ikrd->jkd', dscore, queries_float).reshape(key_row_block, -1)
    value_grad = jnp.einsum('kirj,ikrd->jkd', weights_b, incoming_float).reshape(key_row_block, -1)
    return (query_grad, key_grad, value_grad)

def reference(prompt_hidden, key_matrix, key_gain, prompt_token_value, resp_query, resp_key, response_value, grad_out, resp_length):
    key_value_width = KEY_VALUE_HEADS * HEAD_SIZE
    key_pre = jnp.dot(prompt_hidden.reshape(-1, MODEL_WIDTH), key_matrix, preferred_element_type=jnp.float32)
    prompt_key = rms_keys(key_pre, key_gain).astype(jnp.bfloat16).reshape(PROMPT_GROUPS, PROMPT_TOKENS, key_value_width)

    def per_group(carry, items):
        group_keys, group_values, query_rows, keys_resp, values_resp, incoming_gradient, lengths = items

        def per_response(sums, inner):
            query_one, key_one, value_one, upstream_one, length_one = inner
            keys_combined = jnp.concatenate([group_keys, key_one], axis=0)
            values_combined = jnp.concatenate([group_values, value_one], axis=0)
            query_grad, key_grad, value_grad = attend(query_one, keys_combined, values_combined, upstream_one, length_one)
            sums = (sums[0] + key_grad[:PROMPT_TOKENS], sums[1] + value_grad[:PROMPT_TOKENS])
            return (sums, (query_grad.astype(jnp.bfloat16), key_grad[PROMPT_TOKENS:].astype(jnp.bfloat16), value_grad[PROMPT_TOKENS:].astype(jnp.bfloat16)))
        zeros_sum = jnp.zeros((PROMPT_TOKENS, key_value_width), jnp.float32)
        sums, results = lax.scan(per_response, (zeros_sum, zeros_sum), (query_rows, keys_resp, values_resp, incoming_gradient, lengths))
        return (carry, (sums[0], sums[1], results[0], results[1], results[2]))
    start_carry = jnp.zeros((), jnp.float32)
    _, stacked = lax.scan(per_group, start_carry, (prompt_key, prompt_token_value, resp_query, resp_key, response_value, grad_out, resp_length))
    prompt_key_grad, prompt_value_grad, grad_resp_query, grad_resp_key, grad_resp_value = stacked
    _, pullback = jax.vjp(lambda values: rms_keys(values, key_gain), key_pre)
    key_pre_grad = pullback(prompt_key_grad.reshape(-1, key_value_width))[0].astype(jnp.bfloat16)
    grad_prompt_hidden = jnp.dot(key_pre_grad, key_matrix.T, preferred_element_type=jnp.float32).astype(jnp.bfloat16).reshape(PROMPT_GROUPS, PROMPT_TOKENS, MODEL_WIDTH)
    grad_key_weight = jnp.dot(prompt_hidden.reshape(-1, MODEL_WIDTH).T, key_pre_grad, preferred_element_type=jnp.float32)
    return (grad_prompt_hidden, grad_key_weight, prompt_value_grad.astype(jnp.bfloat16), grad_resp_query, grad_resp_key, grad_resp_value)
```

```python
from functools import partial

import jax
import jax.numpy as jnp
from jax import lax
from jax.experimental import pallas as pl
from jax.experimental.pallas import tpu as pltpu
from jax.sharding import PartitionSpec as P

F32, BF16 = jnp.float32, jnp.bfloat16
LOG2E = 1.4426950408889634


def norm_keys(key_pre, key_gain):
    shaped = key_pre.reshape(key_pre.shape[:-1] + (-1, key_gain.shape[0]))
    inverse = lax.rsqrt(jnp.mean(shaped * shaped, axis=-1, keepdims=True) + 1e-06)
    return (shaped * inverse * key_gain).reshape(key_pre.shape)


def dot(left, right, left_dim=1, right_dim=0):
    dims = (((left_dim,), (right_dim,)), ((), ()))
    return lax.dot_general(left, right, dims, preferred_element_type=F32)


def attend_kernel(
    length_ref, query_ref, upstream_ref, prompt_key_ref, prompt_value_ref, key_ref, value_ref,
    query_grad_ref, prompt_key_grad_ref, prompt_value_grad_ref, key_grad_ref, value_grad_ref,
):
    rows = query_ref.shape[0]
    prompt_len, head_dim = prompt_key_ref.shape
    heads = query_ref.shape[1] // head_dim
    scale = head_dim ** -0.5
    keys = jnp.concatenate([prompt_key_ref[...], key_ref[...]], axis=0)
    values = jnp.concatenate([prompt_value_ref[...], value_ref[...]], axis=0)
    keys_t, values_t = keys.T, values.T
    stacked = heads * rows
    live = lax.broadcasted_iota(jnp.int32, (stacked, 1), 0) % rows < length_ref[0, 0]
    own = (stacked, key_ref.shape[0])
    visible = lax.broadcasted_iota(jnp.int32, own, 1) <= lax.broadcasted_iota(jnp.int32, own, 0) % rows

    def head(ref, index):
        return ref[:, index * head_dim : (index + 1) * head_dim]

    queries = jnp.concatenate([head(query_ref, i) for i in range(heads)], axis=0)
    upstream = jnp.concatenate([head(upstream_ref, i) for i in range(heads)], axis=0)
    prompt_scores = dot(queries, keys_t[:, :prompt_len])
    own_scores = jnp.where(visible, dot(queries, keys_t[:, prompt_len:]), -jnp.inf)
    row_max = jnp.maximum(
        jnp.max(prompt_scores, axis=1, keepdims=True), jnp.max(own_scores, axis=1, keepdims=True)
    )
    scores = jnp.concatenate([prompt_scores, own_scores], axis=1)
    unit = scale * LOG2E
    exponent = jnp.exp2(scores * unit - row_max * unit)
    dprob = dot(upstream, values_t)
    total = jnp.sum(exponent, axis=1, keepdims=True)
    weighted = jnp.sum(exponent * dprob, axis=1, keepdims=True)
    inverse = jnp.where(live, 1.0 / total, 0.0)
    row_delta = weighted * inverse
    weights = (exponent * inverse).astype(BF16)
    dscore = (exponent * ((dprob - row_delta) * (inverse * scale))).astype(BF16)
    query_grad = dot(dscore, keys).astype(BF16)
    for i in range(heads):
        query_grad_ref[:, i * head_dim : (i + 1) * head_dim] = query_grad[i * rows : (i + 1) * rows]
    value_grad = dot(upstream.T, weights).T
    key_grad = dot(queries.T, dscore).T
    prompt_key_grad_ref[...] = key_grad[:prompt_len]
    prompt_value_grad_ref[...] = value_grad[:prompt_len]
    key_grad_ref[...] = key_grad[prompt_len:].astype(BF16)
    value_grad_ref[...] = value_grad[prompt_len:].astype(BF16)


def attend(length, queries, upstream, prompt_keys, prompt_values, keys, values, head_dim):
    rows, width = queries.shape
    prompt_len, kv_width = prompt_keys.shape
    kv_heads = kv_width // head_dim

    def block(count, columns):
        return pl.BlockSpec((count, columns), lambda i: (0, i))

    query_block = block(rows, width // kv_heads)
    prompt_block, own_block = block(prompt_len, head_dim), block(rows, head_dim)
    macs = 5 * rows * width * (prompt_len + rows)
    return pl.pallas_call(
        attend_kernel,
        grid=(kv_heads,),
        in_specs=[
            pl.BlockSpec(memory_space=pltpu.SMEM),
            query_block, query_block, prompt_block, prompt_block, own_block, own_block,
        ],
        out_specs=[query_block, prompt_block, prompt_block, own_block, own_block],
        out_shape=[
            jax.ShapeDtypeStruct((rows, width), BF16),
            jax.ShapeDtypeStruct((prompt_len, kv_width), F32),
            jax.ShapeDtypeStruct((prompt_len, kv_width), F32),
            jax.ShapeDtypeStruct((rows, kv_width), BF16),
            jax.ShapeDtypeStruct((rows, kv_width), BF16),
        ],
        compiler_params=pltpu.CompilerParams(vmem_limit_bytes=56 * 2**20),
        cost_estimate=pl.CostEstimate(flops=2 * macs, bytes_accessed=10**7, transcendentals=0),
        name="attend",
    )(length, queries, upstream, prompt_keys, prompt_values, keys, values)


def swap(array, axis, size, distance):
    return lax.ppermute(array, axis, [(i, i ^ distance) for i in range(size)])


def spread(block, size):
    near = [block] + [swap(block, "resp", size, k) for k in range(2, size, 2)]
    near = jnp.concatenate(near, axis=0)
    return jnp.concatenate([near, swap(near, "resp", size, 1)], axis=0)


def collect(sums, size):
    half = sums.shape[0] // 2
    rows = sums.shape[0] // size
    near = sums[:half] + swap(sums[half:], "resp", size, 1)
    total = near[:rows]
    for p in range(1, size // 2):
        total = total + swap(near[p * rows : (p + 1) * rows], "resp", size, 2 * p)
    return total


def shards(
    groups, responses, prompt_hidden, key_matrix, key_gain, prompt_token_value,
    resp_query, resp_key, response_value, grad_out, resp_length,
):
    hidden = prompt_hidden[0]
    tokens = hidden.shape[0]
    depth, kv_width = key_matrix.shape
    head_dim = key_gain.shape[0]
    group, resp = lax.axis_index("group"), lax.axis_index("resp")

    prompt_values = spread(prompt_token_value[0], responses)

    columns, partials = [], []
    for k in range(groups):
        piece = lax.dynamic_slice(hidden, (0, (group ^ k) * depth), (tokens, depth))
        columns.append(swap(piece, "group", groups, k) if k else piece)
        partials.append(dot(columns[k], key_matrix))
    key_pre = partials[0]
    for k in range(1, groups):
        key_pre = key_pre + swap(partials[k], "group", groups, k)
    prompt_key = norm_keys(key_pre, key_gain).astype(BF16)
    prompt_keys = spread(prompt_key, responses)

    chips = responses // 2
    chip_rows = depth // chips
    hidden_t = jnp.concatenate(columns, axis=0).T
    taken = []
    for k in range(0, responses, 2):
        piece = lax.dynamic_slice(
            hidden_t, (((resp ^ k) // 2) * chip_rows, 0), (chip_rows, hidden_t.shape[1])
        )
        taken.append(swap(piece, "resp", responses, k) if k else piece)

    weight = lax.all_gather(key_matrix, "group", axis=0, tiled=True)

    query_grad, key_sums, value_sums, key_grad, value_grad = attend(
        resp_length, resp_query[0, 0], grad_out[0, 0], prompt_keys, prompt_values,
        resp_key[0, 0], response_value[0, 0], head_dim,
    )
    prompt_key_grad = collect(key_sums, responses)
    _, pullback = jax.vjp(lambda values: norm_keys(values, key_gain), key_pre)
    key_pre_grad = pullback(prompt_key_grad)[0].astype(BF16)

    near = [key_pre_grad] + [swap(key_pre_grad, "resp", responses, k) for k in range(2, responses, 2)]
    near = jnp.stack(near, axis=0)
    partial_weight = 0.0
    for k in range(groups):
        block = swap(near, "group", groups, k) if k else near
        for p in range(chips):
            partial_weight += dot(taken[p][:, k * tokens : (k + 1) * tokens], block[p])
    half = chip_rows // 2
    core = resp % 2
    mine = lax.dynamic_slice(partial_weight, (core * half, 0), (half, kv_width))
    other = lax.dynamic_slice(partial_weight, ((1 - core) * half, 0), (half, kv_width))
    grad_weight = mine + swap(other, "resp", responses, 1)

    prompt_value_grad = collect(value_sums, responses)
    grad_hidden = dot(key_pre_grad, weight, 1, 1).astype(BF16)
    return (
        grad_hidden[None],
        grad_weight,
        prompt_value_grad.astype(BF16)[None],
        query_grad[None, None],
        key_grad[None, None],
        value_grad[None, None],
    )


def solution(mesh):
    return jax.shard_map(
        partial(shards, mesh.shape["group"], mesh.shape["resp"]),
        mesh=mesh,
        in_specs=(
            P("group", "resp", None),
            P("group", None),
            P(),
            P("group", "resp", None),
            P("group", "resp", None, None),
            P("group", "resp", None, None),
            P("group", "resp", None, None),
            P("group", "resp", None, None),
            P("group", "resp"),
        ),
        out_specs=(
            P("group", "resp", None),
            P(("group", "resp"), None),
            P("group", "resp", None),
            P("group", "resp", None, None),
            P("group", "resp", None, None),
            P("group", "resp", None, None),
        ),
        check_vma=False,
    )
```

```python
from functools import partial

import jax
import jax.numpy as jnp
from jax import lax
from jax.experimental import pallas as pl
from jax.experimental.pallas import tpu as pltpu
from jax.sharding import PartitionSpec as P

F32, BF16 = jnp.float32, jnp.bfloat16
LOG2E = 1.4426950408889634
PARAMS = pltpu.CompilerParams(vmem_limit_bytes=56 * 2**20)


def norm_keys(key_pre, key_gain):
    shaped = key_pre.reshape(key_pre.shape[:-1] + (-1, key_gain.shape[0]))
    inverse = lax.rsqrt(jnp.mean(shaped * shaped, axis=-1, keepdims=True) + 1e-06)
    return (shaped * inverse * key_gain).reshape(key_pre.shape)


def dot(left, right, left_dim=1, right_dim=0):
    dims = (((left_dim,), (right_dim,)), ((), ()))
    return lax.dot_general(left, right, dims, preferred_element_type=F32)


def cost(macs, nbytes):
    return pl.CostEstimate(flops=2 * macs, bytes_accessed=nbytes, transcendentals=0)


def stack_heads(ref, head_dim):
    heads = ref.shape[1] // head_dim
    return jnp.concatenate([ref[:, i * head_dim : (i + 1) * head_dim] for i in range(heads)], axis=0)


def score_kernel(pieces, length_ref, query_ref, upstream_ref, key_ref, value_ref, *refs):
    key_pieces, value_pieces = refs[:pieces], refs[pieces : 2 * pieces]
    weights_ref, dscore_ref, near_ref, far_ref, key_grad_ref = refs[2 * pieces :]
    rows = query_ref.shape[0]
    own_len, head_dim = key_ref.shape
    scale = head_dim ** -0.5
    keys_t = jnp.concatenate([ref[...] for ref in key_pieces] + [key_ref[...]], axis=0).T
    values_t = jnp.concatenate([ref[...] for ref in value_pieces] + [value_ref[...]], axis=0).T
    prompt_len = keys_t.shape[1] - own_len
    queries, upstream = stack_heads(query_ref, head_dim), stack_heads(upstream_ref, head_dim)
    stacked = queries.shape[0]
    live = lax.broadcasted_iota(jnp.int32, (stacked, 1), 0) % rows < length_ref[0, 0]
    own = (stacked, own_len)
    visible = lax.broadcasted_iota(jnp.int32, own, 1) <= lax.broadcasted_iota(jnp.int32, own, 0) % rows
    prompt_scores = dot(queries, keys_t[:, :prompt_len])
    own_scores = jnp.where(visible, dot(queries, keys_t[:, prompt_len:]), -jnp.inf)
    row_max = jnp.maximum(
        jnp.max(prompt_scores, axis=1, keepdims=True), jnp.max(own_scores, axis=1, keepdims=True)
    )
    scores = jnp.concatenate([prompt_scores, own_scores], axis=1)
    unit = scale * LOG2E
    exponent = jnp.exp2(scores * unit - row_max * unit)
    dprob = dot(upstream, values_t)
    total = jnp.sum(exponent, axis=1, keepdims=True)
    weighted = jnp.sum(exponent * dprob, axis=1, keepdims=True)
    inverse = jnp.where(live, 1.0 / total, 0.0)
    row_delta = weighted * inverse
    weights_ref[0] = (exponent * inverse).astype(BF16)
    dscore = (exponent * ((dprob - row_delta) * (inverse * scale))).astype(BF16)
    dscore_ref[0] = dscore
    key_grad = dot(queries.T, dscore).T
    near_ref[...] = key_grad[: prompt_len // 2]
    far_ref[...] = key_grad[prompt_len // 2 : prompt_len]
    key_grad_ref[...] = key_grad[prompt_len:].astype(BF16)


def column_block(rows, columns):
    return pl.BlockSpec((rows, columns), lambda i: (0, i))


def head_block(*shape):
    return pl.BlockSpec((1,) + shape, lambda i: (i, 0, 0))


def score_pass(length, queries, upstream, key_pieces, value_pieces, keys, values, head_dim):
    rows, width = queries.shape
    kv_width = keys.shape[1]
    kv_heads = kv_width // head_dim
    stacked = rows * width // kv_width
    prompt_len = sum(piece.shape[0] for piece in key_pieces)
    every = prompt_len + rows
    query_block, own_block = column_block(rows, width // kv_heads), column_block(rows, head_dim)
    piece_blocks = [column_block(piece.shape[0], head_dim) for piece in key_pieces]
    half_block = column_block(prompt_len // 2, head_dim)
    pair = jax.ShapeDtypeStruct((kv_heads, stacked, every), BF16)
    half = jax.ShapeDtypeStruct((prompt_len // 2, kv_width), F32)
    return pl.pallas_call(
        partial(score_kernel, len(key_pieces)),
        grid=(kv_heads,),
        in_specs=[
            pl.BlockSpec(memory_space=pltpu.SMEM), query_block, query_block, own_block, own_block,
            *piece_blocks, *piece_blocks,
        ],
        out_specs=[head_block(stacked, every)] * 2 + [half_block] * 2 + [own_block],
        out_shape=[pair, pair, half, half, jax.ShapeDtypeStruct((rows, kv_width), BF16)],
        compiler_params=PARAMS,
        cost_estimate=cost(6 * rows * width * every, 2 * 10**7),
        name="scores",
    )(length, queries, upstream, keys, values, *key_pieces, *value_pieces)


def value_kernel(upstream_ref, weights_ref, near_ref, far_ref, value_grad_ref):
    half, head_dim = near_ref.shape
    upstream = stack_heads(upstream_ref, head_dim)
    value_grad = dot(upstream.T, weights_ref[0]).T
    near_ref[...] = value_grad[:half]
    far_ref[...] = value_grad[half : 2 * half]
    value_grad_ref[...] = value_grad[2 * half :].astype(BF16)


def value_pass(upstream, weights, head_dim):
    rows, width = upstream.shape
    kv_heads, stacked, every = weights.shape
    kv_width = kv_heads * head_dim
    half = (every - rows) // 2
    out = jax.ShapeDtypeStruct((half, kv_width), F32)
    return pl.pallas_call(
        value_kernel,
        grid=(kv_heads,),
        in_specs=[column_block(rows, width // kv_heads), head_block(stacked, every)],
        out_specs=[column_block(half, head_dim)] * 2 + [column_block(rows, head_dim)],
        out_shape=[out, out, jax.ShapeDtypeStruct((rows, kv_width), BF16)],
        compiler_params=PARAMS,
        cost_estimate=cost(rows * width * every, 1 * 10**7),
        name="value_grads",
    )(upstream, weights)


def query_kernel(dscore_ref, key_ref, *refs):
    key_pieces, query_grad_ref = refs[:-1], refs[-1]
    rows, head_dim = query_grad_ref.shape[0], key_ref.shape[1]
    keys = jnp.concatenate([ref[...] for ref in key_pieces] + [key_ref[...]], axis=0)
    query_grad = dot(dscore_ref[0], keys).astype(BF16)
    for i in range(query_grad_ref.shape[1] // head_dim):
        query_grad_ref[:, i * head_dim : (i + 1) * head_dim] = query_grad[i * rows : (i + 1) * rows]


def query_pass(dscore, key_pieces, keys, head_dim):
    kv_heads, stacked, every = dscore.shape
    rows, kv_width = keys.shape
    width = stacked // rows * kv_width
    return pl.pallas_call(
        query_kernel,
        grid=(kv_heads,),
        in_specs=[head_block(stacked, every)]
        + [column_block(piece.shape[0], head_dim) for piece in [keys] + key_pieces],
        out_specs=column_block(rows, width // kv_heads),
        out_shape=jax.ShapeDtypeStruct((rows, width), BF16),
        compiler_params=PARAMS,
        cost_estimate=cost(rows * width * every, 1 * 10**7),
        name="query_grads",
    )(dscore, keys, *key_pieces)


def hidden_kernel(groups, place_ref, grad_ref, own_ref, *refs):
    near, far, out_ref = refs[: groups - 1], refs[groups - 1 : -1], refs[-1]
    group, core = place_ref[0], place_ref[1]
    depth = own_ref.shape[0]
    half = near[0].shape[1]
    near_grad = grad_ref[:, pl.ds(pl.multiple_of(core * half, half), half)]
    far_grad = grad_ref[:, pl.ds(pl.multiple_of((1 - core) * half, half), half)]
    for k in range(groups):
        if k:
            block = dot(near_grad, near[k - 1][...], 1, 1) + dot(far_grad, far[k - 1][...], 1, 1)
        else:
            block = dot(grad_ref[...], own_ref[...], 1, 1)
        start = pl.multiple_of((group ^ k) * depth, depth)
        out_ref[:, pl.ds(start, depth)] = block.astype(BF16)


def hidden_pass(place, key_pre_grad, own, near, far):
    tokens, kv_width = key_pre_grad.shape
    groups = len(near) + 1
    width = groups * own.shape[0]
    return pl.pallas_call(
        partial(hidden_kernel, groups),
        in_specs=[pl.BlockSpec(memory_space=pltpu.SMEM)]
        + [pl.BlockSpec(memory_space=pltpu.VMEM)] * (2 * groups),
        out_specs=pl.BlockSpec(memory_space=pltpu.VMEM),
        out_shape=jax.ShapeDtypeStruct((tokens, width), BF16),
        compiler_params=PARAMS,
        cost_estimate=cost(tokens * width * kv_width, 6 * 10**6),
        name="hidden_grad",
    )(place, key_pre_grad, own, *near, *far)


def weight_kernel(chips, place_ref, *refs):
    taken, blocks = refs[:chips], refs[chips:-3]
    mine_ref, other_ref, product = refs[-3:]
    half = mine_ref.shape[0]
    core = place_ref[1]
    columns = jnp.concatenate([ref[...] for ref in taken], axis=1)
    grads = jnp.concatenate([ref[p] for p in range(chips) for ref in blocks], axis=0)
    product[...] = dot(columns, grads)
    mine_ref[...] = product[pl.ds(pl.multiple_of(core * half, 8), half)]
    other_ref[...] = product[pl.ds(pl.multiple_of((1 - core) * half, 8), half)]


def weight_pass(place, taken, blocks):
    rows = taken[0].shape[0]
    kv_width = blocks[0].shape[-1]
    out = jax.ShapeDtypeStruct((rows // 2, kv_width), F32)
    return pl.pallas_call(
        partial(weight_kernel, len(taken)),
        in_specs=[pl.BlockSpec(memory_space=pltpu.SMEM)]
        + [pl.BlockSpec(memory_space=pltpu.VMEM)] * (len(taken) + len(blocks)),
        out_specs=[pl.BlockSpec(memory_space=pltpu.VMEM)] * 2,
        out_shape=[out, out],
        scratch_shapes=[pltpu.VMEM((rows, kv_width), F32)],
        compiler_params=PARAMS,
        cost_estimate=cost(rows * kv_width * taken[0].shape[1] * len(taken), 3 * 10**6),
        name="weight_grad",
    )(place, *taken, *blocks)


def swap(array, axis, size, distance):
    return lax.ppermute(array, axis, [(i, i ^ distance) for i in range(size)])


def after(array, *others):
    return lax.optimization_barrier((array, *others))[0]


def spread_near(block, size):
    return [block] + [swap(block, "resp", size, k) for k in range(2, size, 2)]


def spread_far(near, size):
    return [swap(piece, "resp", size, 1) for piece in near]


def collect(near, far, size):
    near = near + swap(far, "resp", size, 1)
    rows = near.shape[0] // (size // 2)
    total = near[:rows]
    for p in range(1, size // 2):
        total = total + swap(near[p * rows : (p + 1) * rows], "resp", size, 2 * p)
    return total


def shards(
    groups, responses, prompt_hidden, key_matrix, key_gain, prompt_token_value,
    resp_query, resp_key, response_value, grad_out, resp_length,
):
    hidden = prompt_hidden[0]
    tokens = hidden.shape[0]
    depth, kv_width = key_matrix.shape
    head_dim = key_gain.shape[0]
    group, resp = lax.axis_index("group"), lax.axis_index("resp")
    core = resp % 2
    place = jnp.stack([group, core]).astype(jnp.int32)

    columns = []
    for k in range(groups):
        piece = lax.dynamic_slice(hidden, (0, (group ^ k) * depth), (tokens, depth))
        columns.append(swap(piece, "group", groups, k) if k else piece)
    partials = [dot(piece, key_matrix) for piece in columns]
    key_pre = partials[0]
    for k in range(1, groups):
        key_pre = key_pre + swap(partials[k], "group", groups, k)
    value_near = spread_near(prompt_token_value[0], responses)
    value_pieces = value_near + spread_far(value_near, responses)

    prompt_key = norm_keys(key_pre, key_gain).astype(BF16)
    key_near = spread_near(prompt_key, responses)
    key_pieces = key_near + spread_far(key_near, responses)

    chips = responses // 2
    chip_rows = depth // chips
    hidden_t = jnp.concatenate(columns, axis=0).T
    hidden_t = after(hidden_t, *key_near)
    taken = []
    for k in range(0, responses, 2):
        start = ((resp ^ k) // 2) * chip_rows
        piece = lax.dynamic_slice(hidden_t, (start, 0), (chip_rows, hidden_t.shape[1]))
        taken.append(swap(piece, "resp", responses, k) if k else piece)

    half_width = kv_width // 2
    half_weight = lax.dynamic_slice(key_matrix, (0, core * half_width), (depth, half_width))
    half_weight = after(half_weight, key_pre)
    weight_near = [swap(half_weight, "group", groups, k) for k in range(1, groups)]

    queries, upstream = resp_query[0, 0], grad_out[0, 0]
    weights, dscore, near, far, key_grad = score_pass(
        resp_length, queries, upstream, key_pieces, value_pieces,
        resp_key[0, 0], response_value[0, 0], head_dim,
    )
    prompt_key_grad = collect(near, far, responses)
    _, pullback = jax.vjp(lambda values: norm_keys(values, key_gain), key_pre)
    key_pre_grad = pullback(prompt_key_grad)[0].astype(BF16)

    value_near, value_far, value_grad = value_pass(upstream, weights, head_dim)
    query_grad = query_pass(dscore, key_pieces, resp_key[0, 0], head_dim)

    block = jnp.stack(spread_near(key_pre_grad, responses), axis=0)
    blocks = [block] + [swap(block, "group", groups, k) for k in range(1, groups)]
    mine, other = weight_pass(place, taken, blocks)
    grad_weight = mine + swap(other, "resp", responses, 1)

    weight_far = [swap(piece, "resp", responses, 1) for piece in weight_near]
    grad_hidden = hidden_pass(place, key_pre_grad, key_matrix, weight_near, weight_far)
    prompt_value_grad = collect(value_near, value_far, responses)
    return (
        grad_hidden[None],
        grad_weight,
        prompt_value_grad.astype(BF16)[None],
        query_grad[None, None],
        key_grad[None, None],
        value_grad[None, None],
    )


def solution(mesh):
    return jax.shard_map(
        partial(shards, mesh.shape["group"], mesh.shape["resp"]),
        mesh=mesh,
        in_specs=(
            P("group", "resp", None),
            P("group", None),
            P(),
            P("group", "resp", None),
            P("group", "resp", None, None),
            P("group", "resp", None, None),
            P("group", "resp", None, None),
            P("group", "resp", None, None),
            P("group", "resp"),
        ),
        out_specs=(
            P("group", "resp", None),
            P(("group", "resp"), None),
            P("group", "resp", None),
            P("group", "resp", None, None),
            P("group", "resp", None, None),
            P("group", "resp", None, None),
        ),
        check_vma=False,
    )
```

```python
from functools import partial

import jax
import jax.numpy as jnp
from jax import lax
from jax.experimental import pallas as pl
from jax.experimental.pallas import tpu as pltpu
from jax.sharding import PartitionSpec as P

F32, BF16 = jnp.float32, jnp.bfloat16
LOG2E = 1.4426950408889634
PARAMS = pltpu.CompilerParams(vmem_limit_bytes=56 * 2**20)


def norm_keys(key_pre, key_gain):
    shaped = key_pre.reshape(key_pre.shape[:-1] + (-1, key_gain.shape[0]))
    inverse = lax.rsqrt(jnp.mean(shaped * shaped, axis=-1, keepdims=True) + 1e-06)
    return (shaped * inverse * key_gain).reshape(key_pre.shape)


def dot(left, right, left_dim=1, right_dim=0):
    dims = (((left_dim,), (right_dim,)), ((), ()))
    return lax.dot_general(left, right, dims, preferred_element_type=F32)


def cost(macs, nbytes):
    return pl.CostEstimate(flops=2 * macs, bytes_accessed=nbytes, transcendentals=0)


def stack_heads(ref, head_dim):
    heads = ref.shape[1] // head_dim
    return jnp.concatenate([ref[:, i * head_dim : (i + 1) * head_dim] for i in range(heads)], axis=0)


def attend_kernel(pieces, chained, length_ref, query_ref, upstream_ref, key_ref, value_ref, *refs):
    key_pieces, value_pieces = refs[:pieces], refs[pieces : 2 * pieces]
    query_grad_ref, key_grad_ref, value_grad_ref, *halves = refs[2 * pieces + 3 * chained :]
    key_near_ref, key_far_ref, value_near_ref, value_far_ref = halves
    rows = query_ref.shape[0]
    own_len, head_dim = key_ref.shape
    heads = query_ref.shape[1] // head_dim
    scale = head_dim ** -0.5
    keys = jnp.concatenate([ref[...] for ref in key_pieces] + [key_ref[...]], axis=0)
    values = jnp.concatenate([ref[...] for ref in value_pieces] + [value_ref[...]], axis=0)
    keys_t, values_t = keys.T, values.T
    prompt_len = keys.shape[0] - own_len
    queries, upstream = stack_heads(query_ref, head_dim), stack_heads(upstream_ref, head_dim)
    stacked = heads * rows
    live = lax.broadcasted_iota(jnp.int32, (stacked, 1), 0) % rows < length_ref[0, 0]
    own = (stacked, own_len)
    visible = lax.broadcasted_iota(jnp.int32, own, 1) <= lax.broadcasted_iota(jnp.int32, own, 0) % rows
    prompt_scores = dot(queries, keys_t[:, :prompt_len])
    own_scores = jnp.where(visible, dot(queries, keys_t[:, prompt_len:]), -jnp.inf)
    row_max = jnp.maximum(
        jnp.max(prompt_scores, axis=1, keepdims=True), jnp.max(own_scores, axis=1, keepdims=True)
    )
    scores = jnp.concatenate([prompt_scores, own_scores], axis=1)
    unit = scale * LOG2E
    exponent = jnp.exp2(scores * unit - row_max * unit)
    dprob = dot(upstream, values_t)
    total = jnp.sum(exponent, axis=1, keepdims=True)
    weighted = jnp.sum(exponent * dprob, axis=1, keepdims=True)
    inverse = jnp.where(live, 1.0 / total, 0.0)
    row_delta = weighted * inverse
    weights = (exponent * inverse).astype(BF16)
    dscore = (exponent * ((dprob - row_delta) * (inverse * scale))).astype(BF16)
    query_grad = dot(dscore, keys).astype(BF16)
    for i in range(heads):
        query_grad_ref[:, i * head_dim : (i + 1) * head_dim] = query_grad[i * rows : (i + 1) * rows]
    key_grad = dot(queries.T, dscore).T
    value_grad = dot(upstream.T, weights).T
    half = prompt_len // 2
    key_near_ref[...], key_far_ref[...] = key_grad[:half], key_grad[half:prompt_len]
    value_near_ref[...], value_far_ref[...] = value_grad[:half], value_grad[half:prompt_len]
    key_grad_ref[...] = key_grad[prompt_len:].astype(BF16)
    value_grad_ref[...] = value_grad[prompt_len:].astype(BF16)


def attend(length, queries, upstream, key_pieces, value_pieces, keys, values, head_dim, first, count, earlier):
    rows, width = queries.shape
    kv_width = keys.shape[1]
    kv_heads = kv_width // head_dim
    prompt_len = sum(piece.shape[0] for piece in key_pieces)

    def block(rows, columns, offset=first):
        return pl.BlockSpec((rows, columns), lambda i: (0, i + offset))

    query_block, own_block = block(rows, width // kv_heads), block(rows, head_dim)
    piece_blocks = [block(piece.shape[0], head_dim) for piece in key_pieces]
    half = jax.ShapeDtypeStruct((prompt_len // 2, count * head_dim), F32)
    own = jax.ShapeDtypeStruct((rows, kv_width), BF16)
    before = 5 + 2 * len(key_pieces)
    macs = 5 * rows * width * (prompt_len + rows) * count // kv_heads
    return pl.pallas_call(
        partial(attend_kernel, len(key_pieces), bool(earlier)),
        grid=(count,),
        in_specs=[
            pl.BlockSpec(memory_space=pltpu.SMEM), query_block, query_block, own_block, own_block,
            *piece_blocks, *piece_blocks, *[pl.BlockSpec(memory_space=pl.ANY) for _ in earlier],
        ],
        out_specs=[query_block, own_block, own_block] + [block(prompt_len // 2, head_dim, 0)] * 4,
        out_shape=[jax.ShapeDtypeStruct((rows, width), BF16), own, own] + [half] * 4,
        input_output_aliases={before + i: i for i in range(len(earlier))},
        compiler_params=PARAMS,
        cost_estimate=cost(2 * macs, 5 * 10**6),
        name="attend",
    )(length, queries, upstream, keys, values, *key_pieces, *value_pieces, *earlier)


def hidden_kernel(groups, place_ref, grad_ref, own_ref, *refs):
    near, far, out_ref = refs[: groups - 1], refs[groups - 1 : -1], refs[-1]
    group, core = place_ref[0], place_ref[1]
    depth = own_ref.shape[0]
    half = near[0].shape[1]
    near_grad = grad_ref[:, pl.ds(pl.multiple_of(core * half, half), half)]
    far_grad = grad_ref[:, pl.ds(pl.multiple_of((1 - core) * half, half), half)]
    for k in range(groups):
        if k:
            block = dot(near_grad, near[k - 1][...], 1, 1) + dot(far_grad, far[k - 1][...], 1, 1)
        else:
            block = dot(grad_ref[...], own_ref[...], 1, 1)
        start = pl.multiple_of((group ^ k) * depth, depth)
        out_ref[:, pl.ds(start, depth)] = block.astype(BF16)


def hidden_pass(place, key_pre_grad, own, near, far):
    tokens, kv_width = key_pre_grad.shape
    groups = len(near) + 1
    width = groups * own.shape[0]
    return pl.pallas_call(
        partial(hidden_kernel, groups),
        in_specs=[pl.BlockSpec(memory_space=pltpu.SMEM)]
        + [pl.BlockSpec(memory_space=pltpu.VMEM)] * (2 * groups),
        out_specs=pl.BlockSpec(memory_space=pltpu.VMEM),
        out_shape=jax.ShapeDtypeStruct((tokens, width), BF16),
        compiler_params=PARAMS,
        cost_estimate=cost(tokens * width * kv_width, 6 * 10**6),
        name="hidden_grad",
    )(place, key_pre_grad, own, *near, *far)


def weight_kernel(chips, place_ref, *refs):
    taken, blocks = refs[:chips], refs[chips:-3]
    mine_ref, other_ref, product = refs[-3:]
    half = mine_ref.shape[0]
    core = place_ref[1]
    columns = jnp.concatenate([ref[...] for ref in taken], axis=1)
    grads = jnp.concatenate([ref[p] for p in range(chips) for ref in blocks], axis=0)
    product[...] = dot(columns, grads)
    mine_ref[...] = product[pl.ds(pl.multiple_of(core * half, 8), half)]
    other_ref[...] = product[pl.ds(pl.multiple_of((1 - core) * half, 8), half)]


def weight_pass(place, taken, blocks):
    rows = taken[0].shape[0]
    kv_width = blocks[0].shape[-1]
    out = jax.ShapeDtypeStruct((rows // 2, kv_width), F32)
    return pl.pallas_call(
        partial(weight_kernel, len(taken)),
        in_specs=[pl.BlockSpec(memory_space=pltpu.SMEM)]
        + [pl.BlockSpec(memory_space=pltpu.VMEM)] * (len(taken) + len(blocks)),
        out_specs=[pl.BlockSpec(memory_space=pltpu.VMEM)] * 2,
        out_shape=[out, out],
        scratch_shapes=[pltpu.VMEM((rows, kv_width), F32)],
        compiler_params=PARAMS,
        cost_estimate=cost(rows * kv_width * taken[0].shape[1] * len(taken), 3 * 10**6),
        name="weight_grad",
    )(place, *taken, *blocks)


def swap(array, axis, size, distance):
    return lax.ppermute(array, axis, [(i, i ^ distance) for i in range(size)])


def after(array, *others):
    return lax.optimization_barrier((array, *others))[0]


def spread_near(block, size):
    return [block] + [swap(block, "resp", size, k) for k in range(2, size, 2)]


def spread_far(near, size):
    return [swap(piece, "resp", size, 1) for piece in near]


def pair_sum(near, far, size):
    return near + swap(far, "resp", size, 1)


def chip_sum(near, size):
    rows = near.shape[0] // (size // 2)
    total = near[:rows]
    for p in range(1, size // 2):
        total = total + swap(near[p * rows : (p + 1) * rows], "resp", size, 2 * p)
    return total


def shards(
    groups, responses, prompt_hidden, key_matrix, key_gain, prompt_token_value,
    resp_query, resp_key, response_value, grad_out, resp_length,
):
    hidden = prompt_hidden[0]
    tokens = hidden.shape[0]
    depth, kv_width = key_matrix.shape
    head_dim = key_gain.shape[0]
    group, resp = lax.axis_index("group"), lax.axis_index("resp")
    core = resp % 2
    place = jnp.stack([group, core]).astype(jnp.int32)

    columns = []
    for k in range(groups):
        piece = lax.dynamic_slice(hidden, (0, (group ^ k) * depth), (tokens, depth))
        columns.append(swap(piece, "group", groups, k) if k else piece)
    partials = [dot(piece, key_matrix) for piece in columns]
    key_pre = partials[0]
    for k in range(1, groups):
        key_pre = key_pre + swap(partials[k], "group", groups, k)
    value_near = spread_near(after(prompt_token_value[0], *columns), responses)
    value_pieces = value_near + spread_far(value_near, responses)

    prompt_key = norm_keys(key_pre, key_gain).astype(BF16)
    key_near = spread_near(prompt_key, responses)
    key_pieces = key_near + spread_far(key_near, responses)

    chips = responses // 2
    chip_rows = depth // chips
    hidden_t = jnp.concatenate(columns, axis=0).T
    hidden_t = after(hidden_t, *key_near)
    taken = []
    for k in range(0, responses, 2):
        start = ((resp ^ k) // 2) * chip_rows
        piece = lax.dynamic_slice(hidden_t, (start, 0), (chip_rows, hidden_t.shape[1]))
        taken.append(swap(piece, "resp", responses, k) if k else piece)

    half_width = kv_width // 2
    half_weight = lax.dynamic_slice(key_matrix, (0, core * half_width), (depth, half_width))
    half_weight = after(half_weight, key_pre)
    weight_near = [swap(half_weight, "group", groups, k) for k in range(1, groups)]

    queries, upstream = resp_query[0, 0], grad_out[0, 0]
    rest = (queries, upstream, key_pieces, value_pieces, resp_key[0, 0], response_value[0, 0], head_dim)
    count = kv_width // head_dim // 2
    earlier, key_parts, value_parts, length = [], [], [], resp_length
    for first in (0, count):
        *earlier, key_near, key_far, value_near, value_far = attend(length, *rest, first, count, earlier)
        key_near = pair_sum(key_near, key_far, responses)
        value_near = pair_sum(value_near, value_far, responses)
        length = after(resp_length, key_near, value_near, *taken)
        key_parts.append(chip_sum(key_near, responses))
        value_parts.append(chip_sum(value_near, responses))
    query_grad, key_grad, value_grad = earlier
    prompt_key_grad = jnp.concatenate(key_parts, axis=1)
    prompt_value_grad = jnp.concatenate(value_parts, axis=1)
    _, pullback = jax.vjp(lambda values: norm_keys(values, key_gain), key_pre)
    key_pre_grad = pullback(prompt_key_grad)[0].astype(BF16)

    block = jnp.stack(spread_near(key_pre_grad, responses), axis=0)
    blocks = [block] + [swap(block, "group", groups, k) for k in range(1, groups)]
    mine, other = weight_pass(place, taken, blocks)
    grad_weight = mine + swap(other, "resp", responses, 1)

    weight_far = [swap(piece, "resp", responses, 1) for piece in weight_near]
    grad_hidden = hidden_pass(place, key_pre_grad, key_matrix, weight_near, weight_far)
    return (
        grad_hidden[None],
        grad_weight,
        prompt_value_grad.astype(BF16)[None],
        query_grad[None, None],
        key_grad[None, None],
        value_grad[None, None],
    )


def solution(mesh):
    return jax.shard_map(
        partial(shards, mesh.shape["group"], mesh.shape["resp"]),
        mesh=mesh,
        in_specs=(
            P("group", "resp", None),
            P("group", None),
            P(),
            P("group", "resp", None),
            P("group", "resp", None, None),
            P("group", "resp", None, None),
            P("group", "resp", None, None),
            P("group", "resp", None, None),
            P("group", "resp"),
        ),
        out_specs=(
            P("group", "resp", None),
            P(("group", "resp"), None),
            P("group", "resp", None),
            P("group", "resp", None, None),
            P("group", "resp", None, None),
            P("group", "resp", None, None),
        ),
        check_vma=False,
    )
```

```python
from functools import partial

import jax
import jax.numpy as jnp
from jax import lax
from jax.experimental import pallas as pl
from jax.experimental.pallas import tpu as pltpu
from jax.sharding import PartitionSpec as P

F32, BF16 = jnp.float32, jnp.bfloat16
LOG2E = 1.4426950408889634
PARAMS = pltpu.CompilerParams(vmem_limit_bytes=56 * 2**20)


def norm_keys(key_pre, key_gain):
    shaped = key_pre.reshape(key_pre.shape[:-1] + (-1, key_gain.shape[0]))
    inverse = lax.rsqrt(jnp.mean(shaped * shaped, axis=-1, keepdims=True) + 1e-06)
    return (shaped * inverse * key_gain).reshape(key_pre.shape)


def dot(left, right, left_dim=1, right_dim=0):
    dims = (((left_dim,), (right_dim,)), ((), ()))
    return lax.dot_general(left, right, dims, preferred_element_type=F32)


def cost(macs, nbytes):
    return pl.CostEstimate(flops=2 * macs, bytes_accessed=nbytes, transcendentals=0)


def stack_heads(ref, head_dim):
    heads = ref.shape[1] // head_dim
    return jnp.concatenate([ref[:, i * head_dim : (i + 1) * head_dim] for i in range(heads)], axis=0)


def attend_kernel(pieces, chained, length_ref, query_ref, upstream_ref, key_ref, value_ref, *refs):
    key_pieces, value_pieces = refs[:pieces], refs[pieces : 2 * pieces]
    query_grad_ref, key_grad_ref, value_grad_ref, *halves = refs[2 * pieces + 3 * chained :]
    key_near_ref, key_far_ref, value_near_ref, value_far_ref = halves
    rows = query_ref.shape[0]
    own_len, head_dim = key_ref.shape
    heads = query_ref.shape[1] // head_dim
    scale = head_dim ** -0.5
    keys = jnp.concatenate([ref[...] for ref in key_pieces] + [key_ref[...]], axis=0)
    values = jnp.concatenate([ref[...] for ref in value_pieces] + [value_ref[...]], axis=0)
    keys_t, values_t = keys.T, values.T
    prompt_len = keys.shape[0] - own_len
    queries, upstream = stack_heads(query_ref, head_dim), stack_heads(upstream_ref, head_dim)
    stacked = heads * rows
    live = lax.broadcasted_iota(jnp.int32, (stacked, 1), 0) % rows < length_ref[0, 0]
    own = (stacked, own_len)
    visible = lax.broadcasted_iota(jnp.int32, own, 1) <= lax.broadcasted_iota(jnp.int32, own, 0) % rows
    prompt_scores = dot(queries, keys_t[:, :prompt_len])
    own_scores = jnp.where(visible, dot(queries, keys_t[:, prompt_len:]), -jnp.inf)
    row_max = jnp.maximum(
        jnp.max(prompt_scores, axis=1, keepdims=True), jnp.max(own_scores, axis=1, keepdims=True)
    )
    scores = jnp.concatenate([prompt_scores, own_scores], axis=1)
    unit = scale * LOG2E
    exponent = jnp.exp2(scores * unit - row_max * unit)
    dprob = dot(upstream, values_t)
    total = jnp.sum(exponent, axis=1, keepdims=True)
    weighted = jnp.sum(exponent * dprob, axis=1, keepdims=True)
    inverse = jnp.where(live, 1.0 / total, 0.0)
    row_delta = weighted * inverse
    weights = (exponent * inverse).astype(BF16)
    dscore = (exponent * ((dprob - row_delta) * (inverse * scale))).astype(BF16)
    query_grad = dot(dscore, keys).astype(BF16)
    for i in range(heads):
        query_grad_ref[:, i * head_dim : (i + 1) * head_dim] = query_grad[i * rows : (i + 1) * rows]
    key_grad = dot(queries.T, dscore).T
    value_grad = dot(upstream.T, weights).T
    half = prompt_len // 2
    key_near_ref[...], key_far_ref[...] = key_grad[:half], key_grad[half:prompt_len]
    value_near_ref[...], value_far_ref[...] = value_grad[:half], value_grad[half:prompt_len]
    key_grad_ref[...] = key_grad[prompt_len:].astype(BF16)
    value_grad_ref[...] = value_grad[prompt_len:].astype(BF16)


def attend(length, queries, upstream, key_pieces, value_pieces, keys, values, head_dim, first, count, earlier):
    rows, width = queries.shape
    kv_width = keys.shape[1]
    kv_heads = kv_width // head_dim
    prompt_len = sum(piece.shape[0] for piece in key_pieces)

    def block(rows, columns, offset=first):
        return pl.BlockSpec((rows, columns), lambda i: (0, i + offset))

    query_block, own_block = block(rows, width // kv_heads), block(rows, head_dim)
    piece_blocks = [block(piece.shape[0], head_dim) for piece in key_pieces]
    half = jax.ShapeDtypeStruct((prompt_len // 2, count * head_dim), F32)
    own = jax.ShapeDtypeStruct((rows, kv_width), BF16)
    before = 5 + 2 * len(key_pieces)
    macs = 5 * rows * width * (prompt_len + rows) * count // kv_heads
    return pl.pallas_call(
        partial(attend_kernel, len(key_pieces), bool(earlier)),
        grid=(count,),
        in_specs=[
            pl.BlockSpec(memory_space=pltpu.SMEM), query_block, query_block, own_block, own_block,
            *piece_blocks, *piece_blocks, *[pl.BlockSpec(memory_space=pl.ANY) for _ in earlier],
        ],
        out_specs=[query_block, own_block, own_block] + [block(prompt_len // 2, head_dim, 0)] * 4,
        out_shape=[jax.ShapeDtypeStruct((rows, width), BF16), own, own] + [half] * 4,
        input_output_aliases={before + i: i for i in range(len(earlier))},
        compiler_params=PARAMS,
        cost_estimate=cost(2 * macs, 5 * 10**6),
        name="attend",
    )(length, queries, upstream, keys, values, *key_pieces, *value_pieces, *earlier)


def hidden_kernel(groups, place_ref, first_ref, second_ref, own_ref, *refs):
    near, far, out_ref = refs[: groups - 1], refs[groups - 1 : -1], refs[-1]
    group, core = place_ref[0], place_ref[1]
    depth = own_ref.shape[0]
    first, second = first_ref[...], second_ref[...]
    near_grad = jnp.where(core == 0, first, second)
    far_grad = jnp.where(core == 0, second, first)
    for k in range(groups):
        if k:
            block = dot(near_grad, near[k - 1][...], 1, 1) + dot(far_grad, far[k - 1][...], 1, 1)
        else:
            block = dot(jnp.concatenate([first, second], axis=1), own_ref[...], 1, 1)
        start = pl.multiple_of((group ^ k) * depth, depth)
        out_ref[:, pl.ds(start, depth)] = block.astype(BF16)


def hidden_pass(place, key_pre_grads, own, near, far):
    tokens = key_pre_grads[0].shape[0]
    groups = len(near) + 1
    width = groups * own.shape[0]
    return pl.pallas_call(
        partial(hidden_kernel, groups),
        in_specs=[pl.BlockSpec(memory_space=pltpu.SMEM)]
        + [pl.BlockSpec(memory_space=pltpu.VMEM)] * (2 * groups + 1),
        out_specs=pl.BlockSpec(memory_space=pltpu.VMEM),
        out_shape=jax.ShapeDtypeStruct((tokens, width), BF16),
        compiler_params=PARAMS,
        cost_estimate=cost(tokens * width * own.shape[1], 6 * 10**6),
        name="hidden_grad",
    )(place, *key_pre_grads, own, *near, *far)


def weight_kernel(chips, place_ref, *refs):
    taken, blocks = refs[:chips], refs[chips:-3]
    mine_ref, other_ref, product = refs[-3:]
    half = mine_ref.shape[0]
    core = place_ref[1]
    columns = jnp.concatenate([ref[...] for ref in taken], axis=1)
    grads = jnp.concatenate([ref[p] for p in range(chips) for ref in blocks], axis=0)
    product[...] = dot(columns, grads)
    mine_ref[...] = product[pl.ds(pl.multiple_of(core * half, 8), half)]
    other_ref[...] = product[pl.ds(pl.multiple_of((1 - core) * half, 8), half)]


def weight_pass(place, taken, blocks):
    rows = taken[0].shape[0]
    kv_width = blocks[0].shape[-1]
    out = jax.ShapeDtypeStruct((rows // 2, kv_width), F32)
    return pl.pallas_call(
        partial(weight_kernel, len(taken)),
        in_specs=[pl.BlockSpec(memory_space=pltpu.SMEM)]
        + [pl.BlockSpec(memory_space=pltpu.VMEM)] * (len(taken) + len(blocks)),
        out_specs=[pl.BlockSpec(memory_space=pltpu.VMEM)] * 2,
        out_shape=[out, out],
        scratch_shapes=[pltpu.VMEM((rows, kv_width), F32)],
        compiler_params=PARAMS,
        cost_estimate=cost(rows * kv_width * taken[0].shape[1] * len(taken), 3 * 10**6),
        name="weight_grad",
    )(place, *taken, *blocks)


def swap(array, axis, size, distance):
    return lax.ppermute(array, axis, [(i, i ^ distance) for i in range(size)])


def together(*arrays):
    return list(lax.optimization_barrier(arrays))


def spread_near(block, size):
    return [block] + [swap(block, "resp", size, k) for k in range(2, size, 2)]


def spread_far(near, size):
    return [swap(piece, "resp", size, 1) for piece in near]


def pair_sum(near, far, size):
    return near + swap(far, "resp", size, 1)


def chip_sum(near, size):
    rows = near.shape[0] // (size // 2)
    total = near[:rows]
    for p in range(1, size // 2):
        total = total + swap(near[p * rows : (p + 1) * rows], "resp", size, 2 * p)
    return total


def shards(
    groups, responses, prompt_hidden, key_matrix, key_gain, prompt_token_value,
    resp_query, resp_key, response_value, grad_out, resp_length,
):
    hidden = prompt_hidden[0]
    tokens = hidden.shape[0]
    depth, kv_width = key_matrix.shape
    head_dim = key_gain.shape[0]
    group, resp = lax.axis_index("group"), lax.axis_index("resp")
    core = resp % 2
    place = jnp.stack([group, core]).astype(jnp.int32)

    pieces = [
        lax.dynamic_slice(hidden, (0, (group ^ k) * depth), (tokens, depth)) for k in range(groups)
    ]
    prompt_value, *pieces = together(prompt_token_value[0], *pieces)
    columns = [swap(piece, "group", groups, k) if k else piece for k, piece in enumerate(pieces)]
    partials = [dot(piece, key_matrix) for piece in columns]
    value_near = spread_near(prompt_value, responses)
    key_pre = partials[0]
    for k in range(1, groups):
        key_pre = key_pre + swap(partials[k], "group", groups, k)
    value_pieces = value_near + spread_far(value_near, responses)

    half_width = kv_width // 2
    half_weight = lax.dynamic_slice(key_matrix, (0, core * half_width), (depth, half_width))
    half_weight, key_pre = together(half_weight, key_pre)
    prompt_key = norm_keys(key_pre, key_gain).astype(BF16)
    key_near = spread_near(prompt_key, responses)
    weight_near = [swap(half_weight, "group", groups, k) for k in range(1, groups)]

    chips = responses // 2
    chip_rows = depth // chips
    hidden_t = jnp.concatenate(columns, axis=0).T
    hidden_t, *key_near = together(hidden_t, *key_near)
    key_pieces = key_near + spread_far(key_near, responses)
    taken = []
    for k in range(0, responses, 2):
        start = ((resp ^ k) // 2) * chip_rows
        piece = lax.dynamic_slice(hidden_t, (start, 0), (chip_rows, hidden_t.shape[1]))
        taken.append(swap(piece, "resp", responses, k) if k else piece)

    rest = (
        resp_query[0, 0], grad_out[0, 0], key_pieces, value_pieces,
        resp_key[0, 0], response_value[0, 0], head_dim,
    )
    count = kv_width // head_dim // 2
    width = count * head_dim
    *earlier, near, far, value_near0, value_far0 = attend(resp_length, *rest, 0, count, [])
    near = pair_sum(near, far, responses)
    length, near, *taken = together(resp_length, near, *taken)
    sums0 = chip_sum(near, responses)
    *outputs, near, far, value_near1, value_far1 = attend(length, *rest, count, count, earlier)
    query_grad, key_grad, value_grad = outputs
    sums1 = chip_sum(pair_sum(near, far, responses), responses)

    halves = []
    for i, sums in enumerate((sums0, sums1)):
        part = key_pre[:, i * width : (i + 1) * width]
        _, pullback = jax.vjp(lambda values: norm_keys(values, key_gain), part)
        halves.append(spread_near(pullback(sums)[0].astype(BF16), responses))
    value_near = jnp.concatenate([value_near0, value_near1], axis=1)
    value_far = jnp.concatenate([value_far0, value_far1], axis=1)
    value_near, value_far, *rest = together(value_near, value_far, *weight_near, *halves[1])
    weight_near, halves[1] = rest[: groups - 1], rest[groups - 1 :]
    weight_far = [swap(piece, "resp", responses, 1) for piece in weight_near]
    grad_hidden = hidden_pass(
        place, [near[0] for near in halves], key_matrix, weight_near, weight_far
    )
    weight_halves = []
    for near in halves:
        block = jnp.stack(near, axis=0)
        blocks = [block] + [swap(block, "group", groups, k) for k in range(1, groups)]
        mine, other = weight_pass(place, taken, blocks)
        weight_halves.append(mine + swap(other, "resp", responses, 1))
    prompt_value_grad = chip_sum(pair_sum(value_near, value_far, responses), responses)
    return (
        grad_hidden[None],
        jnp.concatenate(weight_halves, axis=1),
        prompt_value_grad.astype(BF16)[None],
        query_grad[None, None],
        key_grad[None, None],
        value_grad[None, None],
    )


def solution(mesh):
    return jax.shard_map(
        partial(shards, mesh.shape["group"], mesh.shape["resp"]),
        mesh=mesh,
        in_specs=(
            P("group", "resp", None),
            P("group", None),
            P(),
            P("group", "resp", None),
            P("group", "resp", None, None),
            P("group", "resp", None, None),
            P("group", "resp", None, None),
            P("group", "resp", None, None),
            P("group", "resp"),
        ),
        out_specs=(
            P("group", "resp", None),
            P(("group", "resp"), None),
            P("group", "resp", None),
            P("group", "resp", None, None),
            P("group", "resp", None, None),
            P("group", "resp", None, None),
        ),
        check_vma=False,
    )
```

```python
from functools import partial

import jax
import jax.numpy as jnp
from jax import lax
from jax.experimental import pallas as pl
from jax.experimental.pallas import tpu as pltpu
from jax.sharding import PartitionSpec as P

F32, BF16 = jnp.float32, jnp.bfloat16
LOG2E = 1.4426950408889634
PARAMS = pltpu.CompilerParams(vmem_limit_bytes=56 * 2**20)


def norm_keys(key_pre, key_gain):
    shaped = key_pre.reshape(key_pre.shape[:-1] + (-1, key_gain.shape[0]))
    inverse = lax.rsqrt(jnp.mean(shaped * shaped, axis=-1, keepdims=True) + 1e-06)
    return (shaped * inverse * key_gain).reshape(key_pre.shape)


def dot(left, right, left_dim=1, right_dim=0):
    dims = (((left_dim,), (right_dim,)), ((), ()))
    return lax.dot_general(left, right, dims, preferred_element_type=F32)


def cost(macs, nbytes):
    return pl.CostEstimate(flops=2 * macs, bytes_accessed=nbytes, transcendentals=0)


def stack_heads(ref, head_dim):
    heads = ref.shape[1] // head_dim
    return jnp.concatenate([ref[:, i * head_dim : (i + 1) * head_dim] for i in range(heads)], axis=0)


def attend_kernel(pieces, chained, length_ref, query_ref, upstream_ref, key_ref, value_ref, *refs):
    key_pieces, value_pieces = refs[:pieces], refs[pieces : 2 * pieces]
    query_grad_ref, key_grad_ref, value_grad_ref, *sum_refs = refs[2 * pieces + 3 * chained :]
    rows = query_ref.shape[0]
    own_len, head_dim = key_ref.shape
    heads = query_ref.shape[1] // head_dim
    scale = head_dim ** -0.5
    keys = jnp.concatenate([ref[...] for ref in key_pieces] + [key_ref[...]], axis=0)
    values = jnp.concatenate([ref[...] for ref in value_pieces] + [value_ref[...]], axis=0)
    keys_t, values_t = keys.T, values.T
    prompt_len = keys.shape[0] - own_len
    queries, upstream = stack_heads(query_ref, head_dim), stack_heads(upstream_ref, head_dim)
    stacked = heads * rows
    live = lax.broadcasted_iota(jnp.int32, (stacked, 1), 0) % rows < length_ref[0, 0]
    own = (stacked, own_len)
    visible = lax.broadcasted_iota(jnp.int32, own, 1) <= lax.broadcasted_iota(jnp.int32, own, 0) % rows
    prompt_scores = dot(queries, keys_t[:, :prompt_len])
    own_scores = jnp.where(visible, dot(queries, keys_t[:, prompt_len:]), -jnp.inf)
    row_max = jnp.maximum(
        jnp.max(prompt_scores, axis=1, keepdims=True), jnp.max(own_scores, axis=1, keepdims=True)
    )
    scores = jnp.concatenate([prompt_scores, own_scores], axis=1)
    unit = scale * LOG2E
    exponent = jnp.exp2(scores * unit - row_max * unit)
    dprob = dot(upstream, values_t)
    total = jnp.sum(exponent, axis=1, keepdims=True)
    weighted = jnp.sum(exponent * dprob, axis=1, keepdims=True)
    inverse = jnp.where(live, 1.0 / total, 0.0)
    row_delta = weighted * inverse
    weights = (exponent * inverse).astype(BF16)
    dscore = (exponent * ((dprob - row_delta) * (inverse * scale))).astype(BF16)
    query_grad = dot(dscore, keys).astype(BF16)
    for i in range(heads):
        query_grad_ref[:, i * head_dim : (i + 1) * head_dim] = query_grad[i * rows : (i + 1) * rows]
    key_grad = dot(queries.T, dscore).T
    value_grad = dot(upstream.T, weights).T
    half = prompt_len // 2
    per_array = len(sum_refs) // 2
    for i, grad in enumerate((key_grad, value_grad)):
        near_ref, far_ref = sum_refs[:2] if per_array == 1 else sum_refs[2 * i : 2 * i + 2]
        near_ref[i % (3 - per_array)], far_ref[i % (3 - per_array)] = grad[:half], grad[half:prompt_len]
    key_grad_ref[...] = key_grad[prompt_len:].astype(BF16)
    value_grad_ref[...] = value_grad[prompt_len:].astype(BF16)


def attend(length, queries, upstream, key_pieces, value_pieces, keys, values, head_dim, first, count, earlier):
    rows, width = queries.shape
    kv_width = keys.shape[1]
    kv_heads = kv_width // head_dim
    prompt_len = sum(piece.shape[0] for piece in key_pieces)

    def block(rows, columns, offset=first):
        return pl.BlockSpec((rows, columns), lambda i: (0, i + offset))

    query_block, own_block = block(rows, width // kv_heads), block(rows, head_dim)
    piece_blocks = [block(piece.shape[0], head_dim) for piece in key_pieces]
    kinds, arrays = (1, 2) if earlier else (2, 1)
    half = jax.ShapeDtypeStruct((kinds, prompt_len // 2, count * head_dim), F32)
    half_block = pl.BlockSpec((kinds, prompt_len // 2, head_dim), lambda i: (0, 0, i))
    own = jax.ShapeDtypeStruct((rows, kv_width), BF16)
    before = 5 + 2 * len(key_pieces)
    macs = 5 * rows * width * (prompt_len + rows) * count // kv_heads
    return pl.pallas_call(
        partial(attend_kernel, len(key_pieces), bool(earlier)),
        grid=(count,),
        in_specs=[
            pl.BlockSpec(memory_space=pltpu.SMEM), query_block, query_block, own_block, own_block,
            *piece_blocks, *piece_blocks, *[pl.BlockSpec(memory_space=pl.ANY) for _ in earlier],
        ],
        out_specs=[query_block, own_block, own_block] + [half_block] * (2 * arrays),
        out_shape=[jax.ShapeDtypeStruct((rows, width), BF16), own, own] + [half] * (2 * arrays),
        input_output_aliases={before + i: i for i in range(len(earlier))},
        compiler_params=PARAMS,
        cost_estimate=cost(2 * macs, 5 * 10**6),
        name="attend",
    )(length, queries, upstream, keys, values, *key_pieces, *value_pieces, *earlier)


def hidden_kernel(groups, place_ref, grad_ref, own_ref, *refs):
    near, far, out_ref = refs[: groups - 1], refs[groups - 1 : -1], refs[-1]
    group, core = place_ref[0], place_ref[1]
    depth = own_ref.shape[0]
    half = near[0].shape[1]
    near_grad = grad_ref[:, pl.ds(pl.multiple_of(core * half, half), half)]
    far_grad = grad_ref[:, pl.ds(pl.multiple_of((1 - core) * half, half), half)]
    for k in range(groups):
        if k:
            block = dot(near_grad, near[k - 1][...], 1, 1) + dot(far_grad, far[k - 1][...], 1, 1)
        else:
            block = dot(grad_ref[...], own_ref[...], 1, 1)
        start = pl.multiple_of((group ^ k) * depth, depth)
        out_ref[:, pl.ds(start, depth)] = block.astype(BF16)


def hidden_pass(place, key_pre_grad, own, near, far):
    tokens = key_pre_grad.shape[0]
    groups = len(near) + 1
    width = groups * own.shape[0]
    return pl.pallas_call(
        partial(hidden_kernel, groups),
        in_specs=[pl.BlockSpec(memory_space=pltpu.SMEM)]
        + [pl.BlockSpec(memory_space=pltpu.VMEM)] * (2 * groups),
        out_specs=pl.BlockSpec(memory_space=pltpu.VMEM),
        out_shape=jax.ShapeDtypeStruct((tokens, width), BF16),
        compiler_params=PARAMS,
        cost_estimate=cost(tokens * width * own.shape[1], 6 * 10**6),
        name="hidden_grad",
    )(place, key_pre_grad, own, *near, *far)


def weight_kernel(chips, place_ref, *refs):
    taken, blocks = refs[:chips], refs[chips:-3]
    mine_ref, other_ref, product = refs[-3:]
    half = mine_ref.shape[0]
    core = place_ref[1]
    columns = jnp.concatenate([ref[...] for ref in taken], axis=1)
    grads = jnp.concatenate([ref[p] for p in range(chips) for ref in blocks], axis=0)
    product[...] = dot(columns, grads)
    mine_ref[...] = product[pl.ds(pl.multiple_of(core * half, 8), half)]
    other_ref[...] = product[pl.ds(pl.multiple_of((1 - core) * half, 8), half)]


def weight_pass(place, taken, blocks):
    rows = taken[0].shape[0]
    kv_width = blocks[0].shape[-1]
    out = jax.ShapeDtypeStruct((rows // 2, kv_width), F32)
    return pl.pallas_call(
        partial(weight_kernel, len(taken)),
        in_specs=[pl.BlockSpec(memory_space=pltpu.SMEM)]
        + [pl.BlockSpec(memory_space=pltpu.VMEM)] * (len(taken) + len(blocks)),
        out_specs=[pl.BlockSpec(memory_space=pltpu.VMEM)] * 2,
        out_shape=[out, out],
        scratch_shapes=[pltpu.VMEM((rows, kv_width), F32)],
        compiler_params=PARAMS,
        cost_estimate=cost(rows * kv_width * taken[0].shape[1] * len(taken), 3 * 10**6),
        name="weight_grad",
    )(place, *taken, *blocks)


def swap(array, axis, size, distance):
    return lax.ppermute(array, axis, [(i, i ^ distance) for i in range(size)])


def together(*arrays):
    return list(lax.optimization_barrier(arrays))


def spread_near(block, size):
    return [block] + [swap(block, "resp", size, k) for k in range(2, size, 2)]


def spread_far(near, size):
    return [swap(jnp.concatenate(near, axis=0), "resp", size, 1)]


def pair_sum(near, far, size):
    return near + swap(far, "resp", size, 1)


def chip_sum(near, size):
    rows = near.shape[1] // (size // 2)
    total = near[:, :rows]
    for p in range(1, size // 2):
        total = total + swap(near[:, p * rows : (p + 1) * rows], "resp", size, 2 * p)
    return total


def shards(
    groups, responses, prompt_hidden, key_matrix, key_gain, prompt_token_value,
    resp_query, resp_key, response_value, grad_out, resp_length,
):
    hidden = prompt_hidden[0]
    tokens = hidden.shape[0]
    depth, kv_width = key_matrix.shape
    head_dim = key_gain.shape[0]
    group, resp = lax.axis_index("group"), lax.axis_index("resp")
    core = resp % 2
    place = jnp.stack([group, core]).astype(jnp.int32)

    pieces = [
        lax.dynamic_slice(hidden, (0, (group ^ k) * depth), (tokens, depth)) for k in range(groups)
    ]
    columns = [swap(piece, "group", groups, k) if k else piece for k, piece in enumerate(pieces)]
    prompt_value, columns[1] = together(prompt_token_value[0], columns[1])
    partials = [dot(piece, key_matrix) for piece in columns]
    value_near = spread_near(prompt_value, responses)
    key_pre = partials[0]
    for k in range(1, groups):
        key_pre = key_pre + swap(partials[k], "group", groups, k)
    value_pieces = value_near + spread_far(value_near, responses)

    half_width = kv_width // 2
    half_weight = lax.dynamic_slice(key_matrix, (0, core * half_width), (depth, half_width))
    half_weight, key_pre = together(half_weight, key_pre)
    prompt_key = norm_keys(key_pre, key_gain).astype(BF16)
    key_near = spread_near(prompt_key, responses)
    weight_near = [swap(half_weight, "group", groups, k) for k in range(1, groups)]

    chips = responses // 2
    chip_rows = depth // chips
    hidden_t = jnp.concatenate(columns, axis=0).T
    hidden_t, *key_near = together(hidden_t, *key_near)
    key_pieces = key_near + spread_far(key_near, responses)
    taken = []
    for k in range(0, responses, 2):
        start = ((resp ^ k) // 2) * chip_rows
        piece = lax.dynamic_slice(hidden_t, (start, 0), (chip_rows, hidden_t.shape[1]))
        taken.append(swap(piece, "resp", responses, k) if k else piece)

    rest = (
        resp_query[0, 0], grad_out[0, 0], key_pieces, value_pieces,
        resp_key[0, 0], response_value[0, 0], head_dim,
    )
    count = kv_width // head_dim // 2
    width = count * head_dim
    *earlier, near, far = attend(resp_length, *rest, 0, count, [])
    near, far, *rest_taken = together(near, far, *weight_near[:-1], *taken)
    weight_near[:-1], taken = rest_taken[: groups - 2], rest_taken[groups - 2 :]
    near = pair_sum(near, far, responses)
    length, near = together(resp_length, near)
    sums0 = chip_sum(near, responses)
    *outputs, near, far, value_near, value_far = attend(length, *rest, count, count, earlier)
    query_grad, key_grad, value_grad = outputs
    sums0, near, far, weight_near[-1] = together(sums0, near, far, weight_near[-1])
    sums1 = chip_sum(pair_sum(near, far, responses), responses)
    value_near = pair_sum(value_near, value_far, responses)
    _, pullback = jax.vjp(lambda values: norm_keys(values, key_gain), key_pre)
    key_pre_grad = pullback(jnp.concatenate([sums0[0], sums1[0]], axis=1))[0].astype(BF16)

    key_pre_grad, value_near = together(key_pre_grad, value_near)

    grads = spread_near(key_pre_grad, responses)
    weight_near[0], *grads = together(weight_near[0], *grads)
    block = jnp.stack(grads, axis=0)
    blocks = [block] + [swap(block, "group", groups, k) for k in range(1, groups)]
    weight_far = [swap(piece, "resp", responses, 1) for piece in weight_near]
    grad_hidden = hidden_pass(place, grads[0], key_matrix, weight_near, weight_far)
    grad_hidden, value_near = together(grad_hidden, value_near)
    values1 = chip_sum(value_near, responses)
    grad_hidden, *blocks = together(grad_hidden, *blocks)
    mine, other = weight_pass(place, taken, blocks)
    other, values1 = together(other, values1)
    grad_weight = mine + swap(other, "resp", responses, 1)
    prompt_value_grad = jnp.concatenate([sums0[1], values1[0]], axis=1)
    return (
        grad_hidden[None],
        grad_weight,
        prompt_value_grad.astype(BF16)[None],
        query_grad[None, None],
        key_grad[None, None],
        value_grad[None, None],
    )


def solution(mesh):
    return jax.shard_map(
        partial(shards, mesh.shape["group"], mesh.shape["resp"]),
        mesh=mesh,
        in_specs=(
            P("group", "resp", None),
            P("group", None),
            P(),
            P("group", "resp", None),
            P("group", "resp", None, None),
            P("group", "resp", None, None),
            P("group", "resp", None, None),
            P("group", "resp", None, None),
            P("group", "resp"),
        ),
        out_specs=(
            P("group", "resp", None),
            P(("group", "resp"), None),
            P("group", "resp", None),
            P("group", "resp", None, None),
            P("group", "resp", None, None),
            P("group", "resp", None, None),
        ),
        check_vma=False,
    )
```

```python
from functools import partial

import jax
import jax.numpy as jnp
from jax import lax
from jax.experimental import pallas as pl
from jax.experimental.pallas import tpu as pltpu
from jax.sharding import PartitionSpec as P

F32, BF16 = jnp.float32, jnp.bfloat16
LOG2E = 1.4426950408889634
PARAMS = pltpu.CompilerParams(vmem_limit_bytes=56 * 2**20)


def norm_keys(key_pre, key_gain):
    shaped = key_pre.reshape(key_pre.shape[:-1] + (-1, key_gain.shape[0]))
    inverse = lax.rsqrt(jnp.mean(shaped * shaped, axis=-1, keepdims=True) + 1e-06)
    return (shaped * inverse * key_gain).reshape(key_pre.shape)


def dot(left, right, left_dim=1, right_dim=0):
    dims = (((left_dim,), (right_dim,)), ((), ()))
    return lax.dot_general(left, right, dims, preferred_element_type=F32)


def cost(macs, nbytes):
    return pl.CostEstimate(flops=2 * macs, bytes_accessed=nbytes, transcendentals=0)


def stack_heads(ref, head_dim):
    heads = ref.shape[1] // head_dim
    return jnp.concatenate([ref[:, i * head_dim : (i + 1) * head_dim] for i in range(heads)], axis=0)


def attend_kernel(pieces, length_ref, query_ref, upstream_ref, key_ref, value_ref, *refs):
    key_pieces, value_pieces = refs[:pieces], refs[pieces : 2 * pieces]
    query_grad_ref, key_grad_ref, value_grad_ref, *sum_refs = refs[2 * pieces :]
    rows = query_ref.shape[0]
    own_len, head_dim = key_ref.shape
    heads = query_ref.shape[1] // head_dim
    scale = head_dim ** -0.5
    keys = jnp.concatenate([ref[...] for ref in key_pieces] + [key_ref[...]], axis=0)
    values = jnp.concatenate([ref[...] for ref in value_pieces] + [value_ref[...]], axis=0)
    keys_t, values_t = keys.T, values.T
    prompt_len = keys.shape[0] - own_len
    queries, upstream = stack_heads(query_ref, head_dim), stack_heads(upstream_ref, head_dim)
    stacked = heads * rows
    live = lax.broadcasted_iota(jnp.int32, (stacked, 1), 0) % rows < length_ref[0, 0]
    own = (stacked, own_len)
    visible = lax.broadcasted_iota(jnp.int32, own, 1) <= lax.broadcasted_iota(jnp.int32, own, 0) % rows
    prompt_scores = dot(queries, keys_t[:, :prompt_len])
    own_scores = jnp.where(visible, dot(queries, keys_t[:, prompt_len:]), -jnp.inf)
    row_max = jnp.maximum(
        jnp.max(prompt_scores, axis=1, keepdims=True), jnp.max(own_scores, axis=1, keepdims=True)
    )
    scores = jnp.concatenate([prompt_scores, own_scores], axis=1)
    unit = scale * LOG2E
    exponent = jnp.exp2(scores * unit - row_max * unit)
    dprob = dot(upstream, values_t)
    total = jnp.sum(exponent, axis=1, keepdims=True)
    weighted = jnp.sum(exponent * dprob, axis=1, keepdims=True)
    inverse = jnp.where(live, 1.0 / total, 0.0)
    row_delta = weighted * inverse
    weights = (exponent * inverse).astype(BF16)
    dscore = (exponent * ((dprob - row_delta) * (inverse * scale))).astype(BF16)
    query_grad = dot(dscore, keys).astype(BF16)
    for i in range(heads):
        query_grad_ref[:, i * head_dim : (i + 1) * head_dim] = query_grad[i * rows : (i + 1) * rows]
    key_grad = dot(queries.T, dscore).T
    value_grad = dot(upstream.T, weights).T
    half = prompt_len // 2
    for i, grad in enumerate((key_grad, value_grad)):
        sum_refs[2 * i][...], sum_refs[2 * i + 1][...] = grad[:half], grad[half:prompt_len]
    key_grad_ref[...] = key_grad[prompt_len:].astype(BF16)
    value_grad_ref[...] = value_grad[prompt_len:].astype(BF16)


def attend(length, queries, upstream, key_pieces, value_pieces, keys, values, head_dim):
    rows, width = queries.shape
    kv_width = keys.shape[1]
    kv_heads = kv_width // head_dim
    prompt_len = sum(piece.shape[0] for piece in key_pieces)

    def block(rows, columns):
        return pl.BlockSpec((rows, columns), lambda i: (0, i))

    query_block, own_block = block(rows, width // kv_heads), block(rows, head_dim)
    piece_blocks = [block(piece.shape[0], head_dim) for piece in key_pieces]
    half = jax.ShapeDtypeStruct((prompt_len // 2, kv_width), F32)
    own = jax.ShapeDtypeStruct((rows, kv_width), BF16)
    return pl.pallas_call(
        partial(attend_kernel, len(key_pieces)),
        grid=(kv_heads,),
        in_specs=[
            pl.BlockSpec(memory_space=pltpu.SMEM), query_block, query_block, own_block, own_block,
            *piece_blocks, *piece_blocks,
        ],
        out_specs=[query_block, own_block, own_block] + [block(prompt_len // 2, head_dim)] * 4,
        out_shape=[jax.ShapeDtypeStruct((rows, width), BF16), own, own] + [half] * 4,
        compiler_params=PARAMS,
        cost_estimate=cost(10 * rows * width * (prompt_len + rows), 10**7),
        name="attend",
    )(length, queries, upstream, keys, values, *key_pieces, *value_pieces)


def split_kernel(place_ref, hidden_ref, *piece_refs):
    depth = piece_refs[0].shape[1]
    for k, piece_ref in enumerate(piece_refs):
        start = pl.multiple_of((place_ref[0] ^ k) * depth, depth)
        piece_ref[...] = hidden_ref[:, pl.ds(start, depth)]


def split_pass(place, hidden, groups):
    tokens, width = hidden.shape
    return pl.pallas_call(
        split_kernel,
        in_specs=[pl.BlockSpec(memory_space=pltpu.SMEM), pl.BlockSpec(memory_space=pltpu.VMEM)],
        out_specs=[pl.BlockSpec(memory_space=pltpu.VMEM)] * groups,
        out_shape=[jax.ShapeDtypeStruct((tokens, width // groups), BF16)] * groups,
        compiler_params=PARAMS,
        name="split_hidden",
    )(place, hidden)


def turn_kernel(groups, place_ref, *refs):
    columns, piece_refs, turned = refs[:groups], refs[groups:-1], refs[-1]
    rows = piece_refs[0].shape[0]
    turned[...] = jnp.concatenate([ref[...] for ref in columns], axis=0).T
    for p, piece_ref in enumerate(piece_refs):
        start = pl.multiple_of((place_ref[2] ^ p) * rows, 16)
        piece_ref[...] = turned[pl.ds(start, rows)]


def turn_pass(place, columns, chips):
    tokens, depth = columns[0].shape
    every = tokens * len(columns)
    return pl.pallas_call(
        partial(turn_kernel, len(columns)),
        in_specs=[pl.BlockSpec(memory_space=pltpu.SMEM)]
        + [pl.BlockSpec(memory_space=pltpu.VMEM)] * len(columns),
        out_specs=[pl.BlockSpec(memory_space=pltpu.VMEM)] * chips,
        out_shape=[jax.ShapeDtypeStruct((depth // chips, every), BF16)] * chips,
        scratch_shapes=[pltpu.VMEM((depth, every), BF16)],
        compiler_params=PARAMS,
        name="turn_hidden",
    )(place, *columns)


def hidden_kernel(groups, place_ref, grad_ref, own_ref, *refs):
    near, far, out_ref = refs[: groups - 1], refs[groups - 1 : -1], refs[-1]
    group, core = place_ref[0], place_ref[1]
    depth = own_ref.shape[0]
    half = near[0].shape[1]
    near_grad = grad_ref[:, pl.ds(pl.multiple_of(core * half, half), half)]
    far_grad = grad_ref[:, pl.ds(pl.multiple_of((1 - core) * half, half), half)]
    for k in range(groups):
        if k:
            block = dot(near_grad, near[k - 1][...], 1, 1) + dot(far_grad, far[k - 1][...], 1, 1)
        else:
            block = dot(grad_ref[...], own_ref[...], 1, 1)
        start = pl.multiple_of((group ^ k) * depth, depth)
        out_ref[:, pl.ds(start, depth)] = block.astype(BF16)


def hidden_pass(place, key_pre_grad, own, near, far):
    tokens = key_pre_grad.shape[0]
    groups = len(near) + 1
    width = groups * own.shape[0]
    return pl.pallas_call(
        partial(hidden_kernel, groups),
        in_specs=[pl.BlockSpec(memory_space=pltpu.SMEM)]
        + [pl.BlockSpec(memory_space=pltpu.VMEM)] * (2 * groups),
        out_specs=pl.BlockSpec(memory_space=pltpu.VMEM),
        out_shape=jax.ShapeDtypeStruct((tokens, width), BF16),
        compiler_params=PARAMS,
        cost_estimate=cost(tokens * width * own.shape[1], 6 * 10**6),
        name="hidden_grad",
    )(place, key_pre_grad, own, *near, *far)


def weight_kernel(chips, groups, place_ref, *refs):
    taken, first, rest = refs[:chips], refs[chips : chips + groups], refs[chips + groups : -3]
    mine_ref, other_ref, product = refs[-3:]
    half = mine_ref.shape[0]
    core = place_ref[1]
    columns = jnp.concatenate([ref[...] for ref in taken], axis=1)
    grads = [ref[...] for ref in first] + [ref[p] for p in range(chips - 1) for ref in rest]
    product[...] = dot(columns, jnp.concatenate(grads, axis=0))
    mine_ref[...] = product[pl.ds(pl.multiple_of(core * half, 8), half)]
    other_ref[...] = product[pl.ds(pl.multiple_of((1 - core) * half, 8), half)]


def weight_pass(place, taken, first, rest):
    rows = taken[0].shape[0]
    kv_width = first[0].shape[-1]
    out = jax.ShapeDtypeStruct((rows // 2, kv_width), F32)
    return pl.pallas_call(
        partial(weight_kernel, len(taken), len(first)),
        in_specs=[pl.BlockSpec(memory_space=pltpu.SMEM)]
        + [pl.BlockSpec(memory_space=pltpu.VMEM)] * (len(taken) + len(first) + len(rest)),
        out_specs=[pl.BlockSpec(memory_space=pltpu.VMEM)] * 2,
        out_shape=[out, out],
        scratch_shapes=[pltpu.VMEM((rows, kv_width), F32)],
        compiler_params=PARAMS,
        cost_estimate=cost(rows * kv_width * taken[0].shape[1] * len(taken), 3 * 10**6),
        name="weight_grad",
    )(place, *taken, *first, *rest)


def swap(array, axis, size, distance):
    return lax.ppermute(array, axis, [(i, i ^ distance) for i in range(size)])


def together(*arrays):
    return list(lax.optimization_barrier(arrays))


def spread_near(block, size):
    return [block] + [swap(block, "resp", size, k) for k in range(2, size, 2)]


def spread_far(near, size):
    return [swap(jnp.concatenate(near, axis=0), "resp", size, 1)]


def pair_sum(near, far, size):
    return near + swap(far, "resp", size, 1)


def chip_sum(near, size):
    rows = near.shape[0] // (size // 2)
    total = near[:rows]
    for p in range(1, size // 2):
        piece = near[p * rows : (p + 1) * rows].astype(BF16)
        total = total + swap(piece, "resp", size, 2 * p).astype(F32)
    return total


def shards(
    groups, responses, prompt_hidden, key_matrix, key_gain, prompt_token_value,
    resp_query, resp_key, response_value, grad_out, resp_length,
):
    hidden = prompt_hidden[0]
    tokens = hidden.shape[0]
    depth, kv_width = key_matrix.shape
    head_dim = key_gain.shape[0]
    group, resp = lax.axis_index("group"), lax.axis_index("resp")
    core, chip, chips = resp % 2, resp // 2, responses // 2
    place = jnp.stack([group, core, chip]).astype(jnp.int32)

    pieces = split_pass(place, hidden, groups)
    columns = [swap(piece, "group", groups, k) if k else piece for k, piece in enumerate(pieces)]
    partials = [dot(piece, key_matrix) for piece in columns]
    prompt_value, partials[0] = together(prompt_token_value[0], partials[0])
    value_near = spread_near(prompt_value, responses)
    key_pre = partials[0]
    for k in range(1, groups):
        key_pre = key_pre + swap(partials[k], "group", groups, k)
    value_far = spread_far(value_near, responses)

    half_width = kv_width // 2
    half_weight = lax.dynamic_slice(key_matrix, (0, core * half_width), (depth, half_width))
    half_weight, key_pre, *value_far = together(half_weight, key_pre, *value_far)
    value_pieces = value_near + value_far
    prompt_key = norm_keys(key_pre, key_gain).astype(BF16)
    key_near = spread_near(prompt_key, responses)
    weight_near = [swap(half_weight, "group", groups, k) for k in range(1, groups)]

    taken = turn_pass(place, columns, chips)
    count = len(taken)
    both = together(*taken, *key_near)
    taken, key_near = both[:count], both[count:]
    key_pieces = key_near + spread_far(key_near, responses)
    taken[1:] = [swap(taken[p], "resp", responses, 2 * p) for p in range(1, chips)]

    query_grad, key_grad, value_grad, key_sums, far, value_sums, value_far = attend(
        resp_length, resp_query[0, 0], grad_out[0, 0], key_pieces, value_pieces,
        resp_key[0, 0], response_value[0, 0], head_dim,
    )
    key_sums, far, *rest = together(key_sums, far, *weight_near[:-1], *taken)
    weight_near[:-1], taken = rest[: groups - 2], rest[groups - 2 :]
    key_sums = chip_sum(pair_sum(key_sums, far, responses), responses)
    value_sums = pair_sum(value_sums, value_far, responses)
    weight_far = [swap(piece, "resp", responses, 1) for piece in weight_near[:-1]]
    key_sums, value_sums, weight_near[-1], *weight_far = together(
        key_sums, value_sums, weight_near[-1], *weight_far
    )
    _, pullback = jax.vjp(lambda values: norm_keys(values, key_gain), key_pre)
    key_pre_grad = pullback(key_sums)[0].astype(BF16)

    first = [key_pre_grad] + [swap(key_pre_grad, "group", groups, k) for k in range(1, groups)]
    grads = spread_near(key_pre_grad, responses)[1:]
    weight_far.append(swap(weight_near[-1], "resp", responses, 1))
    *first, weight_far[-1], block = together(*first, weight_far[-1], jnp.stack(grads, axis=0))
    blocks = [block] + [swap(block, "group", groups, k) for k in range(1, groups)]
    grad_hidden = hidden_pass(place, first[0], key_matrix, weight_near, weight_far)
    grad_hidden, value_sums = together(grad_hidden, value_sums)
    value_sums = chip_sum(value_sums, responses)
    grad_hidden, *blocks = together(grad_hidden, *blocks)
    mine, other = weight_pass(place, taken, first, blocks)
    other, value_sums = together(other, value_sums)
    grad_weight = mine + swap(other, "resp", responses, 1)
    return (
        grad_hidden[None],
        grad_weight,
        value_sums.astype(BF16)[None],
        query_grad[None, None],
        key_grad[None, None],
        value_grad[None, None],
    )


def solution(mesh):
    return jax.shard_map(
        partial(shards, mesh.shape["group"], mesh.shape["resp"]),
        mesh=mesh,
        in_specs=(
            P("group", "resp", None),
            P("group", None),
            P(),
            P("group", "resp", None),
            P("group", "resp", None, None),
            P("group", "resp", None, None),
            P("group", "resp", None, None),
            P("group", "resp", None, None),
            P("group", "resp"),
        ),
        out_specs=(
            P("group", "resp", None),
            P(("group", "resp"), None),
            P("group", "resp", None),
            P("group", "resp", None, None),
            P("group", "resp", None, None),
            P("group", "resp", None, None),
        ),
        check_vma=False,
    )
```

```python
from functools import partial

import jax
import jax.numpy as jnp
from jax import lax
from jax.experimental import pallas as pl
from jax.experimental.pallas import tpu as pltpu
from jax.sharding import PartitionSpec as P

F32, BF16 = jnp.float32, jnp.bfloat16
LOG2E = 1.4426950408889634
PARAMS = pltpu.CompilerParams(vmem_limit_bytes=56 * 2**20)


def norm_keys(key_pre, key_gain):
    shaped = key_pre.reshape(key_pre.shape[:-1] + (-1, key_gain.shape[0]))
    inverse = lax.rsqrt(jnp.mean(shaped * shaped, axis=-1, keepdims=True) + 1e-06)
    return (shaped * inverse * key_gain).reshape(key_pre.shape)


def dot(left, right, left_dim=1, right_dim=0):
    dims = (((left_dim,), (right_dim,)), ((), ()))
    return lax.dot_general(left, right, dims, preferred_element_type=F32)


def cost(macs, nbytes):
    return pl.CostEstimate(flops=2 * macs, bytes_accessed=nbytes, transcendentals=0)


def stack_heads(ref, head_dim):
    heads = ref.shape[1] // head_dim
    return jnp.concatenate([ref[:, i * head_dim : (i + 1) * head_dim] for i in range(heads)], axis=0)


def attend_kernel(pieces, length_ref, query_ref, upstream_ref, key_ref, value_ref, *refs):
    key_pieces, value_pieces = refs[:pieces], refs[pieces : 2 * pieces]
    query_grad_ref, key_grad_ref, value_grad_ref, *sum_refs = refs[2 * pieces :]
    rows = query_ref.shape[0]
    own_len, head_dim = key_ref.shape
    heads = query_ref.shape[1] // head_dim
    scale = head_dim ** -0.5
    keys = jnp.concatenate([ref[...] for ref in key_pieces] + [key_ref[...]], axis=0)
    values = jnp.concatenate([ref[...] for ref in value_pieces] + [value_ref[...]], axis=0)
    keys_t, values_t = keys.T, values.T
    prompt_len = keys.shape[0] - own_len
    queries, upstream = stack_heads(query_ref, head_dim), stack_heads(upstream_ref, head_dim)
    stacked = heads * rows
    live = lax.broadcasted_iota(jnp.int32, (stacked, 1), 0) % rows < length_ref[0, 0]
    own = (stacked, own_len)
    visible = lax.broadcasted_iota(jnp.int32, own, 1) <= lax.broadcasted_iota(jnp.int32, own, 0) % rows
    prompt_scores = dot(queries, keys_t[:, :prompt_len])
    own_scores = jnp.where(visible, dot(queries, keys_t[:, prompt_len:]), -jnp.inf)
    row_max = jnp.maximum(
        jnp.max(prompt_scores, axis=1, keepdims=True), jnp.max(own_scores, axis=1, keepdims=True)
    )
    scores = jnp.concatenate([prompt_scores, own_scores], axis=1)
    unit = scale * LOG2E
    exponent = jnp.exp2(scores * unit - row_max * unit)
    dprob = dot(upstream, values_t)
    total = jnp.sum(exponent, axis=1, keepdims=True)
    weighted = jnp.sum(exponent * dprob, axis=1, keepdims=True)
    inverse = jnp.where(live, 1.0 / total, 0.0)
    row_delta = weighted * inverse
    weights = (exponent * inverse).astype(BF16)
    dscore = (exponent * ((dprob - row_delta) * (inverse * scale))).astype(BF16)
    query_grad = dot(dscore, keys).astype(BF16)
    for i in range(heads):
        query_grad_ref[:, i * head_dim : (i + 1) * head_dim] = query_grad[i * rows : (i + 1) * rows]
    key_grad = dot(queries.T, dscore).T
    value_grad = dot(upstream.T, weights).T
    half = prompt_len // 2
    for i, grad in enumerate((key_grad, value_grad)):
        sum_refs[2 * i][...], sum_refs[2 * i + 1][...] = grad[:half], grad[half:prompt_len]
    key_grad_ref[...] = key_grad[prompt_len:].astype(BF16)
    value_grad_ref[...] = value_grad[prompt_len:].astype(BF16)


def attend(length, queries, upstream, key_pieces, value_pieces, keys, values, head_dim):
    rows, width = queries.shape
    kv_width = keys.shape[1]
    kv_heads = kv_width // head_dim
    prompt_len = sum(piece.shape[0] for piece in key_pieces)

    def block(rows, columns):
        return pl.BlockSpec((rows, columns), lambda i: (0, i))

    query_block, own_block = block(rows, width // kv_heads), block(rows, head_dim)
    piece_blocks = [block(piece.shape[0], head_dim) for piece in key_pieces]
    half = jax.ShapeDtypeStruct((prompt_len // 2, kv_width), F32)
    own = jax.ShapeDtypeStruct((rows, kv_width), BF16)
    return pl.pallas_call(
        partial(attend_kernel, len(key_pieces)),
        grid=(kv_heads,),
        in_specs=[
            pl.BlockSpec(memory_space=pltpu.SMEM), query_block, query_block, own_block, own_block,
            *piece_blocks, *piece_blocks,
        ],
        out_specs=[query_block, own_block, own_block] + [block(prompt_len // 2, head_dim)] * 4,
        out_shape=[jax.ShapeDtypeStruct((rows, width), BF16), own, own] + [half] * 4,
        compiler_params=PARAMS,
        cost_estimate=cost(10 * rows * width * (prompt_len + rows), 10**7),
        name="attend",
    )(length, queries, upstream, keys, values, *key_pieces, *value_pieces)


def in_vmem(kernel, name, outs, arrays, macs=0, scratch=()):
    whole = pl.BlockSpec(memory_space=pltpu.VMEM)
    results = pl.pallas_call(
        kernel,
        in_specs=[whole] * len(arrays),
        out_specs=[whole] * len(outs),
        out_shape=[jax.ShapeDtypeStruct(shape, dtype) for shape, dtype in outs],
        scratch_shapes=scratch,
        compiler_params=PARAMS,
        cost_estimate=cost(macs, 3 * 10**6),
        name=name,
    )(*arrays)
    return list(results)


def split_kernel(hidden_ref, *piece_refs):
    depth = piece_refs[0].shape[1]
    group = lax.axis_index("group")
    for k, piece_ref in enumerate(piece_refs):
        start = pl.multiple_of((group ^ k) * depth, depth)
        piece_ref[...] = hidden_ref[:, pl.ds(start, depth)]


def split_pass(hidden, groups):
    tokens, width = hidden.shape
    outs = [((tokens, width // groups), hidden.dtype)] * groups
    return in_vmem(split_kernel, "split_hidden", outs, [hidden])


def turn_kernel(groups, *refs):
    columns, piece_refs, turned = refs[:groups], refs[groups:-1], refs[-1]
    half = piece_refs[0].shape[0] // 2
    resp = lax.axis_index("resp")
    core, chip = resp % 2, resp // 2
    turned[...] = jnp.concatenate([ref[...] for ref in columns], axis=0).astype(F32).T
    for p, piece_ref in enumerate(piece_refs):
        start = (chip ^ p) * (2 * half)
        for i, part in enumerate((core, 1 - core)):
            rows = turned[pl.ds(pl.multiple_of(start + part * half, 8), half)]
            piece_ref[i * half : (i + 1) * half] = rows.astype(BF16)


def turn_pass(columns, chips):
    tokens, depth = columns[0].shape
    every = tokens * len(columns)
    outs = [((depth // chips, every), BF16)] * chips
    scratch = [pltpu.VMEM((depth, every), F32)]
    return in_vmem(partial(turn_kernel, len(columns)), "turn_hidden", outs, columns, 0, scratch)


def hidden_kernel(beside, across, own_ref, *refs):
    grads, refs = refs[: len(across) + 1], refs[len(across) + 1 :]
    near, far = refs[: len(beside)], refs[len(beside) : 2 * len(beside)]
    out_ref, *part_refs = refs[2 * len(beside) :]
    group, core = lax.axis_index("group"), lax.axis_index("resp") % 2
    depth, kv_width = own_ref.shape
    tokens, half = grads[0].shape[0], kv_width // 2
    near_grad = grads[0][:, pl.ds(pl.multiple_of(core * half, half), half)]
    far_grad = grads[0][:, pl.ds(pl.multiple_of((1 - core) * half, half), half)]

    def place(k, block):
        out_ref[:, pl.ds(pl.multiple_of((group ^ k) * depth, depth), depth)] = block

    own = dot(own_ref[...], jnp.concatenate([ref[...] for ref in grads], axis=0), 1, 1).T.astype(BF16)
    place(0, own[:tokens])
    for i, k in enumerate(across):
        part_refs[i][...] = own[(i + 1) * tokens : (i + 2) * tokens]
        place(k, jnp.zeros((tokens, depth), BF16))
    for i, k in enumerate(beside):
        block = dot(near[i][...], near_grad, 1, 1) + dot(far[i][...], far_grad, 1, 1)
        place(k, block.T.astype(BF16))


def hidden_pass(first, own, near, far, across):
    tokens, kv_width = first[0].shape
    depth = own.shape[0]
    outs = [((tokens, len(first) * depth), BF16)] + [((tokens, depth), BF16)] * len(across)
    arrays = [own, first[0], *[first[k] for k in across], *near.values(), *far.values()]
    kernel = partial(hidden_kernel, list(near), across)
    return in_vmem(kernel, "hidden_grad", outs, arrays, tokens * depth * kv_width * len(first))


def weight_kernel(chips, groups, second, *refs):
    taken, first, rest, out_ref = refs[:chips], refs[chips : chips + groups], refs[chips + groups : -1], refs[-1]
    half = out_ref.shape[0]
    start = half if second else 0
    columns = jnp.concatenate([ref[start : start + half] for ref in taken], axis=1)
    grads = [ref[...] for ref in first] + [ref[p] for p in range(chips - 1) for ref in rest]
    out_ref[...] = dot(columns, jnp.concatenate(grads, axis=0))


def weight_pass(taken, first, rest, second):
    rows, tokens = taken[0].shape
    kv_width = first[0].shape[-1]
    kernel = partial(weight_kernel, len(taken), len(first), second)
    macs = rows // 2 * kv_width * tokens * len(taken)
    outs = [((rows // 2, kv_width), F32)]
    return in_vmem(kernel, "weight_grad", outs, [*taken, *first, *rest], macs)[0]


def swap(array, axis, size, distance):
    return lax.ppermute(array, axis, [(i, i ^ distance) for i in range(size)])


def together(*arrays):
    return list(lax.optimization_barrier(arrays))


def spread_near(block, size):
    return [block] + [swap(block, "resp", size, k) for k in range(2, size, 2)]


def spread_far(near, size):
    return [swap(jnp.concatenate(near, axis=0), "resp", size, 1)]


def pair_sum(near, far, size):
    return near + swap(far, "resp", size, 1)


def chip_sum(near, size):
    rows = near.shape[0] // (size // 2)
    total = near[:rows]
    for p in range(1, size // 2):
        piece = near[p * rows : (p + 1) * rows].astype(BF16)
        total = total + swap(piece, "resp", size, 2 * p).astype(F32)
    return total


def shards(
    groups, responses, prompt_hidden, key_matrix, key_gain, prompt_token_value,
    resp_query, resp_key, response_value, grad_out, resp_length,
):
    hidden = prompt_hidden[0]
    tokens = hidden.shape[0]
    depth, kv_width = key_matrix.shape
    head_dim = key_gain.shape[0]
    chips = responses // 2
    beside = [k for k in range(1, groups) if k & (k - 1) == 0]
    across = [k for k in range(1, groups) if k & (k - 1)]

    pieces = split_pass(hidden, groups)
    columns = [swap(piece, "group", groups, k) if k else piece for k, piece in enumerate(pieces)]
    partials = [dot(piece, key_matrix) for piece in columns]
    prompt_value, partials[-1] = together(prompt_token_value[0], partials[-1])
    value_near = spread_near(prompt_value, responses)
    key_pre = partials[0]
    for k in range(1, groups):
        key_pre = key_pre + swap(partials[k], "group", groups, k)
    half_width = kv_width // 2
    start = (lax.axis_index("resp") % 2) * half_width
    half_weight = lax.dynamic_slice(key_matrix, (0, start), (depth, half_width))
    half_weight, key_pre = together(half_weight, key_pre)
    weight_near = [swap(half_weight, "group", groups, k) for k in beside]

    prompt_key = norm_keys(key_pre, key_gain).astype(BF16)
    key_near = spread_near(prompt_key, responses)
    value_pieces = value_near + spread_far(value_near, responses)

    taken = turn_pass(columns, chips)
    both = together(*taken, *key_near)
    taken, key_near = both[:chips], both[chips:]
    key_pieces = key_near + spread_far(key_near, responses)
    taken[1:] = [swap(taken[p], "resp", responses, 2 * p) for p in range(1, chips)]

    query_grad, key_grad, value_grad, key_sums, far, value_sums, value_far = attend(
        resp_length, resp_query[0, 0], grad_out[0, 0], key_pieces, value_pieces,
        resp_key[0, 0], response_value[0, 0], head_dim,
    )
    key_sums, far, *both = together(key_sums, far, *taken, *weight_near)
    taken, weight_near = both[:chips], both[chips:]
    key_sums = chip_sum(pair_sum(key_sums, far, responses), responses)
    value_sums = pair_sum(value_sums, value_far, responses)
    key_sums, value_sums = together(key_sums, value_sums)
    _, pullback = jax.vjp(lambda values: norm_keys(values, key_gain), key_pre)
    key_pre_grad = pullback(key_sums)[0].astype(BF16)

    first = [key_pre_grad] + [swap(key_pre_grad, "group", groups, k) for k in range(1, groups)]
    grads = spread_near(key_pre_grad, responses)[1:]
    weight_far = [swap(piece, "resp", responses, 1) for piece in weight_near]
    block, *both = together(jnp.stack(grads, axis=0), *first, *weight_far)
    first, weight_far = both[:groups], both[groups:]
    rest = [block] + [swap(block, "group", groups, k) for k in range(1, groups)]

    grad_hidden, *parts = hidden_pass(
        first, key_matrix, dict(zip(beside, weight_near)), dict(zip(beside, weight_far)), across
    )
    grad_hidden, value_sums = together(grad_hidden, value_sums)
    value_sums = chip_sum(value_sums, responses)
    grad_hidden, *both = together(grad_hidden, *parts, *rest)
    parts, rest = both[: len(parts)], both[len(parts) :]
    other = weight_pass(taken, first, rest, True)
    other, value_sums = together(other, value_sums)
    other = swap(other, "resp", responses, 1)
    grad_weight = weight_pass(taken, first, rest, False) + other
    for k, part in zip(across, parts):
        start = (lax.axis_index("group") ^ k) * depth
        grad_hidden = lax.dynamic_update_slice(grad_hidden, swap(part, "group", groups, k), (0, start))
    return (
        grad_hidden[None],
        grad_weight,
        value_sums.astype(BF16)[None],
        query_grad[None, None],
        key_grad[None, None],
        value_grad[None, None],
    )


def solution(mesh):
    return jax.shard_map(
        partial(shards, mesh.shape["group"], mesh.shape["resp"]),
        mesh=mesh,
        in_specs=(
            P("group", "resp", None),
            P("group", None),
            P(),
            P("group", "resp", None),
            P("group", "resp", None, None),
            P("group", "resp", None, None),
            P("group", "resp", None, None),
            P("group", "resp", None, None),
            P("group", "resp"),
        ),
        out_specs=(
            P("group", "resp", None),
            P(("group", "resp"), None),
            P("group", "resp", None),
            P("group", "resp", None, None),
            P("group", "resp", None, None),
            P("group", "resp", None, None),
        ),
        check_vma=False,
    )
```

```python
from functools import partial

import jax
import jax.numpy as jnp
from jax import lax
from jax.experimental import pallas as pl
from jax.experimental.pallas import tpu as pltpu
from jax.sharding import PartitionSpec as P

F32, BF16 = jnp.float32, jnp.bfloat16
LOG2E = 1.4426950408889634
PARAMS = pltpu.CompilerParams(vmem_limit_bytes=56 * 2**20)


def norm_keys(key_pre, key_gain):
    shaped = key_pre.reshape(key_pre.shape[:-1] + (-1, key_gain.shape[0]))
    inverse = lax.rsqrt(jnp.mean(shaped * shaped, axis=-1, keepdims=True) + 1e-06)
    return (shaped * inverse * key_gain).reshape(key_pre.shape)


def dot(left, right, left_dim=1, right_dim=0):
    dims = (((left_dim,), (right_dim,)), ((), ()))
    return lax.dot_general(left, right, dims, preferred_element_type=F32)


def cost(macs, nbytes):
    return pl.CostEstimate(flops=2 * macs, bytes_accessed=nbytes, transcendentals=0)


def stack_heads(ref, head_dim):
    heads = ref.shape[1] // head_dim
    return jnp.concatenate([ref[:, i * head_dim : (i + 1) * head_dim] for i in range(heads)], axis=0)


def attend_kernel(pieces, length_ref, query_ref, upstream_ref, key_ref, value_ref, *refs):
    key_pieces, value_pieces = refs[:pieces], refs[pieces : 2 * pieces]
    query_grad_ref, key_grad_ref, value_grad_ref, *sum_refs = refs[2 * pieces :]
    rows = query_ref.shape[0]
    own_len, head_dim = key_ref.shape
    heads = query_ref.shape[1] // head_dim
    scale = head_dim ** -0.5
    keys = jnp.concatenate([ref[...] for ref in key_pieces] + [key_ref[...]], axis=0)
    values = jnp.concatenate([ref[...] for ref in value_pieces] + [value_ref[...]], axis=0)
    keys_t, values_t = keys.T, values.T
    prompt_len = keys.shape[0] - own_len
    queries, upstream = stack_heads(query_ref, head_dim), stack_heads(upstream_ref, head_dim)
    stacked = heads * rows
    live = lax.broadcasted_iota(jnp.int32, (stacked, 1), 0) % rows < length_ref[0, 0]
    own = (stacked, own_len)
    visible = lax.broadcasted_iota(jnp.int32, own, 1) <= lax.broadcasted_iota(jnp.int32, own, 0) % rows
    prompt_scores = dot(queries, keys_t[:, :prompt_len])
    own_scores = jnp.where(visible, dot(queries, keys_t[:, prompt_len:]), -jnp.inf)
    row_max = jnp.maximum(
        jnp.max(prompt_scores, axis=1, keepdims=True), jnp.max(own_scores, axis=1, keepdims=True)
    )
    scores = jnp.concatenate([prompt_scores, own_scores], axis=1)
    unit = scale * LOG2E
    exponent = jnp.exp2(scores * unit - row_max * unit)
    dprob = dot(upstream, values_t)
    total = jnp.sum(exponent, axis=1, keepdims=True)
    weighted = jnp.sum(exponent * dprob, axis=1, keepdims=True)
    inverse = jnp.where(live, 1.0 / total, 0.0)
    row_delta = weighted * inverse
    weights = (exponent * inverse).astype(BF16)
    dscore = (exponent * ((dprob - row_delta) * (inverse * scale))).astype(BF16)
    query_grad = dot(dscore, keys).astype(BF16)
    for i in range(heads):
        query_grad_ref[:, i * head_dim : (i + 1) * head_dim] = query_grad[i * rows : (i + 1) * rows]
    key_grad = dot(queries.T, dscore).T
    value_grad = dot(upstream.T, weights).T
    half = prompt_len // 2
    for i, grad in enumerate((key_grad, value_grad)):
        sum_refs[2 * i][...], sum_refs[2 * i + 1][...] = grad[:half], grad[half:prompt_len]
    key_grad_ref[...] = key_grad[prompt_len:].astype(BF16)
    value_grad_ref[...] = value_grad[prompt_len:].astype(BF16)


def attend(length, queries, upstream, key_pieces, value_pieces, keys, values, head_dim):
    rows, width = queries.shape
    kv_width = keys.shape[1]
    kv_heads = kv_width // head_dim
    prompt_len = sum(piece.shape[0] for piece in key_pieces)

    def block(rows, columns):
        return pl.BlockSpec((rows, columns), lambda i: (0, i))

    query_block, own_block = block(rows, width // kv_heads), block(rows, head_dim)
    piece_blocks = [block(piece.shape[0], head_dim) for piece in key_pieces]
    half = jax.ShapeDtypeStruct((prompt_len // 2, kv_width), F32)
    own = jax.ShapeDtypeStruct((rows, kv_width), BF16)
    return pl.pallas_call(
        partial(attend_kernel, len(key_pieces)),
        grid=(kv_heads,),
        in_specs=[
            pl.BlockSpec(memory_space=pltpu.SMEM), query_block, query_block, own_block, own_block,
            *piece_blocks, *piece_blocks,
        ],
        out_specs=[query_block, own_block, own_block] + [block(prompt_len // 2, head_dim)] * 4,
        out_shape=[jax.ShapeDtypeStruct((rows, width), BF16), own, own] + [half] * 4,
        compiler_params=PARAMS,
        cost_estimate=cost(10 * rows * width * (prompt_len + rows), 10**7),
        name="attend",
    )(length, queries, upstream, keys, values, *key_pieces, *value_pieces)


def in_vmem(kernel, name, outs, arrays, macs=0, scratch=()):
    whole = pl.BlockSpec(memory_space=pltpu.VMEM)
    results = pl.pallas_call(
        kernel,
        in_specs=[whole] * len(arrays),
        out_specs=[whole] * len(outs),
        out_shape=[jax.ShapeDtypeStruct(shape, dtype) for shape, dtype in outs],
        scratch_shapes=scratch,
        compiler_params=PARAMS,
        cost_estimate=cost(macs, 3 * 10**6),
        name=name,
    )(*arrays)
    return list(results)


def split_kernel(hidden_ref, *refs):
    *piece_refs, arrived = refs
    depth = piece_refs[0].shape[1]
    group = lax.axis_index("group")
    copies = []
    for k, piece_ref in enumerate(piece_refs):
        start = pl.multiple_of((group ^ k) * depth, depth)
        copies.append(pltpu.make_async_copy(hidden_ref.at[:, pl.ds(start, depth)], piece_ref, arrived.at[k]))
        copies[-1].start()
    for copy in copies:
        copy.wait()


def split_pass(hidden, groups):
    tokens, width = hidden.shape
    anywhere = pl.BlockSpec(memory_space=pl.ANY)
    return list(pl.pallas_call(
        split_kernel,
        in_specs=[anywhere],
        out_specs=[anywhere] * groups,
        out_shape=[jax.ShapeDtypeStruct((tokens, width // groups), hidden.dtype)] * groups,
        scratch_shapes=[pltpu.SemaphoreType.DMA((groups,))],
        compiler_params=PARAMS,
        name="split_hidden",
    )(hidden))


def turn_kernel(groups, *refs):
    columns, piece_refs, turned = refs[:groups], refs[groups:-1], refs[-1]
    half = piece_refs[0].shape[0] // 2
    resp = lax.axis_index("resp")
    core, chip = resp % 2, resp // 2
    turned[...] = jnp.concatenate([ref[...] for ref in columns], axis=0).astype(F32).T
    for p, piece_ref in enumerate(piece_refs):
        start = (chip ^ p) * (2 * half)
        for i, part in enumerate((core, 1 - core)):
            rows = turned[pl.ds(pl.multiple_of(start + part * half, 8), half)]
            piece_ref[i * half : (i + 1) * half] = rows.astype(BF16)


def turn_pass(columns, chips):
    tokens, depth = columns[0].shape
    every = tokens * len(columns)
    outs = [((depth // chips, every), BF16)] * chips
    scratch = [pltpu.VMEM((depth, every), F32)]
    return in_vmem(partial(turn_kernel, len(columns)), "turn_hidden", outs, columns, 0, scratch)


def hidden_kernel(beside, across, own_ref, *refs):
    grads, refs = refs[: len(across) + 1], refs[len(across) + 1 :]
    near, far = refs[: len(beside)], refs[len(beside) : 2 * len(beside)]
    out_ref, *part_refs = refs[2 * len(beside) :]
    group, core = lax.axis_index("group"), lax.axis_index("resp") % 2
    depth, kv_width = own_ref.shape
    tokens, half = grads[0].shape[0], kv_width // 2
    near_grad = grads[0][:, pl.ds(pl.multiple_of(core * half, half), half)]
    far_grad = grads[0][:, pl.ds(pl.multiple_of((1 - core) * half, half), half)]

    def place(k, block):
        out_ref[:, pl.ds(pl.multiple_of((group ^ k) * depth, depth), depth)] = block

    own = dot(own_ref[...], jnp.concatenate([ref[...] for ref in grads], axis=0), 1, 1).T.astype(BF16)
    place(0, own[:tokens])
    for i, k in enumerate(across):
        part_refs[i][...] = own[(i + 1) * tokens : (i + 2) * tokens]
        place(k, jnp.zeros((tokens, depth), BF16))
    for i, k in enumerate(beside):
        block = dot(near[i][...], near_grad, 1, 1) + dot(far[i][...], far_grad, 1, 1)
        place(k, block.T.astype(BF16))


def hidden_pass(key_pre_grad, first, own, near, far):
    tokens, kv_width = key_pre_grad.shape
    depth = own.shape[0]
    groups = 1 + len(first) + len(near)
    outs = [((tokens, groups * depth), BF16)] + [((tokens, depth), BF16)] * len(first)
    arrays = [own, key_pre_grad, *first.values(), *near.values(), *far.values()]
    kernel = partial(hidden_kernel, list(near), list(first))
    return in_vmem(kernel, "hidden_grad", outs, arrays, tokens * depth * kv_width * groups)


def weight_pass(taken, blocks):
    rows, tokens = taken[0].shape
    chips, groups = len(taken), len(blocks)
    token_rows = tokens // groups
    kv_width = blocks[0][0].shape[1]
    counts = [len(arrays) for arrays in blocks]

    def kernel(*refs):
        columns = jnp.concatenate([ref[...] for ref in refs[:chips]], axis=1)
        parts = [jnp.concatenate([ref[...] for ref in arrays], axis=0) for arrays in nested(refs[chips:-2], counts)]
        grads = [part[p * token_rows : (p + 1) * token_rows] for p in range(chips) for part in parts]
        product = dot(columns, jnp.concatenate(grads, axis=0))
        refs[-2][...], refs[-1][...] = product[: rows // 2], product[rows // 2 :]

    outs = [((rows // 2, kv_width), F32)] * 2
    arrays = [*taken, *[array for arrays in blocks for array in arrays]]
    return in_vmem(kernel, "weight_grad", outs, arrays, rows * kv_width * tokens * chips)


def nested(items, counts):
    items = iter(items)
    return [[next(items) for _ in range(count)] for count in counts]


def swap(array, axis, size, distance):
    return lax.ppermute(array, axis, [(i, i ^ distance) for i in range(size)])


def together(*arrays):
    return list(lax.optimization_barrier(arrays))


def spread_near(block, size):
    return [block] + [swap(block, "resp", size, k) for k in range(2, size, 2)]


def spread_far(near, size):
    return [swap(jnp.concatenate(near, axis=0), "resp", size, 1)]


def pair_sum(near, far, size):
    return near + swap(far, "resp", size, 1)


def chip_parts(near, size):
    rows = near.shape[0] // (size // 2)
    pieces = [near[p * rows : (p + 1) * rows] for p in range(size // 2)]
    return pieces[:1] + [swap(pieces[p].astype(BF16), "resp", size, 2 * p) for p in range(1, size // 2)]


def total(parts):
    return sum(part.astype(F32) for part in parts[1:]) + parts[0]


def shards(
    groups, responses, prompt_hidden, key_matrix, key_gain, prompt_token_value,
    resp_query, resp_key, response_value, grad_out, resp_length,
):
    hidden = prompt_hidden[0]
    tokens = hidden.shape[0]
    depth, kv_width = key_matrix.shape
    head_dim = key_gain.shape[0]
    chips = responses // 2
    beside = [k for k in range(1, groups) if k & (k - 1) == 0]
    across = [k for k in range(1, groups) if k & (k - 1)]

    pieces = split_pass(hidden, groups)
    columns = [swap(piece, "group", groups, k) if k else piece for k, piece in enumerate(pieces)]
    partials = [dot(piece, key_matrix) for piece in columns]
    prompt_value, partials[-1] = together(prompt_token_value[0], partials[-1])
    value_near = spread_near(prompt_value, responses)
    key_pre = partials[0]
    for k in range(1, groups):
        key_pre = key_pre + swap(partials[k], "group", groups, k)
    half_width = kv_width // 2
    start = (lax.axis_index("resp") % 2) * half_width
    half_weight = lax.dynamic_slice(key_matrix, (0, start), (depth, half_width))
    half_weight, key_pre = together(half_weight, key_pre)
    weight_near = [swap(half_weight, "group", groups, k) for k in beside]

    prompt_key = norm_keys(key_pre, key_gain).astype(BF16)
    key_near = spread_near(prompt_key, responses)
    value_pieces = value_near + spread_far(value_near, responses)

    taken = turn_pass(columns, chips)
    both = together(*taken, *key_near)
    taken, key_near = both[:chips], both[chips:]
    key_pieces = key_near + spread_far(key_near, responses)
    taken[1:] = [swap(taken[p], "resp", responses, 2 * p) for p in range(1, chips)]

    query_grad, key_grad, value_grad, key_sums, far, value_sums, value_far = attend(
        resp_length, resp_query[0, 0], grad_out[0, 0], key_pieces, value_pieces,
        resp_key[0, 0], response_value[0, 0], head_dim,
    )
    key_sums, far, *both = together(key_sums, far, *taken, *weight_near)
    taken, weight_near = both[:chips], both[chips:]
    key_sums = total(chip_parts(pair_sum(key_sums, far, responses), responses))
    value_sums = pair_sum(value_sums, value_far, responses)
    weight_far = [swap(piece, "resp", responses, 1) for piece in weight_near]
    key_sums, value_sums, *weight_far = together(key_sums, value_sums, *weight_far)
    _, pullback = jax.vjp(lambda values: norm_keys(values, key_gain), key_pre)
    key_pre_grad = pullback(key_sums)[0].astype(BF16)

    first = {k: swap(key_pre_grad, "group", groups, k) for k in across}
    grads = spread_near(key_pre_grad, responses)
    grad_hidden, *parts = hidden_pass(
        key_pre_grad, first, key_matrix, dict(zip(beside, weight_near)), dict(zip(beside, weight_far))
    )

    grad_hidden, *both = together(grad_hidden, *parts, *grads)
    parts, grads = both[: len(parts)], both[len(parts) :]
    some, every = jnp.concatenate(grads[1:], axis=0), jnp.concatenate(grads, axis=0)
    blocks = [[every]] + [None] * (groups - 1)
    for k in beside:
        blocks[k] = [swap(every, "group", groups, k)]
    for k in across:
        blocks[k] = [first[k], swap(some, "group", groups, k)]
    grad_hidden, value_sums = together(grad_hidden, value_sums)
    value_parts = chip_parts(value_sums, responses)
    for k in across:
        *parts, blocks[k][-1] = together(*parts, blocks[k][-1])
    parts = [swap(part, "group", groups, k) for k, part in zip(across, parts)]
    mine, other, *value_parts = together(*weight_pass(taken, blocks), *value_parts)
    value_sums = total(value_parts)
    grad_weight = mine + swap(other, "resp", responses, 1)
    for k, part in zip(across, parts):
        start = (lax.axis_index("group") ^ k) * depth
        grad_hidden = lax.dynamic_update_slice(grad_hidden, part, (0, start))
    return (
        grad_hidden[None],
        grad_weight,
        value_sums.astype(BF16)[None],
        query_grad[None, None],
        key_grad[None, None],
        value_grad[None, None],
    )


def solution(mesh):
    return jax.shard_map(
        partial(shards, mesh.shape["group"], mesh.shape["resp"]),
        mesh=mesh,
        in_specs=(
            P("group", "resp", None),
            P("group", None),
            P(),
            P("group", "resp", None),
            P("group", "resp", None, None),
            P("group", "resp", None, None),
            P("group", "resp", None, None),
            P("group", "resp", None, None),
            P("group", "resp"),
        ),
        out_specs=(
            P("group", "resp", None),
            P(("group", "resp"), None),
            P("group", "resp", None),
            P("group", "resp", None, None),
            P("group", "resp", None, None),
            P("group", "resp", None, None),
        ),
        check_vma=False,
    )
```

```python
from functools import partial

import jax
import jax.numpy as jnp
from jax import lax
from jax.experimental import pallas as pl
from jax.experimental.pallas import tpu as pltpu
from jax.sharding import PartitionSpec as P

F32, BF16 = jnp.float32, jnp.bfloat16
LOG2E = 1.4426950408889634
PARAMS = pltpu.CompilerParams(vmem_limit_bytes=56 * 2**20)


def norm_keys(key_pre, key_gain):
    shaped = key_pre.reshape(key_pre.shape[:-1] + (-1, key_gain.shape[0]))
    inverse = lax.rsqrt(jnp.mean(shaped * shaped, axis=-1, keepdims=True) + 1e-06)
    return (shaped * inverse * key_gain).reshape(key_pre.shape)


def dot(left, right, left_dim=1, right_dim=0):
    dims = (((left_dim,), (right_dim,)), ((), ()))
    return lax.dot_general(left, right, dims, preferred_element_type=F32)


def cost(macs, nbytes):
    return pl.CostEstimate(flops=2 * macs, bytes_accessed=nbytes, transcendentals=0)


def stack_heads(ref, head_dim):
    heads = ref.shape[1] // head_dim
    return jnp.concatenate([ref[:, i * head_dim : (i + 1) * head_dim] for i in range(heads)], axis=0)


def attend_kernel(pieces, length_ref, query_ref, upstream_ref, key_ref, value_ref, *refs):
    key_pieces, value_pieces = refs[:pieces], refs[pieces : 2 * pieces]
    query_grad_ref, key_grad_ref, value_grad_ref, *sum_refs = refs[2 * pieces :]
    rows = query_ref.shape[0]
    own_len, head_dim = key_ref.shape
    heads = query_ref.shape[1] // head_dim
    scale = head_dim ** -0.5
    keys = jnp.concatenate([ref[...] for ref in key_pieces] + [key_ref[...]], axis=0)
    values = jnp.concatenate([ref[...] for ref in value_pieces] + [value_ref[...]], axis=0)
    keys_t, values_t = keys.T, values.T
    prompt_len = keys.shape[0] - own_len
    queries, upstream = stack_heads(query_ref, head_dim), stack_heads(upstream_ref, head_dim)
    stacked = heads * rows
    live = lax.broadcasted_iota(jnp.int32, (stacked, 1), 0) % rows < length_ref[0, 0]
    own = (stacked, own_len)
    visible = lax.broadcasted_iota(jnp.int32, own, 1) <= lax.broadcasted_iota(jnp.int32, own, 0) % rows
    prompt_scores = dot(queries, keys_t[:, :prompt_len])
    own_scores = jnp.where(visible, dot(queries, keys_t[:, prompt_len:]), -jnp.inf)
    row_max = jnp.maximum(
        jnp.max(prompt_scores, axis=1, keepdims=True), jnp.max(own_scores, axis=1, keepdims=True)
    )
    scores = jnp.concatenate([prompt_scores, own_scores], axis=1)
    unit = scale * LOG2E
    exponent = jnp.exp2(scores * unit - row_max * unit)
    dprob = dot(upstream, values_t)
    total = jnp.sum(exponent, axis=1, keepdims=True)
    weighted = jnp.sum(exponent * dprob, axis=1, keepdims=True)
    inverse = jnp.where(live, 1.0 / total, 0.0)
    row_delta = weighted * inverse
    weights = (exponent * inverse).astype(BF16)
    dscore = (exponent * ((dprob - row_delta) * (inverse * scale))).astype(BF16)
    query_grad = dot(dscore, keys).astype(BF16)
    for i in range(heads):
        query_grad_ref[:, i * head_dim : (i + 1) * head_dim] = query_grad[i * rows : (i + 1) * rows]
    key_grad = dot(queries.T, dscore).T
    value_grad = dot(upstream.T, weights).T
    half = prompt_len // 2
    for i, grad in enumerate((key_grad, value_grad)):
        sum_refs[2 * i][...], sum_refs[2 * i + 1][...] = grad[:half], grad[half:prompt_len]
    key_grad_ref[...] = key_grad[prompt_len:].astype(BF16)
    value_grad_ref[...] = value_grad[prompt_len:].astype(BF16)


def attend(length, queries, upstream, key_pieces, value_pieces, keys, values, head_dim):
    rows, width = queries.shape
    kv_width = keys.shape[1]
    kv_heads = kv_width // head_dim
    prompt_len = sum(piece.shape[0] for piece in key_pieces)

    def block(rows, columns):
        return pl.BlockSpec((rows, columns), lambda i: (0, i))

    query_block, own_block = block(rows, width // kv_heads), block(rows, head_dim)
    piece_blocks = [block(piece.shape[0], head_dim) for piece in key_pieces]
    half = jax.ShapeDtypeStruct((prompt_len // 2, kv_width), F32)
    own = jax.ShapeDtypeStruct((rows, kv_width), BF16)
    return pl.pallas_call(
        partial(attend_kernel, len(key_pieces)),
        grid=(kv_heads,),
        in_specs=[
            pl.BlockSpec(memory_space=pltpu.SMEM), query_block, query_block, own_block, own_block,
            *piece_blocks, *piece_blocks,
        ],
        out_specs=[query_block, own_block, own_block] + [block(prompt_len // 2, head_dim)] * 4,
        out_shape=[jax.ShapeDtypeStruct((rows, width), BF16), own, own] + [half] * 4,
        compiler_params=PARAMS,
        cost_estimate=cost(10 * rows * width * (prompt_len + rows), 10**7),
        name="attend",
    )(length, queries, upstream, keys, values, *key_pieces, *value_pieces)


def in_vmem(kernel, name, outs, arrays, macs=0, scratch=()):
    whole = pl.BlockSpec(memory_space=pltpu.VMEM)
    results = pl.pallas_call(
        kernel,
        in_specs=[whole] * len(arrays),
        out_specs=[whole] * len(outs),
        out_shape=[jax.ShapeDtypeStruct(shape, dtype) for shape, dtype in outs],
        scratch_shapes=scratch,
        compiler_params=PARAMS,
        cost_estimate=cost(macs, 3 * 10**6),
        name=name,
    )(*arrays)
    return list(results)


def split_kernel(hidden_ref, *piece_refs):
    depth = piece_refs[0].shape[1]
    group = lax.axis_index("group")
    for k, piece_ref in enumerate(piece_refs):
        start = pl.multiple_of((group ^ k) * depth, depth)
        piece_ref[...] = hidden_ref[:, pl.ds(start, depth)]


def split_pass(hidden, groups):
    tokens, width = hidden.shape
    outs = [((tokens, width // groups), hidden.dtype)] * groups
    return in_vmem(split_kernel, "split_hidden", outs, [hidden])


def turn_kernel(groups, *refs):
    columns, piece_refs, turned = refs[:groups], refs[groups:-1], refs[-1]
    half = piece_refs[0].shape[0] // 2
    resp = lax.axis_index("resp")
    core, chip = resp % 2, resp // 2
    turned[...] = jnp.concatenate([ref[...] for ref in columns], axis=0).astype(F32).T
    for p, piece_ref in enumerate(piece_refs):
        start = (chip ^ p) * (2 * half)
        for i, part in enumerate((core, 1 - core)):
            rows = turned[pl.ds(pl.multiple_of(start + part * half, 8), half)]
            piece_ref[i * half : (i + 1) * half] = rows.astype(BF16)


def turn_pass(columns, chips):
    tokens, depth = columns[0].shape
    every = tokens * len(columns)
    outs = [((depth // chips, every), BF16)] * chips
    scratch = [pltpu.VMEM((depth, every), F32)]
    return in_vmem(partial(turn_kernel, len(columns)), "turn_hidden", outs, columns, 0, scratch)


def hidden_kernel(beside, across, own_ref, *refs):
    grads, refs = refs[: len(across) + 1], refs[len(across) + 1 :]
    near, far = refs[: len(beside)], refs[len(beside) : 2 * len(beside)]
    out_ref, *part_refs = refs[2 * len(beside) :]
    group, core = lax.axis_index("group"), lax.axis_index("resp") % 2
    depth, kv_width = own_ref.shape
    tokens, half = grads[0].shape[0], kv_width // 2
    near_grad = grads[0][:, pl.ds(pl.multiple_of(core * half, half), half)]
    far_grad = grads[0][:, pl.ds(pl.multiple_of((1 - core) * half, half), half)]

    def place(k, block):
        out_ref[:, pl.ds(pl.multiple_of((group ^ k) * depth, depth), depth)] = block

    own = dot(own_ref[...], jnp.concatenate([ref[...] for ref in grads], axis=0), 1, 1).T.astype(BF16)
    place(0, own[:tokens])
    for i, k in enumerate(across):
        part_refs[i][...] = own[(i + 1) * tokens : (i + 2) * tokens]
        place(k, jnp.zeros((tokens, depth), BF16))
    for i, k in enumerate(beside):
        block = dot(near[i][...], near_grad, 1, 1) + dot(far[i][...], far_grad, 1, 1)
        place(k, block.T.astype(BF16))


def hidden_pass(key_pre_grad, first, own, near, far):
    tokens, kv_width = key_pre_grad.shape
    depth = own.shape[0]
    groups = 1 + len(first) + len(near)
    outs = [((tokens, groups * depth), BF16)] + [((tokens, depth), BF16)] * len(first)
    arrays = [own, key_pre_grad, *first.values(), *near.values(), *far.values()]
    kernel = partial(hidden_kernel, list(near), list(first))
    return in_vmem(kernel, "hidden_grad", outs, arrays, tokens * depth * kv_width * groups)


def weight_pass(taken, blocks):
    rows, tokens = taken[0].shape
    chips, groups = len(taken), len(blocks)
    token_rows = tokens // groups
    kv_width = blocks[0][0].shape[1]
    counts = [len(arrays) for arrays in blocks]

    def kernel(*refs):
        columns = jnp.concatenate([ref[...] for ref in refs[:chips]], axis=1)
        parts = [jnp.concatenate([ref[...] for ref in arrays], axis=0) for arrays in nested(refs[chips:-2], counts)]
        grads = [part[p * token_rows : (p + 1) * token_rows] for p in range(chips) for part in parts]
        product = dot(columns, jnp.concatenate(grads, axis=0))
        refs[-2][...], refs[-1][...] = product[: rows // 2], product[rows // 2 :]

    outs = [((rows // 2, kv_width), F32)] * 2
    arrays = [*taken, *[array for arrays in blocks for array in arrays]]
    return in_vmem(kernel, "weight_grad", outs, arrays, rows * kv_width * tokens * chips)


def nested(items, counts):
    items = iter(items)
    return [[next(items) for _ in range(count)] for count in counts]


def swap(array, axis, size, distance):
    return lax.ppermute(array, axis, [(i, i ^ distance) for i in range(size)])


def together(*arrays):
    return list(lax.optimization_barrier(arrays))


def spread_near(block, size):
    return [block] + [swap(block, "resp", size, k) for k in range(2, size, 2)]


def spread_far(near, size):
    return [swap(jnp.concatenate(near, axis=0), "resp", size, 1)]


def pair_sum(near, far, size):
    return near + swap(far, "resp", size, 1)


def chip_parts(near, size):
    rows = near.shape[0] // (size // 2)
    pieces = [near[p * rows : (p + 1) * rows] for p in range(size // 2)]
    return pieces[:1] + [swap(pieces[p].astype(BF16), "resp", size, 2 * p) for p in range(1, size // 2)]


def total(parts):
    return sum(part.astype(F32) for part in parts[1:]) + parts[0]


def shards(
    groups, responses, prompt_hidden, key_matrix, key_gain, prompt_token_value,
    resp_query, resp_key, response_value, grad_out, resp_length,
):
    hidden = prompt_hidden[0]
    tokens = hidden.shape[0]
    depth, kv_width = key_matrix.shape
    head_dim = key_gain.shape[0]
    chips = responses // 2
    beside = [k for k in range(1, groups) if k & (k - 1) == 0]
    across = [k for k in range(1, groups) if k & (k - 1)]

    pieces = split_pass(hidden, groups)
    columns = [swap(piece, "group", groups, k) if k else piece for k, piece in enumerate(pieces)]
    partials = [dot(piece, key_matrix) for piece in columns]
    prompt_value, partials[-1] = together(prompt_token_value[0], partials[-1])
    value_near = spread_near(prompt_value, responses)
    key_pre = partials[0]
    for k in range(1, groups):
        key_pre = key_pre + swap(partials[k], "group", groups, k)
    half_width = kv_width // 2
    start = (lax.axis_index("resp") % 2) * half_width
    half_weight = lax.dynamic_slice(key_matrix, (0, start), (depth, half_width))
    half_weight, key_pre = together(half_weight, key_pre)
    weight_near = [swap(half_weight, "group", groups, k) for k in beside]

    prompt_key = norm_keys(key_pre, key_gain).astype(BF16)
    key_near = spread_near(prompt_key, responses)
    value_pieces = value_near + spread_far(value_near, responses)

    taken = turn_pass(columns, chips)
    both = together(*taken, *key_near)
    taken, key_near = both[:chips], both[chips:]
    key_pieces = key_near + spread_far(key_near, responses)
    taken[1:] = [swap(taken[p], "resp", responses, 2 * p) for p in range(1, chips)]

    query_grad, key_grad, value_grad, key_sums, far, value_sums, value_far = attend(
        resp_length, resp_query[0, 0], grad_out[0, 0], key_pieces, value_pieces,
        resp_key[0, 0], response_value[0, 0], head_dim,
    )
    key_sums, far, *both = together(key_sums, far, *taken, *weight_near)
    taken, weight_near = both[:chips], both[chips:]
    key_sums = total(chip_parts(pair_sum(key_sums, far, responses), responses))
    value_sums = pair_sum(value_sums, value_far, responses)
    weight_far = [swap(piece, "resp", responses, 1) for piece in weight_near]
    key_sums, value_sums, *weight_far = together(key_sums, value_sums, *weight_far)
    _, pullback = jax.vjp(lambda values: norm_keys(values, key_gain), key_pre)
    key_pre_grad = pullback(key_sums)[0].astype(BF16)

    first = {k: swap(key_pre_grad, "group", groups, k) for k in across}
    grads = spread_near(key_pre_grad, responses)
    grad_hidden, *parts = hidden_pass(
        key_pre_grad, first, key_matrix, dict(zip(beside, weight_near)), dict(zip(beside, weight_far))
    )

    grad_hidden, *both = together(grad_hidden, *parts, *grads)
    parts, grads = both[: len(parts)], both[len(parts) :]
    some, every = jnp.concatenate(grads[1:], axis=0), jnp.concatenate(grads, axis=0)
    blocks = [[every]] + [None] * (groups - 1)
    for k in beside:
        blocks[k] = [swap(every, "group", groups, k)]
    for k in across:
        blocks[k] = [first[k], swap(some, "group", groups, k)]
    grad_hidden, value_sums = together(grad_hidden, value_sums)
    value_parts = chip_parts(value_sums, responses)
    for k in across:
        *parts, blocks[k][-1] = together(*parts, blocks[k][-1])
    parts = [swap(part, "group", groups, k) for k, part in zip(across, parts)]
    mine, other, *value_parts = together(*weight_pass(taken, blocks), *value_parts)
    value_sums = total(value_parts)
    grad_weight = mine + swap(other, "resp", responses, 1)
    for k, part in zip(across, parts):
        start = (lax.axis_index("group") ^ k) * depth
        grad_hidden = lax.dynamic_update_slice(grad_hidden, part, (0, start))
    return (
        grad_hidden[None],
        grad_weight,
        value_sums.astype(BF16)[None],
        query_grad[None, None],
        key_grad[None, None],
        value_grad[None, None],
    )


def solution(mesh):
    return jax.shard_map(
        partial(shards, mesh.shape["group"], mesh.shape["resp"]),
        mesh=mesh,
        in_specs=(
            P("group", "resp", None),
            P("group", None),
            P(),
            P("group", "resp", None),
            P("group", "resp", None, None),
            P("group", "resp", None, None),
            P("group", "resp", None, None),
            P("group", "resp", None, None),
            P("group", "resp"),
        ),
        out_specs=(
            P("group", "resp", None),
            P(("group", "resp"), None),
            P("group", "resp", None),
            P("group", "resp", None, None),
            P("group", "resp", None, None),
            P("group", "resp", None, None),
        ),
        check_vma=False,
    )
```

```python
from functools import partial

import jax
import jax.numpy as jnp
from jax import lax
from jax.experimental import pallas as pl
from jax.experimental.pallas import tpu as pltpu
from jax.sharding import PartitionSpec as P

F32, BF16 = jnp.float32, jnp.bfloat16
LOG2E = 1.4426950408889634
PARAMS = pltpu.CompilerParams(vmem_limit_bytes=56 * 2**20)


def norm_keys(key_pre, key_gain):
    shaped = key_pre.reshape(key_pre.shape[:-1] + (-1, key_gain.shape[0]))
    inverse = lax.rsqrt(jnp.mean(shaped * shaped, axis=-1, keepdims=True) + 1e-06)
    return (shaped * inverse * key_gain).reshape(key_pre.shape)


def dot(left, right, left_dim=1, right_dim=0):
    dims = (((left_dim,), (right_dim,)), ((), ()))
    return lax.dot_general(left, right, dims, preferred_element_type=F32)


def cost(macs, nbytes):
    return pl.CostEstimate(flops=2 * macs, bytes_accessed=nbytes, transcendentals=0)


def stack_heads(ref, head_dim):
    heads = ref.shape[1] // head_dim
    return jnp.concatenate([ref[:, i * head_dim : (i + 1) * head_dim] for i in range(heads)], axis=0)


def attend_kernel(pieces, length_ref, query_ref, upstream_ref, key_ref, value_ref, *refs):
    key_pieces, value_pieces = refs[:pieces], refs[pieces : 2 * pieces]
    query_grad_ref, key_grad_ref, value_grad_ref, *sum_refs = refs[2 * pieces :]
    rows = query_ref.shape[0]
    own_len, head_dim = key_ref.shape
    heads = query_ref.shape[1] // head_dim
    scale = head_dim ** -0.5
    keys = jnp.concatenate([ref[...] for ref in key_pieces] + [key_ref[...]], axis=0)
    values = jnp.concatenate([ref[...] for ref in value_pieces] + [value_ref[...]], axis=0)
    keys_t, values_t = keys.T, values.T
    prompt_len = keys.shape[0] - own_len
    queries, upstream = stack_heads(query_ref, head_dim), stack_heads(upstream_ref, head_dim)
    stacked = heads * rows
    live = lax.broadcasted_iota(jnp.int32, (stacked, 1), 0) % rows < length_ref[0, 0]
    own = (stacked, own_len)
    visible = lax.broadcasted_iota(jnp.int32, own, 1) <= lax.broadcasted_iota(jnp.int32, own, 0) % rows
    prompt_scores = dot(queries, keys_t[:, :prompt_len])
    own_scores = jnp.where(visible, dot(queries, keys_t[:, prompt_len:]), -jnp.inf)
    row_max = jnp.maximum(
        jnp.max(prompt_scores, axis=1, keepdims=True), jnp.max(own_scores, axis=1, keepdims=True)
    )
    scores = jnp.concatenate([prompt_scores, own_scores], axis=1)
    unit = scale * LOG2E
    exponent = jnp.exp2(scores * unit - row_max * unit)
    dprob = dot(upstream, values_t)
    total = jnp.sum(exponent, axis=1, keepdims=True)
    weighted = jnp.sum(exponent * dprob, axis=1, keepdims=True)
    inverse = jnp.where(live, 1.0 / total, 0.0)
    row_delta = weighted * inverse
    weights = (exponent * inverse).astype(BF16)
    dscore = (exponent * ((dprob - row_delta) * (inverse * scale))).astype(BF16)
    query_grad = dot(dscore, keys).astype(BF16)
    for i in range(heads):
        query_grad_ref[:, i * head_dim : (i + 1) * head_dim] = query_grad[i * rows : (i + 1) * rows]
    key_grad = dot(queries.T, dscore).T
    value_grad = dot(upstream.T, weights).T
    half = prompt_len // 2
    for i, grad in enumerate((key_grad, value_grad)):
        sum_refs[2 * i][...], sum_refs[2 * i + 1][...] = grad[:half], grad[half:prompt_len]
    key_grad_ref[...] = key_grad[prompt_len:].astype(BF16)
    value_grad_ref[...] = value_grad[prompt_len:].astype(BF16)


def attend(length, queries, upstream, key_pieces, value_pieces, keys, values, head_dim):
    rows, width = queries.shape
    kv_width = keys.shape[1]
    kv_heads = kv_width // head_dim
    prompt_len = sum(piece.shape[0] for piece in key_pieces)

    def block(rows, columns):
        return pl.BlockSpec((rows, columns), lambda i: (0, i))

    query_block, own_block = block(rows, width // kv_heads), block(rows, head_dim)
    piece_blocks = [block(piece.shape[0], head_dim) for piece in key_pieces]
    half = jax.ShapeDtypeStruct((prompt_len // 2, kv_width), F32)
    own = jax.ShapeDtypeStruct((rows, kv_width), BF16)
    return pl.pallas_call(
        partial(attend_kernel, len(key_pieces)),
        grid=(kv_heads,),
        in_specs=[
            pl.BlockSpec(memory_space=pltpu.SMEM), query_block, query_block, own_block, own_block,
            *piece_blocks, *piece_blocks,
        ],
        out_specs=[query_block, own_block, own_block] + [block(prompt_len // 2, head_dim)] * 4,
        out_shape=[jax.ShapeDtypeStruct((rows, width), BF16), own, own] + [half] * 4,
        compiler_params=PARAMS,
        cost_estimate=cost(10 * rows * width * (prompt_len + rows), 10**7),
        name="attend",
    )(length, queries, upstream, keys, values, *key_pieces, *value_pieces)


def in_vmem(kernel, name, outs, arrays, macs=0, scratch=()):
    whole = pl.BlockSpec(memory_space=pltpu.VMEM)
    results = pl.pallas_call(
        kernel,
        in_specs=[whole] * len(arrays),
        out_specs=[whole] * len(outs),
        out_shape=[jax.ShapeDtypeStruct(shape, dtype) for shape, dtype in outs],
        scratch_shapes=scratch,
        compiler_params=PARAMS,
        cost_estimate=cost(macs, 3 * 10**6),
        name=name,
    )(*arrays)
    return list(results)


def split_kernel(hidden_ref, *piece_refs):
    depth = piece_refs[0].shape[1]
    group = lax.axis_index("group")
    for k, piece_ref in enumerate(piece_refs):
        start = pl.multiple_of((group ^ k) * depth, depth)
        piece_ref[...] = hidden_ref[:, pl.ds(start, depth)]


def split_pass(hidden, groups):
    tokens, width = hidden.shape
    outs = [((tokens, width // groups), hidden.dtype)] * groups
    return in_vmem(split_kernel, "split_hidden", outs, [hidden])


def turn_kernel(groups, *refs):
    columns, piece_refs, turned = refs[:groups], refs[groups:-1], refs[-1]
    half = piece_refs[0].shape[0] // 2
    resp = lax.axis_index("resp")
    core, chip = resp % 2, resp // 2
    turned[...] = jnp.concatenate([ref[...] for ref in columns], axis=0).astype(F32).T
    for p, piece_ref in enumerate(piece_refs):
        start = (chip ^ p) * (2 * half)
        for i, part in enumerate((core, 1 - core)):
            rows = turned[pl.ds(pl.multiple_of(start + part * half, 8), half)]
            piece_ref[i * half : (i + 1) * half] = rows.astype(BF16)


def turn_pass(columns, chips):
    tokens, depth = columns[0].shape
    every = tokens * len(columns)
    outs = [((depth // chips, every), BF16)] * chips
    scratch = [pltpu.VMEM((depth, every), F32)]
    return in_vmem(partial(turn_kernel, len(columns)), "turn_hidden", outs, columns, 0, scratch)


def hidden_kernel(beside, across, own_ref, *refs):
    grads, refs = refs[: len(across) + 1], refs[len(across) + 1 :]
    near, far = refs[: len(beside)], refs[len(beside) : 2 * len(beside)]
    out_ref, *part_refs = refs[2 * len(beside) :]
    group, core = lax.axis_index("group"), lax.axis_index("resp") % 2
    depth, kv_width = own_ref.shape
    tokens, half = grads[0].shape[0], kv_width // 2
    near_grad = grads[0][:, pl.ds(pl.multiple_of(core * half, half), half)]
    far_grad = grads[0][:, pl.ds(pl.multiple_of((1 - core) * half, half), half)]

    def place(k, block):
        out_ref[:, pl.ds(pl.multiple_of((group ^ k) * depth, depth), depth)] = block

    own = dot(own_ref[...], jnp.concatenate([ref[...] for ref in grads], axis=0), 1, 1).T.astype(BF16)
    place(0, own[:tokens])
    for i, k in enumerate(across):
        part_refs[i][...] = own[(i + 1) * tokens : (i + 2) * tokens]
        place(k, jnp.zeros((tokens, depth), BF16))
    for i, k in enumerate(beside):
        block = dot(near[i][...], near_grad, 1, 1) + dot(far[i][...], far_grad, 1, 1)
        place(k, block.T.astype(BF16))


def hidden_pass(key_pre_grad, first, own, near, far):
    tokens, kv_width = key_pre_grad.shape
    depth = own.shape[0]
    groups = 1 + len(first) + len(near)
    outs = [((tokens, groups * depth), BF16)] + [((tokens, depth), BF16)] * len(first)
    arrays = [own, key_pre_grad, *first.values(), *near.values(), *far.values()]
    kernel = partial(hidden_kernel, list(near), list(first))
    return in_vmem(kernel, "hidden_grad", outs, arrays, tokens * depth * kv_width * groups)


def weight_pass(taken, blocks):
    rows, tokens = taken[0].shape
    chips, groups = len(taken), len(blocks)
    token_rows = tokens // groups
    kv_width = blocks[0][0].shape[1]
    counts = [len(arrays) for arrays in blocks]

    def kernel(*refs):
        columns = jnp.concatenate([ref[...] for ref in refs[:chips]], axis=1)
        parts = [jnp.concatenate([ref[...] for ref in arrays], axis=0) for arrays in nested(refs[chips:-2], counts)]
        grads = [part[p * token_rows : (p + 1) * token_rows] for p in range(chips) for part in parts]
        product = dot(columns, jnp.concatenate(grads, axis=0))
        refs[-2][...], refs[-1][...] = product[: rows // 2], product[rows // 2 :]

    outs = [((rows // 2, kv_width), F32)] * 2
    arrays = [*taken, *[array for arrays in blocks for array in arrays]]
    return in_vmem(kernel, "weight_grad", outs, arrays, rows * kv_width * tokens * chips)


def nested(items, counts):
    items = iter(items)
    return [[next(items) for _ in range(count)] for count in counts]


def swap(array, axis, size, distance):
    return lax.ppermute(array, axis, [(i, i ^ distance) for i in range(size)])


def together(*arrays):
    return list(lax.optimization_barrier(arrays))


def spread_near(block, size):
    return [block] + [swap(block, "resp", size, k) for k in range(2, size, 2)]


def spread_far(near, size):
    return [swap(piece, "resp", size, 1) for piece in near]


def pair_sum(near, far, size):
    return near + swap(far, "resp", size, 1)


def chip_parts(near, size, distances):
    rows = near.shape[0] // (size // 2)
    pieces = [near[p * rows : (p + 1) * rows] for p in range(size // 2)]
    return pieces[:1] + [swap(pieces[p].astype(BF16), "resp", size, 2 * p) for p in distances]


def total(parts):
    return sum(part.astype(F32) for part in parts[1:]) + parts[0]


def shards(
    groups, responses, prompt_hidden, key_matrix, key_gain, prompt_token_value,
    resp_query, resp_key, response_value, grad_out, resp_length,
):
    hidden = prompt_hidden[0]
    tokens = hidden.shape[0]
    depth, kv_width = key_matrix.shape
    head_dim = key_gain.shape[0]
    chips = responses // 2
    beside = [k for k in range(1, groups) if k & (k - 1) == 0]
    across = [k for k in range(1, groups) if k & (k - 1)]

    pieces = split_pass(hidden, groups)
    columns = [swap(piece, "group", groups, k) if k else piece for k, piece in enumerate(pieces)]
    partials = [dot(piece, key_matrix) for piece in columns]
    prompt_value, partials[-1] = together(prompt_token_value[0], partials[-1])
    value_near = spread_near(prompt_value, responses)
    key_pre = partials[0]
    for k in range(1, groups):
        key_pre = key_pre + swap(partials[k], "group", groups, k)
    half_width = kv_width // 2
    start = (lax.axis_index("resp") % 2) * half_width
    half_weight = lax.dynamic_slice(key_matrix, (0, start), (depth, half_width))
    half_weight, key_pre = together(half_weight, key_pre)
    weight_near = [swap(half_weight, "group", groups, k) for k in beside]

    prompt_key = norm_keys(key_pre, key_gain).astype(BF16)
    key_near = spread_near(prompt_key, responses)
    value_pieces = value_near + spread_far(value_near, responses)

    taken = turn_pass(columns, chips)
    both = together(*taken, *key_near)
    taken, key_near = both[:chips], both[chips:]
    key_pieces = key_near + spread_far(key_near, responses)
    taken[1:] = [swap(taken[p], "resp", responses, 2 * p) for p in range(1, chips)]

    query_grad, key_grad, value_grad, key_sums, far, value_sums, value_far = attend(
        resp_length, resp_query[0, 0], grad_out[0, 0], key_pieces, value_pieces,
        resp_key[0, 0], response_value[0, 0], head_dim,
    )
    key_sums, far, *both = together(key_sums, far, *taken, *weight_near)
    taken, weight_near = both[:chips], both[chips:]
    key_sums = total(chip_parts(pair_sum(key_sums, far, responses), responses, range(1, chips)))
    value_sums = pair_sum(value_sums, value_far, responses)
    weight_far = [swap(piece, "resp", responses, 1) for piece in weight_near]
    key_sums, value_sums, *weight_far = together(key_sums, value_sums, *weight_far)
    _, pullback = jax.vjp(lambda values: norm_keys(values, key_gain), key_pre)
    key_pre_grad = pullback(key_sums)[0].astype(BF16)

    first = {k: swap(key_pre_grad, "group", groups, k) for k in across}
    grads = spread_near(key_pre_grad, responses)
    value_parts = chip_parts(value_sums, responses, (1,))
    grads_first = together(*grads, value_parts[1], value_sums, *first.values())
    grads, value_parts[1], value_sums = grads_first[:chips], grads_first[chips], grads_first[chips + 1]
    first = dict(zip(first, grads_first[chips + 2 :]))
    some, every = jnp.concatenate(grads[1:], axis=0), jnp.concatenate(grads, axis=0)
    grad_hidden, *parts = hidden_pass(
        key_pre_grad, first, key_matrix, dict(zip(beside, weight_near)), dict(zip(beside, weight_far))
    )

    blocks = [[every]] + [None] * (groups - 1)
    for k in beside:
        blocks[k] = [swap(every, "group", groups, k)]
    for k in across:
        blocks[k] = [first[k], swap(some, "group", groups, k)]
    value_parts += chip_parts(value_sums, responses, range(2, chips))[1:]
    for k in across:
        *parts, blocks[k][-1] = together(*parts, blocks[k][-1])
    parts = [swap(part, "group", groups, k) for k, part in zip(across, parts)]
    mine, other, *value_parts = together(*weight_pass(taken, blocks), *value_parts)
    value_sums = total(value_parts)
    grad_weight = mine + swap(other, "resp", responses, 1)
    for k, part in zip(across, parts):
        start = (lax.axis_index("group") ^ k) * depth
        grad_hidden = lax.dynamic_update_slice(grad_hidden, part, (0, start))
    return (
        grad_hidden[None],
        grad_weight,
        value_sums.astype(BF16)[None],
        query_grad[None, None],
        key_grad[None, None],
        value_grad[None, None],
    )


def solution(mesh):
    return jax.shard_map(
        partial(shards, mesh.shape["group"], mesh.shape["resp"]),
        mesh=mesh,
        in_specs=(
            P("group", "resp", None),
            P("group", None),
            P(),
            P("group", "resp", None),
            P("group", "resp", None, None),
            P("group", "resp", None, None),
            P("group", "resp", None, None),
            P("group", "resp", None, None),
            P("group", "resp"),
        ),
        out_specs=(
            P("group", "resp", None),
            P(("group", "resp"), None),
            P("group", "resp", None),
            P("group", "resp", None, None),
            P("group", "resp", None, None),
            P("group", "resp", None, None),
        ),
        check_vma=False,
    )
```

```python
from functools import partial

import jax
import jax.numpy as jnp
from jax import lax
from jax.experimental import pallas as pl
from jax.experimental.pallas import tpu as pltpu
from jax.sharding import PartitionSpec as P

F32, BF16 = jnp.float32, jnp.bfloat16
LOG2E = 1.4426950408889634
PARAMS = pltpu.CompilerParams(vmem_limit_bytes=56 * 2**20)


def norm_keys(key_pre, key_gain):
    shaped = key_pre.reshape(key_pre.shape[:-1] + (-1, key_gain.shape[0]))
    inverse = lax.rsqrt(jnp.mean(shaped * shaped, axis=-1, keepdims=True) + 1e-06)
    return (shaped * inverse * key_gain).reshape(key_pre.shape)


def dot(left, right, left_dim=1, right_dim=0):
    dims = (((left_dim,), (right_dim,)), ((), ()))
    return lax.dot_general(left, right, dims, preferred_element_type=F32)


def cost(macs, nbytes):
    return pl.CostEstimate(flops=2 * macs, bytes_accessed=nbytes, transcendentals=0)


def stack_heads(ref, head_dim):
    heads = ref.shape[1] // head_dim
    return jnp.concatenate([ref[:, i * head_dim : (i + 1) * head_dim] for i in range(heads)], axis=0)


def attend_kernel(pieces, length_ref, query_ref, upstream_ref, key_ref, value_ref, *refs):
    key_pieces, value_pieces = refs[:pieces], refs[pieces : 2 * pieces]
    query_grad_ref, key_grad_ref, value_grad_ref, *sum_refs = refs[2 * pieces :]
    rows = query_ref.shape[0]
    own_len, head_dim = key_ref.shape
    heads = query_ref.shape[1] // head_dim
    scale = head_dim ** -0.5
    keys = jnp.concatenate([ref[...] for ref in key_pieces] + [key_ref[...]], axis=0)
    values = jnp.concatenate([ref[...] for ref in value_pieces] + [value_ref[...]], axis=0)
    keys_t, values_t = keys.T, values.T
    prompt_len = keys.shape[0] - own_len
    queries, upstream = stack_heads(query_ref, head_dim), stack_heads(upstream_ref, head_dim)
    stacked = heads * rows
    live = lax.broadcasted_iota(jnp.int32, (stacked, 1), 0) % rows < length_ref[0, 0]
    own = (stacked, own_len)
    visible = lax.broadcasted_iota(jnp.int32, own, 1) <= lax.broadcasted_iota(jnp.int32, own, 0) % rows
    prompt_scores = dot(queries, keys_t[:, :prompt_len])
    own_scores = jnp.where(visible, dot(queries, keys_t[:, prompt_len:]), -jnp.inf)
    row_max = jnp.maximum(
        jnp.max(prompt_scores, axis=1, keepdims=True), jnp.max(own_scores, axis=1, keepdims=True)
    )
    scores = jnp.concatenate([prompt_scores, own_scores], axis=1)
    unit = scale * LOG2E
    exponent = jnp.exp2(scores * unit - row_max * unit)
    dprob = dot(upstream, values_t)
    total = jnp.sum(exponent, axis=1, keepdims=True)
    weighted = jnp.sum(exponent * dprob, axis=1, keepdims=True)
    inverse = jnp.where(live, 1.0 / total, 0.0)
    row_delta = weighted * inverse
    weights = (exponent * inverse).astype(BF16)
    dscore = (exponent * ((dprob - row_delta) * (inverse * scale))).astype(BF16)
    query_grad = dot(dscore, keys).astype(BF16)
    for i in range(heads):
        query_grad_ref[:, i * head_dim : (i + 1) * head_dim] = query_grad[i * rows : (i + 1) * rows]
    key_grad = dot(queries.T, dscore).T
    value_grad = dot(upstream.T, weights).T
    half = prompt_len // 2
    for i, grad in enumerate((key_grad, value_grad)):
        sum_refs[2 * i][...], sum_refs[2 * i + 1][...] = grad[:half], grad[half:prompt_len]
    key_grad_ref[...] = key_grad[prompt_len:].astype(BF16)
    value_grad_ref[...] = value_grad[prompt_len:].astype(BF16)


def attend(length, queries, upstream, key_pieces, value_pieces, keys, values, head_dim):
    rows, width = queries.shape
    kv_width = keys.shape[1]
    kv_heads = kv_width // head_dim
    prompt_len = sum(piece.shape[0] for piece in key_pieces)

    def block(rows, columns):
        return pl.BlockSpec((rows, columns), lambda i: (0, i))

    query_block, own_block = block(rows, width // kv_heads), block(rows, head_dim)
    piece_blocks = [block(piece.shape[0], head_dim) for piece in key_pieces]
    half = jax.ShapeDtypeStruct((prompt_len // 2, kv_width), F32)
    own = jax.ShapeDtypeStruct((rows, kv_width), BF16)
    return pl.pallas_call(
        partial(attend_kernel, len(key_pieces)),
        grid=(kv_heads,),
        in_specs=[
            pl.BlockSpec(memory_space=pltpu.SMEM), query_block, query_block, own_block, own_block,
            *piece_blocks, *piece_blocks,
        ],
        out_specs=[query_block, own_block, own_block] + [block(prompt_len // 2, head_dim)] * 4,
        out_shape=[jax.ShapeDtypeStruct((rows, width), BF16), own, own] + [half] * 4,
        compiler_params=PARAMS,
        cost_estimate=cost(10 * rows * width * (prompt_len + rows), 10**7),
        name="attend",
    )(length, queries, upstream, keys, values, *key_pieces, *value_pieces)


def in_vmem(kernel, name, outs, arrays, macs=0, scratch=()):
    whole = pl.BlockSpec(memory_space=pltpu.VMEM)
    results = pl.pallas_call(
        kernel,
        in_specs=[whole] * len(arrays),
        out_specs=[whole] * len(outs),
        out_shape=[jax.ShapeDtypeStruct(shape, dtype) for shape, dtype in outs],
        scratch_shapes=scratch,
        compiler_params=PARAMS,
        cost_estimate=cost(macs, 3 * 10**6),
        name=name,
    )(*arrays)
    return list(results)


def split_kernel(hidden_ref, *piece_refs):
    depth = piece_refs[0].shape[1]
    group = lax.axis_index("group")
    for k, piece_ref in enumerate(piece_refs):
        start = pl.multiple_of((group ^ k) * depth, depth)
        piece_ref[...] = hidden_ref[:, pl.ds(start, depth)]


def split_pass(hidden, groups):
    tokens, width = hidden.shape
    outs = [((tokens, width // groups), hidden.dtype)] * groups
    return in_vmem(split_kernel, "split_hidden", outs, [hidden])


def turn_kernel(groups, *refs):
    columns, piece_refs, turned = refs[:groups], refs[groups:-1], refs[-1]
    half = piece_refs[0].shape[0] // 2
    resp = lax.axis_index("resp")
    core, chip = resp % 2, resp // 2
    turned[...] = jnp.concatenate([ref[...] for ref in columns], axis=0).astype(F32).T
    for p, piece_ref in enumerate(piece_refs):
        start = (chip ^ p) * (2 * half)
        for i, part in enumerate((core, 1 - core)):
            rows = turned[pl.ds(pl.multiple_of(start + part * half, 8), half)]
            piece_ref[i * half : (i + 1) * half] = rows.astype(BF16)


def turn_pass(columns, chips):
    tokens, depth = columns[0].shape
    every = tokens * len(columns)
    outs = [((depth // chips, every), BF16)] * chips
    scratch = [pltpu.VMEM((depth, every), F32)]
    return in_vmem(partial(turn_kernel, len(columns)), "turn_hidden", outs, columns, 0, scratch)


def hidden_kernel(beside, across, own_ref, *refs):
    grads, refs = refs[: len(across) + 1], refs[len(across) + 1 :]
    near, far = refs[: len(beside)], refs[len(beside) : 2 * len(beside)]
    out_ref, *part_refs = refs[2 * len(beside) :]
    group, core = lax.axis_index("group"), lax.axis_index("resp") % 2
    depth, kv_width = own_ref.shape
    tokens, half = grads[0].shape[0], kv_width // 2
    near_grad = grads[0][:, pl.ds(pl.multiple_of(core * half, half), half)]
    far_grad = grads[0][:, pl.ds(pl.multiple_of((1 - core) * half, half), half)]

    def place(k, block):
        out_ref[:, pl.ds(pl.multiple_of((group ^ k) * depth, depth), depth)] = block

    own = dot(own_ref[...], jnp.concatenate([ref[...] for ref in grads], axis=0), 1, 1).T.astype(BF16)
    place(0, own[:tokens])
    for i, k in enumerate(across):
        part_refs[i][...] = own[(i + 1) * tokens : (i + 2) * tokens]
        place(k, jnp.zeros((tokens, depth), BF16))
    for i, k in enumerate(beside):
        block = dot(near[i][...], near_grad, 1, 1) + dot(far[i][...], far_grad, 1, 1)
        place(k, block.T.astype(BF16))


def hidden_pass(key_pre_grad, first, own, near, far):
    tokens, kv_width = key_pre_grad.shape
    depth = own.shape[0]
    groups = 1 + len(first) + len(near)
    outs = [((tokens, groups * depth), BF16)] + [((tokens, depth), BF16)] * len(first)
    arrays = [own, key_pre_grad, *first.values(), *near.values(), *far.values()]
    kernel = partial(hidden_kernel, list(near), list(first))
    return in_vmem(kernel, "hidden_grad", outs, arrays, tokens * depth * kv_width * groups)


def order_kernel(chips, widths, *refs):
    taken, out_refs = refs[:chips], nested(refs[chips:], [len(parts) for parts in widths for _ in range(2)])
    half = taken[0].shape[0] // 2
    tokens = taken[0].shape[1] // len(widths)
    for k, parts in enumerate(widths):
        for i in range(2):
            rows = slice(i * half, (i + 1) * half)
            columns = [ref[rows, k * tokens : (k + 1) * tokens] for ref in taken]
            for out_ref, count in zip(out_refs[2 * k + i], parts):
                out_ref[...] = jnp.concatenate(columns[:count], axis=1)
                columns = columns[count:]


def order_pass(taken, parts):
    rows, tokens = taken[0].shape
    groups = len(parts)
    outs = [
        ((rows // 2, tokens // groups * count), BF16)
        for counts in parts for _ in range(2) for count in counts
    ]
    arrays = in_vmem(partial(order_kernel, len(taken), parts), "order_columns", outs, taken)
    halves = nested(arrays, [len(counts) for counts in parts for _ in range(2)])
    return halves[0::2], halves[1::2]


def weight_sum(columns, blocks, order):
    total = None
    for k, i in order:
        product = dot(columns[k][i], blocks[k][i])
        total = product if total is None else total + product
    return total


def flat(lists):
    return [item for items in lists for item in items]


def nested(items, counts):
    items = iter(items)
    return [[next(items) for _ in range(count)] for count in counts]


def swap(array, axis, size, distance):
    return lax.ppermute(array, axis, [(i, i ^ distance) for i in range(size)])


def together(*arrays):
    return list(lax.optimization_barrier(arrays))


def spread_near(block, size):
    return [block] + [swap(block, "resp", size, k) for k in range(2, size, 2)]


def spread_far(near, size):
    return [swap(piece, "resp", size, 1) for piece in near]


def pair_sum(near, far, size):
    return near + swap(far, "resp", size, 1)


def chip_parts(near, size, distances):
    rows = near.shape[0] // (size // 2)
    pieces = [near[p * rows : (p + 1) * rows] for p in range(size // 2)]
    return pieces[:1] + [swap(pieces[p].astype(BF16), "resp", size, 2 * p) for p in distances]


def total(parts):
    return sum(part.astype(F32) for part in parts[1:]) + parts[0]


def shards(
    groups, responses, prompt_hidden, key_matrix, key_gain, prompt_token_value,
    resp_query, resp_key, response_value, grad_out, resp_length,
):
    hidden = prompt_hidden[0]
    tokens = hidden.shape[0]
    depth, kv_width = key_matrix.shape
    head_dim = key_gain.shape[0]
    chips = responses // 2
    beside = [k for k in range(1, groups) if k & (k - 1) == 0]
    across = [k for k in range(1, groups) if k & (k - 1)]

    pieces = split_pass(hidden, groups)
    columns = [swap(piece, "group", groups, k) if k else piece for k, piece in enumerate(pieces)]
    partials = [dot(piece, key_matrix) for piece in columns]
    prompt_value, partials[-1] = together(prompt_token_value[0], partials[-1])
    value_near = spread_near(prompt_value, responses)
    key_pre = partials[0]
    for k in range(1, groups):
        key_pre = key_pre + swap(partials[k], "group", groups, k)
    half_width = kv_width // 2
    start = (lax.axis_index("resp") % 2) * half_width
    half_weight = lax.dynamic_slice(key_matrix, (0, start), (depth, half_width))
    half_weight, key_pre = together(half_weight, key_pre)
    weight_near = [swap(half_weight, "group", groups, k) for k in beside]

    prompt_key = norm_keys(key_pre, key_gain).astype(BF16)
    key_near = spread_near(prompt_key, responses)
    value_pieces = value_near + spread_far(value_near, responses)

    taken = turn_pass(columns, chips)
    both = together(*taken, *key_near)
    taken, key_near = both[:chips], both[chips:]
    key_pieces = key_near + spread_far(key_near, responses)
    taken[1:] = [swap(taken[p], "resp", responses, 2 * p) for p in range(1, chips)]

    query_grad, key_grad, value_grad, key_sums, far, value_sums, value_far = attend(
        resp_length, resp_query[0, 0], grad_out[0, 0], key_pieces, value_pieces,
        resp_key[0, 0], response_value[0, 0], head_dim,
    )
    key_sums, far, *both = together(key_sums, far, *taken, *weight_near)
    taken, weight_near = both[:chips], both[chips:]
    key_sums = total(chip_parts(pair_sum(key_sums, far, responses), responses, range(1, chips)))
    value_sums = pair_sum(value_sums, value_far, responses)
    weight_far = [swap(piece, "resp", responses, 1) for piece in weight_near]
    value_parts = chip_parts(value_sums, responses, (1,))
    parts = [[1, chips - 1] if k in across else [chips] for k in range(groups)]
    mine, other = order_pass(taken, parts)
    count = len(weight_far)
    key_sums, value_sums, value_parts[1], *both = together(
        key_sums, value_sums, value_parts[1], *weight_far, *flat(mine), *flat(other)
    )
    weight_far, halves = both[:count], nested(both[count:], [len(counts) for counts in parts + parts])
    mine, other = halves[:groups], halves[groups:]
    _, pullback = jax.vjp(lambda values: norm_keys(values, key_gain), key_pre)
    key_pre_grad = pullback(key_sums)[0].astype(BF16)

    first = {k: swap(key_pre_grad, "group", groups, k) for k in across}
    grads = spread_near(key_pre_grad, responses)
    both = together(*grads, value_sums, *first.values())
    grads, value_sums, first = both[:chips], both[chips], dict(zip(first, both[chips + 1 :]))
    some, every = jnp.concatenate(grads[1:], axis=0), jnp.concatenate(grads, axis=0)
    grad_hidden, *parts = hidden_pass(
        key_pre_grad, first, key_matrix, dict(zip(beside, weight_near)), dict(zip(beside, weight_far))
    )

    blocks = [[every]] + [None] * (groups - 1)
    for k in beside:
        blocks[k] = [swap(every, "group", groups, k)]
    for k in across:
        blocks[k] = [first[k], swap(some, "group", groups, k)]
    value_parts += chip_parts(value_sums, responses, range(2, chips))[1:]
    for k in across:
        *parts, blocks[k][-1] = together(*parts, blocks[k][-1])
    parts = [swap(part, "group", groups, k) for k, part in zip(across, parts)]
    order = [(0, 0)] + [(k, 0) for k in across] + [(k, 0) for k in beside] + [(k, 1) for k in across]
    other, *value_parts = together(weight_sum(other, blocks, order), *value_parts)
    value_sums = total(value_parts)
    grad_weight = weight_sum(mine, blocks, order) + swap(other, "resp", responses, 1)
    for k, part in zip(across, parts):
        start = (lax.axis_index("group") ^ k) * depth
        grad_hidden = lax.dynamic_update_slice(grad_hidden, part, (0, start))
    return (
        grad_hidden[None],
        grad_weight,
        value_sums.astype(BF16)[None],
        query_grad[None, None],
        key_grad[None, None],
        value_grad[None, None],
    )


def solution(mesh):
    return jax.shard_map(
        partial(shards, mesh.shape["group"], mesh.shape["resp"]),
        mesh=mesh,
        in_specs=(
            P("group", "resp", None),
            P("group", None),
            P(),
            P("group", "resp", None),
            P("group", "resp", None, None),
            P("group", "resp", None, None),
            P("group", "resp", None, None),
            P("group", "resp", None, None),
            P("group", "resp"),
        ),
        out_specs=(
            P("group", "resp", None),
            P(("group", "resp"), None),
            P("group", "resp", None),
            P("group", "resp", None, None),
            P("group", "resp", None, None),
            P("group", "resp", None, None),
        ),
        check_vma=False,
    )
```

```python
from functools import partial

import jax
import jax.numpy as jnp
from jax import lax
from jax.experimental import pallas as pl
from jax.experimental.pallas import tpu as pltpu
from jax.sharding import PartitionSpec as P

F32, BF16 = jnp.float32, jnp.bfloat16
LOG2E = 1.4426950408889634
PARAMS = pltpu.CompilerParams(vmem_limit_bytes=56 * 2**20)


def norm_keys(key_pre, key_gain):
    shaped = key_pre.reshape(key_pre.shape[:-1] + (-1, key_gain.shape[0]))
    inverse = lax.rsqrt(jnp.mean(shaped * shaped, axis=-1, keepdims=True) + 1e-06)
    return (shaped * inverse * key_gain).reshape(key_pre.shape)


def dot(left, right, left_dim=1, right_dim=0):
    dims = (((left_dim,), (right_dim,)), ((), ()))
    return lax.dot_general(left, right, dims, preferred_element_type=F32)


def cost(macs, nbytes):
    return pl.CostEstimate(flops=2 * macs, bytes_accessed=nbytes, transcendentals=0)


def stack_heads(ref, head_dim):
    heads = ref.shape[1] // head_dim
    return jnp.concatenate([ref[:, i * head_dim : (i + 1) * head_dim] for i in range(heads)], axis=0)


def attend_kernel(pieces, length_ref, query_ref, upstream_ref, key_ref, value_ref, *refs):
    key_pieces, value_pieces = refs[:pieces], refs[pieces : 2 * pieces]
    query_grad_ref, key_grad_ref, value_grad_ref, *sum_refs = refs[2 * pieces :]
    rows = query_ref.shape[0]
    own_len, head_dim = key_ref.shape
    heads = query_ref.shape[1] // head_dim
    scale = head_dim ** -0.5
    keys = jnp.concatenate([ref[...] for ref in key_pieces] + [key_ref[...]], axis=0)
    values = jnp.concatenate([ref[...] for ref in value_pieces] + [value_ref[...]], axis=0)
    keys_t, values_t = keys.T, values.T
    prompt_len = keys.shape[0] - own_len
    queries, upstream = stack_heads(query_ref, head_dim), stack_heads(upstream_ref, head_dim)
    stacked = heads * rows
    live = lax.broadcasted_iota(jnp.int32, (stacked, 1), 0) % rows < length_ref[0, 0]
    own = (stacked, own_len)
    visible = lax.broadcasted_iota(jnp.int32, own, 1) <= lax.broadcasted_iota(jnp.int32, own, 0) % rows
    prompt_scores = dot(queries, keys_t[:, :prompt_len])
    own_scores = jnp.where(visible, dot(queries, keys_t[:, prompt_len:]), -jnp.inf)
    row_max = jnp.maximum(
        jnp.max(prompt_scores, axis=1, keepdims=True), jnp.max(own_scores, axis=1, keepdims=True)
    )
    scores = jnp.concatenate([prompt_scores, own_scores], axis=1)
    unit = scale * LOG2E
    exponent = jnp.exp2(scores * unit - row_max * unit)
    dprob = dot(upstream, values_t)
    total = jnp.sum(exponent, axis=1, keepdims=True)
    weighted = jnp.sum(exponent * dprob, axis=1, keepdims=True)
    inverse = jnp.where(live, 1.0 / total, 0.0)
    row_delta = weighted * inverse
    weights = (exponent * inverse).astype(BF16)
    dscore = (exponent * ((dprob - row_delta) * (inverse * scale))).astype(BF16)
    query_grad = dot(dscore, keys).astype(BF16)
    for i in range(heads):
        query_grad_ref[:, i * head_dim : (i + 1) * head_dim] = query_grad[i * rows : (i + 1) * rows]
    key_grad = dot(queries.T, dscore).T
    value_grad = dot(upstream.T, weights).T
    half = prompt_len // 2
    for i, grad in enumerate((key_grad, value_grad)):
        sum_refs[2 * i][...], sum_refs[2 * i + 1][...] = grad[:half], grad[half:prompt_len]
    key_grad_ref[...] = key_grad[prompt_len:].astype(BF16)
    value_grad_ref[...] = value_grad[prompt_len:].astype(BF16)


def attend(length, queries, upstream, key_pieces, value_pieces, keys, values, head_dim):
    rows, width = queries.shape
    kv_width = keys.shape[1]
    kv_heads = kv_width // head_dim
    prompt_len = sum(piece.shape[0] for piece in key_pieces)

    def block(rows, columns):
        return pl.BlockSpec((rows, columns), lambda i: (0, i))

    query_block, own_block = block(rows, width // kv_heads), block(rows, head_dim)
    piece_blocks = [block(piece.shape[0], head_dim) for piece in key_pieces]
    half = jax.ShapeDtypeStruct((prompt_len // 2, kv_width), F32)
    own = jax.ShapeDtypeStruct((rows, kv_width), BF16)
    return pl.pallas_call(
        partial(attend_kernel, len(key_pieces)),
        grid=(kv_heads,),
        in_specs=[
            pl.BlockSpec(memory_space=pltpu.SMEM), query_block, query_block, own_block, own_block,
            *piece_blocks, *piece_blocks,
        ],
        out_specs=[query_block, own_block, own_block] + [block(prompt_len // 2, head_dim)] * 4,
        out_shape=[jax.ShapeDtypeStruct((rows, width), BF16), own, own] + [half] * 4,
        compiler_params=PARAMS,
        cost_estimate=cost(10 * rows * width * (prompt_len + rows), 10**7),
        name="attend",
    )(length, queries, upstream, keys, values, *key_pieces, *value_pieces)


def in_vmem(kernel, name, outs, arrays, macs=0, scratch=()):
    whole = pl.BlockSpec(memory_space=pltpu.VMEM)
    results = pl.pallas_call(
        kernel,
        in_specs=[whole] * len(arrays),
        out_specs=[whole] * len(outs),
        out_shape=[jax.ShapeDtypeStruct(shape, dtype) for shape, dtype in outs],
        scratch_shapes=scratch,
        compiler_params=PARAMS,
        cost_estimate=cost(macs, 3 * 10**6),
        name=name,
    )(*arrays)
    return list(results)


def split_kernel(hidden_ref, *piece_refs):
    depth = piece_refs[0].shape[1]
    group = lax.axis_index("group")
    for k, piece_ref in enumerate(piece_refs):
        start = pl.multiple_of((group ^ k) * depth, depth)
        piece_ref[...] = hidden_ref[:, pl.ds(start, depth)]


def split_pass(hidden, groups):
    tokens, width = hidden.shape
    outs = [((tokens, width // groups), hidden.dtype)] * groups
    return in_vmem(split_kernel, "split_hidden", outs, [hidden])


def turn_kernel(groups, *refs):
    columns, piece_refs, turned = refs[:groups], refs[groups:-1], refs[-1]
    half = piece_refs[0].shape[0] // 2
    resp = lax.axis_index("resp")
    core, chip = resp % 2, resp // 2
    turned[...] = jnp.concatenate([ref[...] for ref in columns], axis=0).astype(F32).T
    for p, piece_ref in enumerate(piece_refs):
        start = (chip ^ p) * (2 * half)
        for i, part in enumerate((core, 1 - core)):
            rows = turned[pl.ds(pl.multiple_of(start + part * half, 8), half)]
            piece_ref[i * half : (i + 1) * half] = rows.astype(BF16)


def turn_pass(columns, chips):
    tokens, depth = columns[0].shape
    every = tokens * len(columns)
    outs = [((depth // chips, every), BF16)] * chips
    scratch = [pltpu.VMEM((depth, every), F32)]
    return in_vmem(partial(turn_kernel, len(columns)), "turn_hidden", outs, columns, 0, scratch)


def hidden_kernel(beside, across, own_ref, *refs):
    grads, refs = refs[: len(across) + 1], refs[len(across) + 1 :]
    near, far = refs[: len(beside)], refs[len(beside) : 2 * len(beside)]
    out_ref, *part_refs = refs[2 * len(beside) :]
    group, core = lax.axis_index("group"), lax.axis_index("resp") % 2
    depth, kv_width = own_ref.shape
    tokens, half = grads[0].shape[0], kv_width // 2
    near_grad = grads[0][:, pl.ds(pl.multiple_of(core * half, half), half)]
    far_grad = grads[0][:, pl.ds(pl.multiple_of((1 - core) * half, half), half)]

    def place(k, block):
        out_ref[:, pl.ds(pl.multiple_of((group ^ k) * depth, depth), depth)] = block

    own = dot(own_ref[...], jnp.concatenate([ref[...] for ref in grads], axis=0), 1, 1).T.astype(BF16)
    place(0, own[:tokens])
    for i, k in enumerate(across):
        part_refs[i][...] = own[(i + 1) * tokens : (i + 2) * tokens]
        place(k, jnp.zeros((tokens, depth), BF16))
    for i, k in enumerate(beside):
        block = dot(near[i][...], near_grad, 1, 1) + dot(far[i][...], far_grad, 1, 1)
        place(k, block.T.astype(BF16))


def hidden_pass(key_pre_grad, first, own, near, far):
    tokens, kv_width = key_pre_grad.shape
    depth = own.shape[0]
    groups = 1 + len(first) + len(near)
    outs = [((tokens, groups * depth), BF16)] + [((tokens, depth), BF16)] * len(first)
    arrays = [own, key_pre_grad, *first.values(), *near.values(), *far.values()]
    kernel = partial(hidden_kernel, list(near), list(first))
    return in_vmem(kernel, "hidden_grad", outs, arrays, tokens * depth * kv_width * groups)


def order_kernel(chips, widths, *refs):
    taken, out_refs = refs[:chips], nested(refs[chips:], [len(parts) for parts in widths for _ in range(2)])
    half = taken[0].shape[0] // 2
    tokens = taken[0].shape[1] // len(widths)
    for k, parts in enumerate(widths):
        for i in range(2):
            rows = slice(i * half, (i + 1) * half)
            columns = [ref[rows, k * tokens : (k + 1) * tokens] for ref in taken]
            for out_ref, count in zip(out_refs[2 * k + i], parts):
                out_ref[...] = jnp.concatenate(columns[:count], axis=1)
                columns = columns[count:]


def order_pass(taken, parts):
    rows, tokens = taken[0].shape
    groups = len(parts)
    outs = [
        ((rows // 2, tokens // groups * count), BF16)
        for counts in parts for _ in range(2) for count in counts
    ]
    arrays = in_vmem(partial(order_kernel, len(taken), parts), "order_columns", outs, taken)
    halves = nested(arrays, [len(counts) for counts in parts for _ in range(2)])
    return halves[0::2], halves[1::2]


def weight_sum(columns, blocks, order):
    total = None
    for k, i in order:
        product = dot(columns[k][i], blocks[k][i])
        total = product if total is None else total + product
    return total


def flat(lists):
    return [item for items in lists for item in items]


def nested(items, counts):
    items = iter(items)
    return [[next(items) for _ in range(count)] for count in counts]


def swap(array, axis, size, distance):
    return lax.ppermute(array, axis, [(i, i ^ distance) for i in range(size)])


def together(*arrays):
    return list(lax.optimization_barrier(arrays))


def spread_near(block, size):
    return [block] + [swap(block, "resp", size, k) for k in range(2, size, 2)]


def spread_far(near, size):
    return [swap(piece, "resp", size, 1) for piece in near]


def pair_sum(near, far, size):
    return near + swap(far, "resp", size, 1)


def chip_parts(near, size, distances):
    rows = near.shape[0] // (size // 2)
    pieces = [near[p * rows : (p + 1) * rows] for p in range(size // 2)]
    return pieces[:1] + [swap(pieces[p].astype(BF16), "resp", size, 2 * p) for p in distances]


def total(parts):
    return sum(part.astype(F32) for part in parts[1:]) + parts[0]


def shards(
    groups, responses, prompt_hidden, key_matrix, key_gain, prompt_token_value,
    resp_query, resp_key, response_value, grad_out, resp_length,
):
    hidden = prompt_hidden[0]
    tokens = hidden.shape[0]
    depth, kv_width = key_matrix.shape
    head_dim = key_gain.shape[0]
    chips = responses // 2
    beside = [k for k in range(1, groups) if k & (k - 1) == 0]
    across = [k for k in range(1, groups) if k & (k - 1)]

    pieces = split_pass(hidden, groups)
    columns = [swap(piece, "group", groups, k) if k else piece for k, piece in enumerate(pieces)]
    partials = [dot(piece, key_matrix) for piece in columns]
    prompt_value, partials[-1] = together(prompt_token_value[0], partials[-1])
    value_near = spread_near(prompt_value, responses)
    key_pre = partials[0]
    for k in range(1, groups):
        key_pre = key_pre + swap(partials[k], "group", groups, k)
    half_width = kv_width // 2
    start = (lax.axis_index("resp") % 2) * half_width
    half_weight = lax.dynamic_slice(key_matrix, (0, start), (depth, half_width))
    half_weight, key_pre = together(half_weight, key_pre)
    weight_near = [swap(half_weight, "group", groups, k) for k in beside]

    prompt_key = norm_keys(key_pre, key_gain).astype(BF16)
    key_near = spread_near(prompt_key, responses)
    value_pieces = value_near + spread_far(value_near, responses)

    taken = turn_pass(columns, chips)
    both = together(*taken, *key_near)
    taken, key_near = both[:chips], both[chips:]
    key_pieces = key_near + spread_far(key_near, responses)
    taken[1:] = [swap(taken[p], "resp", responses, 2 * p) for p in range(1, chips)]

    query_grad, key_grad, value_grad, key_sums, far, value_sums, value_far = attend(
        resp_length, resp_query[0, 0], grad_out[0, 0], key_pieces, value_pieces,
        resp_key[0, 0], response_value[0, 0], head_dim,
    )
    key_sums, far, *both = together(key_sums, far, *taken, *weight_near)
    taken, weight_near = both[:chips], both[chips:]
    key_sums = total(chip_parts(pair_sum(key_sums, far, responses), responses, range(1, chips)))
    value_sums = pair_sum(value_sums, value_far, responses)
    weight_far = [swap(piece, "resp", responses, 1) for piece in weight_near]
    parts = [[1, chips - 1] if k in across else [chips] for k in range(groups)]
    mine, other = order_pass(taken, parts)
    count = len(weight_far)
    key_sums, value_sums, *both = together(
        key_sums, value_sums, *weight_far, *flat(mine), *flat(other)
    )
    weight_far, halves = both[:count], nested(both[count:], [len(counts) for counts in parts + parts])
    mine, other = halves[:groups], halves[groups:]
    _, pullback = jax.vjp(lambda values: norm_keys(values, key_gain), key_pre)
    key_pre_grad = pullback(key_sums)[0].astype(BF16)

    first = {k: swap(key_pre_grad, "group", groups, k) for k in across}
    grads = spread_near(key_pre_grad, responses)
    value_parts = chip_parts(value_sums, responses, (1,))
    value_parts[1], value_sums, *both = together(value_parts[1], value_sums, *grads, *first.values())
    grads, first = both[:chips], dict(zip(first, both[chips:]))
    some, every = jnp.concatenate(grads[1:], axis=0), jnp.concatenate(grads, axis=0)
    grad_hidden, *parts = hidden_pass(
        key_pre_grad, first, key_matrix, dict(zip(beside, weight_near)), dict(zip(beside, weight_far))
    )

    blocks = [[every]] + [None] * (groups - 1)
    for k in beside:
        blocks[k] = [swap(every, "group", groups, k)]
    for k in across:
        blocks[k] = [first[k], swap(some, "group", groups, k)]
    value_parts += chip_parts(value_sums, responses, range(2, chips))[1:]
    for k in across:
        *parts, blocks[k][-1] = together(*parts, blocks[k][-1])
    parts = [swap(part, "group", groups, k) for k, part in zip(across, parts)]
    order = [(0, 0)] + [(k, 0) for k in across] + [(k, 0) for k in beside] + [(k, 1) for k in across]
    other, *value_parts = together(weight_sum(other, blocks, order), *value_parts)
    value_sums = total(value_parts)
    grad_weight = weight_sum(mine, blocks, order) + swap(other, "resp", responses, 1)
    for k, part in zip(across, parts):
        start = (lax.axis_index("group") ^ k) * depth
        grad_hidden = lax.dynamic_update_slice(grad_hidden, part, (0, start))
    return (
        grad_hidden[None],
        grad_weight,
        value_sums.astype(BF16)[None],
        query_grad[None, None],
        key_grad[None, None],
        value_grad[None, None],
    )


def solution(mesh):
    return jax.shard_map(
        partial(shards, mesh.shape["group"], mesh.shape["resp"]),
        mesh=mesh,
        in_specs=(
            P("group", "resp", None),
            P("group", None),
            P(),
            P("group", "resp", None),
            P("group", "resp", None, None),
            P("group", "resp", None, None),
            P("group", "resp", None, None),
            P("group", "resp", None, None),
            P("group", "resp"),
        ),
        out_specs=(
            P("group", "resp", None),
            P(("group", "resp"), None),
            P("group", "resp", None),
            P("group", "resp", None, None),
            P("group", "resp", None, None),
            P("group", "resp", None, None),
        ),
        check_vma=False,
    )
```

```python
from functools import partial

import jax
import jax.numpy as jnp
from jax import lax
from jax.experimental import pallas as pl
from jax.experimental.pallas import tpu as pltpu
from jax.sharding import PartitionSpec as P

F32, BF16 = jnp.float32, jnp.bfloat16
LOG2E = 1.4426950408889634
PARAMS = pltpu.CompilerParams(vmem_limit_bytes=56 * 2**20)


def norm_keys(key_pre, key_gain):
    shaped = key_pre.reshape(key_pre.shape[:-1] + (-1, key_gain.shape[0]))
    inverse = lax.rsqrt(jnp.mean(shaped * shaped, axis=-1, keepdims=True) + 1e-06)
    return (shaped * inverse * key_gain).reshape(key_pre.shape)


def dot(left, right, left_dim=1, right_dim=0):
    dims = (((left_dim,), (right_dim,)), ((), ()))
    return lax.dot_general(left, right, dims, preferred_element_type=F32)


def cost(macs, nbytes):
    return pl.CostEstimate(flops=2 * macs, bytes_accessed=nbytes, transcendentals=0)


def stack_heads(ref, head_dim):
    heads = ref.shape[1] // head_dim
    return jnp.concatenate([ref[:, i * head_dim : (i + 1) * head_dim] for i in range(heads)], axis=0)


def attend_kernel(pieces, length_ref, query_ref, upstream_ref, key_ref, value_ref, *refs):
    key_pieces, value_pieces = refs[:pieces], refs[pieces : 2 * pieces]
    query_grad_ref, key_grad_ref, value_grad_ref, *sum_refs = refs[2 * pieces :]
    rows = query_ref.shape[0]
    own_len, head_dim = key_ref.shape
    heads = query_ref.shape[1] // head_dim
    scale = head_dim ** -0.5
    keys = jnp.concatenate([ref[...] for ref in key_pieces] + [key_ref[...]], axis=0)
    values = jnp.concatenate([ref[...] for ref in value_pieces] + [value_ref[...]], axis=0)
    keys_t, values_t = keys.T, values.T
    prompt_len = keys.shape[0] - own_len
    queries, upstream = stack_heads(query_ref, head_dim), stack_heads(upstream_ref, head_dim)
    stacked = heads * rows
    live = lax.broadcasted_iota(jnp.int32, (stacked, 1), 0) % rows < length_ref[0, 0]
    own = (stacked, own_len)
    visible = lax.broadcasted_iota(jnp.int32, own, 1) <= lax.broadcasted_iota(jnp.int32, own, 0) % rows
    prompt_scores = dot(queries, keys_t[:, :prompt_len])
    own_scores = jnp.where(visible, dot(queries, keys_t[:, prompt_len:]), -jnp.inf)
    row_max = jnp.maximum(
        jnp.max(prompt_scores, axis=1, keepdims=True), jnp.max(own_scores, axis=1, keepdims=True)
    )
    scores = jnp.concatenate([prompt_scores, own_scores], axis=1)
    unit = scale * LOG2E
    exponent = jnp.exp2(scores * unit - row_max * unit)
    dprob = dot(upstream, values_t)
    total = jnp.sum(exponent, axis=1, keepdims=True)
    weighted = jnp.sum(exponent * dprob, axis=1, keepdims=True)
    inverse = jnp.where(live, 1.0 / total, 0.0)
    row_delta = weighted * inverse
    weights = (exponent * inverse).astype(BF16)
    dscore = (exponent * ((dprob - row_delta) * (inverse * scale))).astype(BF16)
    query_grad = dot(dscore, keys).astype(BF16)
    for i in range(heads):
        query_grad_ref[:, i * head_dim : (i + 1) * head_dim] = query_grad[i * rows : (i + 1) * rows]
    key_grad = dot(queries.T, dscore).T
    value_grad = dot(upstream.T, weights).T
    half = prompt_len // 2
    for i, grad in enumerate((key_grad, value_grad)):
        sum_refs[2 * i][...], sum_refs[2 * i + 1][...] = grad[:half], grad[half:prompt_len]
    key_grad_ref[...] = key_grad[prompt_len:].astype(BF16)
    value_grad_ref[...] = value_grad[prompt_len:].astype(BF16)


def attend(length, queries, upstream, key_pieces, value_pieces, keys, values, head_dim):
    rows, width = queries.shape
    kv_width = keys.shape[1]
    kv_heads = kv_width // head_dim
    prompt_len = sum(piece.shape[0] for piece in key_pieces)

    def block(rows, columns):
        return pl.BlockSpec((rows, columns), lambda i: (0, i))

    query_block, own_block = block(rows, width // kv_heads), block(rows, head_dim)
    piece_blocks = [block(piece.shape[0], head_dim) for piece in key_pieces]
    half = jax.ShapeDtypeStruct((prompt_len // 2, kv_width), F32)
    own = jax.ShapeDtypeStruct((rows, kv_width), BF16)
    return pl.pallas_call(
        partial(attend_kernel, len(key_pieces)),
        grid=(kv_heads,),
        in_specs=[
            pl.BlockSpec(memory_space=pltpu.SMEM), query_block, query_block, own_block, own_block,
            *piece_blocks, *piece_blocks,
        ],
        out_specs=[query_block, own_block, own_block] + [block(prompt_len // 2, head_dim)] * 4,
        out_shape=[jax.ShapeDtypeStruct((rows, width), BF16), own, own] + [half] * 4,
        compiler_params=PARAMS,
        cost_estimate=cost(10 * rows * width * (prompt_len + rows), 10**7),
        name="attend",
    )(length, queries, upstream, keys, values, *key_pieces, *value_pieces)


def in_vmem(kernel, name, outs, arrays, macs=0, scratch=()):
    whole = pl.BlockSpec(memory_space=pltpu.VMEM)
    results = pl.pallas_call(
        kernel,
        in_specs=[whole] * len(arrays),
        out_specs=[whole] * len(outs),
        out_shape=[jax.ShapeDtypeStruct(shape, dtype) for shape, dtype in outs],
        scratch_shapes=scratch,
        compiler_params=PARAMS,
        cost_estimate=cost(macs, 3 * 10**6),
        name=name,
    )(*arrays)
    return list(results)


def split_kernel(hidden_ref, *piece_refs):
    depth = piece_refs[0].shape[1]
    group = lax.axis_index("group")
    for k, piece_ref in enumerate(piece_refs):
        start = pl.multiple_of((group ^ k) * depth, depth)
        piece_ref[...] = hidden_ref[:, pl.ds(start, depth)]


def split_pass(hidden, groups):
    tokens, width = hidden.shape
    outs = [((tokens, width // groups), hidden.dtype)] * groups
    return in_vmem(split_kernel, "split_hidden", outs, [hidden])


def turn_kernel(groups, *refs):
    columns, piece_refs, turned = refs[:groups], refs[groups:-1], refs[-1]
    half = piece_refs[0].shape[0] // 2
    resp = lax.axis_index("resp")
    core, chip = resp % 2, resp // 2
    turned[...] = jnp.concatenate([ref[...] for ref in columns], axis=0).astype(F32).T
    for p, piece_ref in enumerate(piece_refs):
        start = (chip ^ p) * (2 * half)
        for i, part in enumerate((core, 1 - core)):
            rows = turned[pl.ds(pl.multiple_of(start + part * half, 8), half)]
            piece_ref[i * half : (i + 1) * half] = rows.astype(BF16)


def turn_pass(columns, chips):
    tokens, depth = columns[0].shape
    every = tokens * len(columns)
    outs = [((depth // chips, every), BF16)] * chips
    scratch = [pltpu.VMEM((depth, every), F32)]
    return in_vmem(partial(turn_kernel, len(columns)), "turn_hidden", outs, columns, 0, scratch)


def order_kernel(chips, widths, *refs):
    taken, out_refs = refs[:chips], nested(refs[chips:], [len(parts) for parts in widths for _ in range(2)])
    half = taken[0].shape[0] // 2
    tokens = taken[0].shape[1] // len(widths)
    for k, parts in enumerate(widths):
        for i in range(2):
            rows = slice(i * half, (i + 1) * half)
            columns = [ref[rows, k * tokens : (k + 1) * tokens] for ref in taken]
            for out_ref, count in zip(out_refs[2 * k + i], parts):
                out_ref[...] = jnp.concatenate(columns[:count], axis=1)
                columns = columns[count:]


def order_pass(taken, parts):
    rows, tokens = taken[0].shape
    groups = len(parts)
    outs = [
        ((rows // 2, tokens // groups * count), BF16)
        for counts in parts for _ in range(2) for count in counts
    ]
    arrays = in_vmem(partial(order_kernel, len(taken), parts), "order_columns", outs, taken)
    halves = nested(arrays, [len(counts) for counts in parts for _ in range(2)])
    return halves[0::2], halves[1::2]


def weight_sum(columns, blocks, order):
    total = None
    for k, i in order:
        product = dot(columns[k][i], blocks[k][i])
        total = product if total is None else total + product
    return total


def flat(lists):
    return [item for items in lists for item in items]


def nested(items, counts):
    items = iter(items)
    return [[next(items) for _ in range(count)] for count in counts]


def swap(array, axis, size, distance):
    return lax.ppermute(array, axis, [(i, i ^ distance) for i in range(size)])


def together(*arrays):
    return list(lax.optimization_barrier(arrays))


def spread_near(block, size):
    return [block] + [swap(block, "resp", size, k) for k in range(2, size, 2)]


def spread_far(near, size):
    return [swap(piece, "resp", size, 1) for piece in near]


def pair_sum(near, far, size):
    return near + swap(far, "resp", size, 1)


def chip_parts(near, size, distances):
    rows = near.shape[0] // (size // 2)
    pieces = [near[p * rows : (p + 1) * rows] for p in range(size // 2)]
    return pieces[:1] + [swap(pieces[p].astype(BF16), "resp", size, 2 * p) for p in distances]


def total(parts):
    return sum(part.astype(F32) for part in parts[1:]) + parts[0]


def shards(
    groups, responses, prompt_hidden, key_matrix, key_gain, prompt_token_value,
    resp_query, resp_key, response_value, grad_out, resp_length,
):
    hidden = prompt_hidden[0]
    tokens = hidden.shape[0]
    depth, kv_width = key_matrix.shape
    head_dim = key_gain.shape[0]
    chips = responses // 2
    beside = [k for k in range(1, groups) if k & (k - 1) == 0]
    across = [k for k in range(1, groups) if k & (k - 1)]

    pieces = split_pass(hidden, groups)
    columns = [swap(piece, "group", groups, k) if k else piece for k, piece in enumerate(pieces)]
    partials = [dot(piece, key_matrix) for piece in columns]
    prompt_value, partials[-1] = together(prompt_token_value[0], partials[-1])
    value_near = spread_near(prompt_value, responses)
    key_pre = partials[0]
    for k in range(1, groups):
        key_pre = key_pre + swap(partials[k], "group", groups, k)
    half_width = kv_width // 2
    start = (lax.axis_index("resp") % 2) * half_width
    half_weight = lax.dynamic_slice(key_matrix, (0, start), (depth, half_width))
    half_weight, key_pre = together(half_weight, key_pre)
    weight_near = [swap(half_weight, "group", groups, k) for k in beside]

    prompt_key = norm_keys(key_pre, key_gain).astype(BF16)
    key_near = spread_near(prompt_key, responses)
    value_pieces = value_near + spread_far(value_near, responses)

    taken = turn_pass(columns, chips)
    both = together(*taken, *key_near)
    taken, key_near = both[:chips], both[chips:]
    key_pieces = key_near + spread_far(key_near, responses)
    taken[1:] = [swap(taken[p], "resp", responses, 2 * p) for p in range(1, chips)]

    query_grad, key_grad, value_grad, key_sums, far, value_sums, value_far = attend(
        resp_length, resp_query[0, 0], grad_out[0, 0], key_pieces, value_pieces,
        resp_key[0, 0], response_value[0, 0], head_dim,
    )
    key_sums, far, *both = together(key_sums, far, *taken, *weight_near)
    taken, weight_near = both[:chips], both[chips:]
    key_sums = total(chip_parts(pair_sum(key_sums, far, responses), responses, range(1, chips)))
    value_sums = pair_sum(value_sums, value_far, responses)
    weight_far = [swap(piece, "resp", responses, 1) for piece in weight_near]
    parts = [[1, chips - 1] if k in across else [chips] for k in range(groups)]
    mine, other = order_pass(taken, parts)
    count = len(weight_far)
    key_sums, value_sums, *both = together(
        key_sums, value_sums, *weight_far, *flat(mine), *flat(other)
    )
    weight_far, halves = both[:count], nested(both[count:], [len(counts) for counts in parts + parts])
    mine, other = halves[:groups], halves[groups:]
    _, pullback = jax.vjp(lambda values: norm_keys(values, key_gain), key_pre)
    key_pre_grad = pullback(key_sums)[0].astype(BF16)

    first = {k: swap(key_pre_grad, "group", groups, k) for k in across}
    grads = spread_near(key_pre_grad, responses)
    value_parts = chip_parts(value_sums, responses, (1,))
    value_parts[1], value_sums, *both = together(value_parts[1], value_sums, *grads, *first.values())
    grads, first = both[:chips], dict(zip(first, both[chips:]))
    some, every = jnp.concatenate(grads[1:], axis=0), jnp.concatenate(grads, axis=0)
    group, core = lax.axis_index("group"), lax.axis_index("resp") % 2
    grad_hidden = jnp.zeros((tokens, groups * depth), BF16)
    own = dot(jnp.concatenate([key_pre_grad, *first.values()], axis=0), key_matrix, 1, 1).astype(BF16)
    parts = [own[(i + 1) * tokens : (i + 2) * tokens] for i in range(len(across))]
    grad_hidden = lax.dynamic_update_slice(grad_hidden, own[:tokens], (0, group * depth))
    near_grad = lax.dynamic_slice(key_pre_grad, (0, core * half_width), (tokens, half_width))
    far_grad = lax.dynamic_slice(key_pre_grad, (0, (1 - core) * half_width), (tokens, half_width))
    for k, near, far in zip(beside, weight_near, weight_far):
        block = (dot(near_grad, near, 1, 1) + dot(far_grad, far, 1, 1)).astype(BF16)
        grad_hidden = lax.dynamic_update_slice(grad_hidden, block, (0, (group ^ k) * depth))

    blocks = [[every]] + [None] * (groups - 1)
    for k in beside:
        blocks[k] = [swap(every, "group", groups, k)]
    for k in across:
        blocks[k] = [first[k], swap(some, "group", groups, k)]
    value_parts += chip_parts(value_sums, responses, range(2, chips))[1:]
    for k in across:
        *parts, blocks[k][-1] = together(*parts, blocks[k][-1])
    parts = [swap(part, "group", groups, k) for k, part in zip(across, parts)]
    order = [(0, 0)] + [(k, 0) for k in across] + [(k, 0) for k in beside] + [(k, 1) for k in across]
    other, *value_parts = together(weight_sum(other, blocks, order), *value_parts)
    value_sums = total(value_parts)
    grad_weight = weight_sum(mine, blocks, order) + swap(other, "resp", responses, 1)
    for k, part in zip(across, parts):
        grad_hidden = lax.dynamic_update_slice(grad_hidden, part, (0, (group ^ k) * depth))
    return (
        grad_hidden[None],
        grad_weight,
        value_sums.astype(BF16)[None],
        query_grad[None, None],
        key_grad[None, None],
        value_grad[None, None],
    )


def solution(mesh):
    return jax.shard_map(
        partial(shards, mesh.shape["group"], mesh.shape["resp"]),
        mesh=mesh,
        in_specs=(
            P("group", "resp", None),
            P("group", None),
            P(),
            P("group", "resp", None),
            P("group", "resp", None, None),
            P("group", "resp", None, None),
            P("group", "resp", None, None),
            P("group", "resp", None, None),
            P("group", "resp"),
        ),
        out_specs=(
            P("group", "resp", None),
            P(("group", "resp"), None),
            P("group", "resp", None),
            P("group", "resp", None, None),
            P("group", "resp", None, None),
            P("group", "resp", None, None),
        ),
        check_vma=False,
    )
```

```python
from functools import partial

import jax
import jax.numpy as jnp
from jax import lax
from jax.experimental import pallas as pl
from jax.experimental.pallas import tpu as pltpu
from jax.sharding import PartitionSpec as P

F32, BF16 = jnp.float32, jnp.bfloat16
LOG2E = 1.4426950408889634
SMALL = pltpu.CompilerParams(vmem_limit_bytes=16 * 2**20)
LARGE = pltpu.CompilerParams(vmem_limit_bytes=40 * 2**20)


def norm_keys(key_pre, key_gain):
    shaped = key_pre.reshape(key_pre.shape[:-1] + (-1, key_gain.shape[0]))
    inverse = lax.rsqrt(jnp.mean(shaped * shaped, axis=-1, keepdims=True) + 1e-06)
    return (shaped * inverse * key_gain).reshape(key_pre.shape)


def dot(left, right, left_dim=1, right_dim=0):
    dims = (((left_dim,), (right_dim,)), ((), ()))
    return lax.dot_general(left, right, dims, preferred_element_type=F32)


def cost(macs, nbytes):
    return pl.CostEstimate(flops=2 * macs, bytes_accessed=nbytes, transcendentals=0)


def stack_heads(ref, head_dim):
    heads = ref.shape[1] // head_dim
    return jnp.concatenate([ref[:, i * head_dim : (i + 1) * head_dim] for i in range(heads)], axis=0)


def attend_kernel(pieces, length_ref, query_ref, upstream_ref, key_ref, value_ref, *refs):
    key_pieces, value_pieces = refs[:pieces], refs[pieces : 2 * pieces]
    query_grad_ref, key_grad_ref, value_grad_ref, *sum_refs = refs[2 * pieces :]
    rows = query_ref.shape[0]
    own_len, head_dim = key_ref.shape
    heads = query_ref.shape[1] // head_dim
    scale = head_dim ** -0.5
    keys = jnp.concatenate([ref[...] for ref in key_pieces] + [key_ref[...]], axis=0)
    values = jnp.concatenate([ref[...] for ref in value_pieces] + [value_ref[...]], axis=0)
    keys_t, values_t = keys.T, values.T
    prompt_len = keys.shape[0] - own_len
    queries, upstream = stack_heads(query_ref, head_dim), stack_heads(upstream_ref, head_dim)
    stacked = heads * rows
    live = lax.broadcasted_iota(jnp.int32, (stacked, 1), 0) % rows < length_ref[0, 0]
    own = (stacked, own_len)
    visible = lax.broadcasted_iota(jnp.int32, own, 1) <= lax.broadcasted_iota(jnp.int32, own, 0) % rows
    prompt_scores = dot(queries, keys_t[:, :prompt_len])
    own_scores = jnp.where(visible, dot(queries, keys_t[:, prompt_len:]), -jnp.inf)
    row_max = jnp.maximum(
        jnp.max(prompt_scores, axis=1, keepdims=True), jnp.max(own_scores, axis=1, keepdims=True)
    )
    scores = jnp.concatenate([prompt_scores, own_scores], axis=1)
    unit = scale * LOG2E
    exponent = jnp.exp2(scores * unit - row_max * unit)
    dprob = dot(upstream, values_t)
    total = jnp.sum(exponent, axis=1, keepdims=True)
    weighted = jnp.sum(exponent * dprob, axis=1, keepdims=True)
    inverse = jnp.where(live, 1.0 / total, 0.0)
    row_delta = weighted * inverse
    weights = (exponent * inverse).astype(BF16)
    dscore = (exponent * ((dprob - row_delta) * (inverse * scale))).astype(BF16)
    query_grad = dot(dscore, keys).astype(BF16)
    for i in range(heads):
        query_grad_ref[:, i * head_dim : (i + 1) * head_dim] = query_grad[i * rows : (i + 1) * rows]
    key_grad = dot(queries.T, dscore).T
    value_grad = dot(upstream.T, weights).T
    half = prompt_len // 2
    for i, grad in enumerate((key_grad, value_grad)):
        sum_refs[2 * i][...], sum_refs[2 * i + 1][...] = grad[:half], grad[half:prompt_len]
    key_grad_ref[...] = key_grad[prompt_len:].astype(BF16)
    value_grad_ref[...] = value_grad[prompt_len:].astype(BF16)


def attend(length, queries, upstream, key_pieces, value_pieces, keys, values, head_dim):
    rows, width = queries.shape
    kv_width = keys.shape[1]
    kv_heads = kv_width // head_dim
    prompt_len = sum(piece.shape[0] for piece in key_pieces)

    def block(rows, columns):
        return pl.BlockSpec((rows, columns), lambda i: (0, i))

    query_block, own_block = block(rows, width // kv_heads), block(rows, head_dim)
    piece_blocks = [block(piece.shape[0], head_dim) for piece in key_pieces]
    half = jax.ShapeDtypeStruct((prompt_len // 2, kv_width), F32)
    own = jax.ShapeDtypeStruct((rows, kv_width), BF16)
    return pl.pallas_call(
        partial(attend_kernel, len(key_pieces)),
        grid=(kv_heads,),
        in_specs=[
            pl.BlockSpec(memory_space=pltpu.SMEM), query_block, query_block, own_block, own_block,
            *piece_blocks, *piece_blocks,
        ],
        out_specs=[query_block, own_block, own_block] + [block(prompt_len // 2, head_dim)] * 4,
        out_shape=[jax.ShapeDtypeStruct((rows, width), BF16), own, own] + [half] * 4,
        compiler_params=LARGE,
        cost_estimate=cost(10 * rows * width * (prompt_len + rows), 10**7),
        name="attend",
    )(length, queries, upstream, keys, values, *key_pieces, *value_pieces)


def in_vmem(kernel, name, outs, arrays, macs=0, scratch=()):
    whole = pl.BlockSpec(memory_space=pltpu.VMEM)
    results = pl.pallas_call(
        kernel,
        in_specs=[whole] * len(arrays),
        out_specs=[whole] * len(outs),
        out_shape=[jax.ShapeDtypeStruct(shape, dtype) for shape, dtype in outs],
        scratch_shapes=scratch,
        compiler_params=SMALL,
        cost_estimate=cost(macs, 3 * 10**6),
        name=name,
    )(*arrays)
    return list(results)


def split_kernel(hidden_ref, *piece_refs):
    depth = piece_refs[0].shape[1]
    group = lax.axis_index("group")
    for k, piece_ref in enumerate(piece_refs):
        start = pl.multiple_of((group ^ k) * depth, depth)
        piece_ref[...] = hidden_ref[:, pl.ds(start, depth)]


def split_pass(hidden, groups):
    tokens, width = hidden.shape
    outs = [((tokens, width // groups), hidden.dtype)] * groups
    return in_vmem(split_kernel, "split_hidden", outs, [hidden])


def turn_kernel(groups, *refs):
    columns, piece_refs, turned = refs[:groups], refs[groups:-1], refs[-1]
    half = piece_refs[0].shape[0] // 2
    resp = lax.axis_index("resp")
    core, chip = resp % 2, resp // 2
    turned[...] = jnp.concatenate([ref[...] for ref in columns], axis=0).astype(F32).T
    for p, piece_ref in enumerate(piece_refs):
        start = (chip ^ p) * (2 * half)
        for i, part in enumerate((core, 1 - core)):
            rows = turned[pl.ds(pl.multiple_of(start + part * half, 8), half)]
            piece_ref[i * half : (i + 1) * half] = rows.astype(BF16)


def turn_pass(columns, chips):
    tokens, depth = columns[0].shape
    every = tokens * len(columns)
    outs = [((depth // chips, every), BF16)] * chips
    scratch = [pltpu.VMEM((depth, every), F32)]
    return in_vmem(partial(turn_kernel, len(columns)), "turn_hidden", outs, columns, 0, scratch)


def hidden_kernel(beside, across, own_ref, *refs):
    grads, refs = refs[: len(across) + 1], refs[len(across) + 1 :]
    near, far = refs[: len(beside)], refs[len(beside) : 2 * len(beside)]
    out_ref, *part_refs = refs[2 * len(beside) :]
    group, core = lax.axis_index("group"), lax.axis_index("resp") % 2
    depth, kv_width = own_ref.shape
    tokens, half = grads[0].shape[0], kv_width // 2
    near_grad = grads[0][:, pl.ds(pl.multiple_of(core * half, half), half)]
    far_grad = grads[0][:, pl.ds(pl.multiple_of((1 - core) * half, half), half)]

    def place(k, block):
        out_ref[:, pl.ds(pl.multiple_of((group ^ k) * depth, depth), depth)] = block

    own = dot(own_ref[...], jnp.concatenate([ref[...] for ref in grads], axis=0), 1, 1).T.astype(BF16)
    place(0, own[:tokens])
    for i, k in enumerate(across):
        part_refs[i][...] = own[(i + 1) * tokens : (i + 2) * tokens]
        place(k, jnp.zeros((tokens, depth), BF16))
    for i, k in enumerate(beside):
        block = dot(near[i][...], near_grad, 1, 1) + dot(far[i][...], far_grad, 1, 1)
        place(k, block.T.astype(BF16))


def hidden_pass(key_pre_grad, first, own, near, far):
    tokens, kv_width = key_pre_grad.shape
    depth = own.shape[0]
    groups = 1 + len(first) + len(near)
    outs = [((tokens, groups * depth), BF16)] + [((tokens, depth), BF16)] * len(first)
    arrays = [own, key_pre_grad, *first.values(), *near.values(), *far.values()]
    kernel = partial(hidden_kernel, list(near), list(first))
    return in_vmem(kernel, "hidden_grad", outs, arrays, tokens * depth * kv_width * groups)


def order_kernel(chips, widths, *refs):
    taken, out_refs = refs[:chips], nested(refs[chips:], [len(parts) for parts in widths for _ in range(2)])
    half = taken[0].shape[0] // 2
    tokens = taken[0].shape[1] // len(widths)
    for k, parts in enumerate(widths):
        for i in range(2):
            rows = slice(i * half, (i + 1) * half)
            columns = [ref[rows, k * tokens : (k + 1) * tokens] for ref in taken]
            for out_ref, count in zip(out_refs[2 * k + i], parts):
                out_ref[...] = jnp.concatenate(columns[:count], axis=1)
                columns = columns[count:]


def order_pass(taken, parts):
    rows, tokens = taken[0].shape
    groups = len(parts)
    outs = [
        ((rows // 2, tokens // groups * count), BF16)
        for counts in parts for _ in range(2) for count in counts
    ]
    arrays = in_vmem(partial(order_kernel, len(taken), parts), "order_columns", outs, taken)
    halves = nested(arrays, [len(counts) for counts in parts for _ in range(2)])
    return halves[0::2], halves[1::2]


def weight_sum(columns, blocks, order):
    total = None
    for k, i in order:
        product = dot(columns[k][i], blocks[k][i])
        total = product if total is None else total + product
    return total


def flat(lists):
    return [item for items in lists for item in items]


def nested(items, counts):
    items = iter(items)
    return [[next(items) for _ in range(count)] for count in counts]


def swap(array, axis, size, distance):
    return lax.ppermute(array, axis, [(i, i ^ distance) for i in range(size)])


def together(*arrays):
    return list(lax.optimization_barrier(arrays))


def spread_near(block, size):
    return [block] + [swap(block, "resp", size, k) for k in range(2, size, 2)]


def spread_far(near, size):
    return [swap(piece, "resp", size, 1) for piece in near]


def pair_sum(near, far, size):
    return near + swap(far, "resp", size, 1)


def chip_parts(near, size, distances):
    rows = near.shape[0] // (size // 2)
    pieces = [near[p * rows : (p + 1) * rows] for p in range(size // 2)]
    return pieces[:1] + [swap(pieces[p].astype(BF16), "resp", size, 2 * p) for p in distances]


def total(parts):
    return sum(part.astype(F32) for part in parts[1:]) + parts[0]


def shards(
    groups, responses, prompt_hidden, key_matrix, key_gain, prompt_token_value,
    resp_query, resp_key, response_value, grad_out, resp_length,
):
    hidden = prompt_hidden[0]
    tokens = hidden.shape[0]
    depth, kv_width = key_matrix.shape
    head_dim = key_gain.shape[0]
    chips = responses // 2
    beside = [k for k in range(1, groups) if k & (k - 1) == 0]
    across = [k for k in range(1, groups) if k & (k - 1)]

    pieces = split_pass(hidden, groups)
    columns = [swap(piece, "group", groups, k) if k else piece for k, piece in enumerate(pieces)]
    partials = [dot(piece, key_matrix) for piece in columns]
    prompt_value, partials[-1] = together(prompt_token_value[0], partials[-1])
    value_near = spread_near(prompt_value, responses)
    key_pre = partials[0]
    for k in range(1, groups):
        key_pre = key_pre + swap(partials[k], "group", groups, k)
    half_width = kv_width // 2
    start = (lax.axis_index("resp") % 2) * half_width
    half_weight = lax.dynamic_slice(key_matrix, (0, start), (depth, half_width))
    half_weight, key_pre = together(half_weight, key_pre)
    weight_near = [swap(half_weight, "group", groups, k) for k in beside]

    prompt_key = norm_keys(key_pre, key_gain).astype(BF16)
    key_near = spread_near(prompt_key, responses)
    value_pieces = value_near + spread_far(value_near, responses)

    taken = turn_pass(columns, chips)
    both = together(*taken, *key_near)
    taken, key_near = both[:chips], both[chips:]
    key_pieces = key_near + spread_far(key_near, responses)
    taken[1:] = [swap(taken[p], "resp", responses, 2 * p) for p in range(1, chips)]

    query_grad, key_grad, value_grad, key_sums, far, value_sums, value_far = attend(
        resp_length, resp_query[0, 0], grad_out[0, 0], key_pieces, value_pieces,
        resp_key[0, 0], response_value[0, 0], head_dim,
    )
    key_sums, far, *both = together(key_sums, far, *taken, *weight_near)
    taken, weight_near = both[:chips], both[chips:]
    key_sums = total(chip_parts(pair_sum(key_sums, far, responses), responses, range(1, chips)))
    value_sums = pair_sum(value_sums, value_far, responses)
    weight_far = [swap(piece, "resp", responses, 1) for piece in weight_near]
    parts = [[1, chips - 1] if k in across else [chips] for k in range(groups)]
    mine, other = order_pass(taken, parts)
    count = len(weight_far)
    key_sums, value_sums, *both = together(
        key_sums, value_sums, *weight_far, *flat(mine), *flat(other)
    )
    weight_far, halves = both[:count], nested(both[count:], [len(counts) for counts in parts + parts])
    mine, other = halves[:groups], halves[groups:]
    _, pullback = jax.vjp(lambda values: norm_keys(values, key_gain), key_pre)
    key_pre_grad = pullback(key_sums)[0].astype(BF16)

    first = {k: swap(key_pre_grad, "group", groups, k) for k in across}
    grads = spread_near(key_pre_grad, responses)
    value_parts = chip_parts(value_sums, responses, (1,))
    value_parts[1], value_sums, *both = together(value_parts[1], value_sums, *grads, *first.values())
    grads, first = both[:chips], dict(zip(first, both[chips:]))
    some, every = jnp.concatenate(grads[1:], axis=0), jnp.concatenate(grads, axis=0)
    grad_hidden, *parts = hidden_pass(
        key_pre_grad, first, key_matrix, dict(zip(beside, weight_near)), dict(zip(beside, weight_far))
    )

    blocks = [[every]] + [None] * (groups - 1)
    for k in beside:
        blocks[k] = [swap(every, "group", groups, k)]
    for k in across:
        blocks[k] = [first[k], swap(some, "group", groups, k)]
    value_parts += chip_parts(value_sums, responses, range(2, chips))[1:]
    for k in across:
        *parts, blocks[k][-1] = together(*parts, blocks[k][-1])
    parts = [swap(part, "group", groups, k) for k, part in zip(across, parts)]
    order = [(0, 0)] + [(k, 0) for k in across] + [(k, 0) for k in beside] + [(k, 1) for k in across]
    other, *value_parts = together(weight_sum(other, blocks, order), *value_parts)
    value_sums = total(value_parts)
    grad_weight = weight_sum(mine, blocks, order) + swap(other, "resp", responses, 1)
    for k, part in zip(across, parts):
        start = (lax.axis_index("group") ^ k) * depth
        grad_hidden = lax.dynamic_update_slice(grad_hidden, part, (0, start))
    return (
        grad_hidden[None],
        grad_weight,
        value_sums.astype(BF16)[None],
        query_grad[None, None],
        key_grad[None, None],
        value_grad[None, None],
    )


def solution(mesh):
    return jax.shard_map(
        partial(shards, mesh.shape["group"], mesh.shape["resp"]),
        mesh=mesh,
        in_specs=(
            P("group", "resp", None),
            P("group", None),
            P(),
            P("group", "resp", None),
            P("group", "resp", None, None),
            P("group", "resp", None, None),
            P("group", "resp", None, None),
            P("group", "resp", None, None),
            P("group", "resp"),
        ),
        out_specs=(
            P("group", "resp", None),
            P(("group", "resp"), None),
            P("group", "resp", None),
            P("group", "resp", None, None),
            P("group", "resp", None, None),
            P("group", "resp", None, None),
        ),
        check_vma=False,
    )
```

```python
from functools import partial

import jax
import jax.numpy as jnp
from jax import lax
from jax.experimental import pallas as pl
from jax.experimental.pallas import tpu as pltpu
from jax.sharding import PartitionSpec as P

F32, BF16 = jnp.float32, jnp.bfloat16
LOG2E = 1.4426950408889634
SMALL = pltpu.CompilerParams(vmem_limit_bytes=16 * 2**20)
LARGE = pltpu.CompilerParams(vmem_limit_bytes=56 * 2**20)


def norm_keys(key_pre, key_gain):
    shaped = key_pre.reshape(key_pre.shape[:-1] + (-1, key_gain.shape[0]))
    inverse = lax.rsqrt(jnp.mean(shaped * shaped, axis=-1, keepdims=True) + 1e-06)
    return (shaped * inverse * key_gain).reshape(key_pre.shape)


def dot(left, right, left_dim=1, right_dim=0):
    dims = (((left_dim,), (right_dim,)), ((), ()))
    return lax.dot_general(left, right, dims, preferred_element_type=F32)


def cost(macs, nbytes):
    return pl.CostEstimate(flops=2 * macs, bytes_accessed=nbytes, transcendentals=0)


def stack_heads(ref, head_dim):
    heads = ref.shape[1] // head_dim
    return jnp.concatenate([ref[:, i * head_dim : (i + 1) * head_dim] for i in range(heads)], axis=0)


def attend_kernel(pieces, length_ref, query_ref, upstream_ref, key_ref, value_ref, *refs):
    key_pieces, value_pieces = refs[:pieces], refs[pieces : 2 * pieces]
    query_grad_ref, key_grad_ref, value_grad_ref, *sum_refs = refs[2 * pieces :]
    rows = query_ref.shape[0]
    own_len, head_dim = key_ref.shape
    heads = query_ref.shape[1] // head_dim
    scale = head_dim ** -0.5
    keys = jnp.concatenate([ref[...] for ref in key_pieces] + [key_ref[...]], axis=0)
    values = jnp.concatenate([ref[...] for ref in value_pieces] + [value_ref[...]], axis=0)
    keys_t, values_t = keys.T, values.T
    prompt_len = keys.shape[0] - own_len
    queries, upstream = stack_heads(query_ref, head_dim), stack_heads(upstream_ref, head_dim)
    stacked = heads * rows
    live = lax.broadcasted_iota(jnp.int32, (stacked, 1), 0) % rows < length_ref[0, 0]
    own = (stacked, own_len)
    visible = lax.broadcasted_iota(jnp.int32, own, 1) <= lax.broadcasted_iota(jnp.int32, own, 0) % rows
    prompt_scores = dot(queries, keys_t[:, :prompt_len])
    own_scores = jnp.where(visible, dot(queries, keys_t[:, prompt_len:]), -jnp.inf)
    row_max = jnp.maximum(
        jnp.max(prompt_scores, axis=1, keepdims=True), jnp.max(own_scores, axis=1, keepdims=True)
    )
    scores = jnp.concatenate([prompt_scores, own_scores], axis=1)
    unit = scale * LOG2E
    exponent = jnp.exp2(scores * unit - row_max * unit)
    dprob = dot(upstream, values_t)
    total = jnp.sum(exponent, axis=1, keepdims=True)
    weighted = jnp.sum(exponent * dprob, axis=1, keepdims=True)
    inverse = jnp.where(live, 1.0 / total, 0.0)
    row_delta = weighted * inverse
    weights = (exponent * inverse).astype(BF16)
    dscore = (exponent * ((dprob - row_delta) * (inverse * scale))).astype(BF16)
    query_grad = dot(dscore, keys).astype(BF16)
    for i in range(heads):
        query_grad_ref[:, i * head_dim : (i + 1) * head_dim] = query_grad[i * rows : (i + 1) * rows]
    key_grad = dot(queries.T, dscore).T
    value_grad = dot(upstream.T, weights).T
    half = prompt_len // 2
    for i, grad in enumerate((key_grad, value_grad)):
        sum_refs[2 * i][...], sum_refs[2 * i + 1][...] = grad[:half], grad[half:prompt_len]
    key_grad_ref[...] = key_grad[prompt_len:].astype(BF16)
    value_grad_ref[...] = value_grad[prompt_len:].astype(BF16)


def attend(length, queries, upstream, key_pieces, value_pieces, keys, values, head_dim):
    rows, width = queries.shape
    kv_width = keys.shape[1]
    kv_heads = kv_width // head_dim
    prompt_len = sum(piece.shape[0] for piece in key_pieces)

    def block(rows, columns):
        return pl.BlockSpec((rows, columns), lambda i: (0, i))

    query_block, own_block = block(rows, width // kv_heads), block(rows, head_dim)
    piece_blocks = [block(piece.shape[0], head_dim) for piece in key_pieces]
    half = jax.ShapeDtypeStruct((prompt_len // 2, kv_width), F32)
    own = jax.ShapeDtypeStruct((rows, kv_width), BF16)
    return pl.pallas_call(
        partial(attend_kernel, len(key_pieces)),
        grid=(kv_heads,),
        in_specs=[
            pl.BlockSpec(memory_space=pltpu.SMEM), query_block, query_block, own_block, own_block,
            *piece_blocks, *piece_blocks,
        ],
        out_specs=[query_block, own_block, own_block] + [block(prompt_len // 2, head_dim)] * 4,
        out_shape=[jax.ShapeDtypeStruct((rows, width), BF16), own, own] + [half] * 4,
        compiler_params=LARGE,
        cost_estimate=cost(10 * rows * width * (prompt_len + rows), 10**7),
        name="attend",
    )(length, queries, upstream, keys, values, *key_pieces, *value_pieces)


def in_vmem(kernel, name, outs, arrays, macs=0, scratch=()):
    whole = pl.BlockSpec(memory_space=pltpu.VMEM)
    results = pl.pallas_call(
        kernel,
        in_specs=[whole] * len(arrays),
        out_specs=[whole] * len(outs),
        out_shape=[jax.ShapeDtypeStruct(shape, dtype) for shape, dtype in outs],
        scratch_shapes=scratch,
        compiler_params=SMALL,
        cost_estimate=cost(macs, 3 * 10**6),
        name=name,
    )(*arrays)
    return list(results)


def split_kernel(hidden_ref, *piece_refs):
    depth = piece_refs[0].shape[1]
    group = lax.axis_index("group")
    for k, piece_ref in enumerate(piece_refs):
        start = pl.multiple_of((group ^ k) * depth, depth)
        piece_ref[...] = hidden_ref[:, pl.ds(start, depth)]


def split_pass(hidden, groups):
    tokens, width = hidden.shape
    outs = [((tokens, width // groups), hidden.dtype)] * groups
    return in_vmem(split_kernel, "split_hidden", outs, [hidden])


def turn_kernel(groups, *refs):
    columns, piece_refs, turned = refs[:groups], refs[groups:-1], refs[-1]
    half = piece_refs[0].shape[0] // 2
    resp = lax.axis_index("resp")
    core, chip = resp % 2, resp // 2
    turned[...] = jnp.concatenate([ref[...] for ref in columns], axis=0).astype(F32).T
    for p, piece_ref in enumerate(piece_refs):
        start = (chip ^ p) * (2 * half)
        for i, part in enumerate((core, 1 - core)):
            rows = turned[pl.ds(pl.multiple_of(start + part * half, 8), half)]
            piece_ref[i * half : (i + 1) * half] = rows.astype(BF16)


def turn_pass(columns, chips):
    tokens, depth = columns[0].shape
    every = tokens * len(columns)
    outs = [((depth // chips, every), BF16)] * chips
    scratch = [pltpu.VMEM((depth, every), F32)]
    return in_vmem(partial(turn_kernel, len(columns)), "turn_hidden", outs, columns, 0, scratch)


def hidden_kernel(beside, across, own_ref, *refs):
    grads, refs = refs[: len(across) + 1], refs[len(across) + 1 :]
    near, far = refs[: len(beside)], refs[len(beside) : 2 * len(beside)]
    out_ref, *part_refs = refs[2 * len(beside) :]
    group, core = lax.axis_index("group"), lax.axis_index("resp") % 2
    depth, kv_width = own_ref.shape
    tokens, half = grads[0].shape[0], kv_width // 2
    near_grad = grads[0][:, pl.ds(pl.multiple_of(core * half, half), half)]
    far_grad = grads[0][:, pl.ds(pl.multiple_of((1 - core) * half, half), half)]

    def place(k, block):
        out_ref[:, pl.ds(pl.multiple_of((group ^ k) * depth, depth), depth)] = block

    own = dot(own_ref[...], jnp.concatenate([ref[...] for ref in grads], axis=0), 1, 1).T.astype(BF16)
    place(0, own[:tokens])
    for i, k in enumerate(across):
        part_refs[i][...] = own[(i + 1) * tokens : (i + 2) * tokens]
        place(k, jnp.zeros((tokens, depth), BF16))
    for i, k in enumerate(beside):
        block = dot(near[i][...], near_grad, 1, 1) + dot(far[i][...], far_grad, 1, 1)
        place(k, block.T.astype(BF16))


def hidden_pass(key_pre_grad, first, own, near, far):
    tokens, kv_width = key_pre_grad.shape
    depth = own.shape[0]
    groups = 1 + len(first) + len(near)
    outs = [((tokens, groups * depth), BF16)] + [((tokens, depth), BF16)] * len(first)
    arrays = [own, key_pre_grad, *first.values(), *near.values(), *far.values()]
    kernel = partial(hidden_kernel, list(near), list(first))
    return in_vmem(kernel, "hidden_grad", outs, arrays, tokens * depth * kv_width * groups)


def order_kernel(chips, widths, *refs):
    taken, out_refs = refs[:chips], nested(refs[chips:], [len(parts) for parts in widths for _ in range(2)])
    half = taken[0].shape[0] // 2
    tokens = taken[0].shape[1] // len(widths)
    for k, parts in enumerate(widths):
        for i in range(2):
            rows = slice(i * half, (i + 1) * half)
            columns = [ref[rows, k * tokens : (k + 1) * tokens] for ref in taken]
            for out_ref, count in zip(out_refs[2 * k + i], parts):
                out_ref[...] = jnp.concatenate(columns[:count], axis=1)
                columns = columns[count:]


def order_pass(taken, parts):
    rows, tokens = taken[0].shape
    groups = len(parts)
    outs = [
        ((rows // 2, tokens // groups * count), BF16)
        for counts in parts for _ in range(2) for count in counts
    ]
    arrays = in_vmem(partial(order_kernel, len(taken), parts), "order_columns", outs, taken)
    halves = nested(arrays, [len(counts) for counts in parts for _ in range(2)])
    return halves[0::2], halves[1::2]


def weight_sum(columns, blocks, order):
    total = None
    for k, i in order:
        product = dot(columns[k][i], blocks[k][i])
        total = product if total is None else total + product
    return total


def flat(lists):
    return [item for items in lists for item in items]


def nested(items, counts):
    items = iter(items)
    return [[next(items) for _ in range(count)] for count in counts]


def swap(array, axis, size, distance):
    return lax.ppermute(array, axis, [(i, i ^ distance) for i in range(size)])


def together(*arrays):
    return list(lax.optimization_barrier(arrays))


def spread_near(block, size):
    return [block] + [swap(block, "resp", size, k) for k in range(2, size, 2)]


def spread_far(near, size):
    return [swap(piece, "resp", size, 1) for piece in near]


def pair_sum(near, far, size):
    return near + swap(far, "resp", size, 1)


def chip_parts(near, size, distances):
    rows = near.shape[0] // (size // 2)
    pieces = [near[p * rows : (p + 1) * rows] for p in range(size // 2)]
    return pieces[:1] + [swap(pieces[p].astype(BF16), "resp", size, 2 * p) for p in distances]


def total(parts):
    return sum(part.astype(F32) for part in parts[1:]) + parts[0]


def shards(
    groups, responses, prompt_hidden, key_matrix, key_gain, prompt_token_value,
    resp_query, resp_key, response_value, grad_out, resp_length,
):
    hidden = prompt_hidden[0]
    tokens = hidden.shape[0]
    depth, kv_width = key_matrix.shape
    head_dim = key_gain.shape[0]
    chips = responses // 2
    beside = [k for k in range(1, groups) if k & (k - 1) == 0]
    across = [k for k in range(1, groups) if k & (k - 1)]

    pieces = split_pass(hidden, groups)
    columns = [swap(piece, "group", groups, k) if k else piece for k, piece in enumerate(pieces)]
    partials = [dot(piece, key_matrix) for piece in columns]
    prompt_value, partials[-1] = together(prompt_token_value[0], partials[-1])
    value_near = spread_near(prompt_value, responses)
    key_pre = partials[0]
    for k in range(1, groups):
        key_pre = key_pre + swap(partials[k], "group", groups, k)
    half_width = kv_width // 2
    start = (lax.axis_index("resp") % 2) * half_width
    half_weight = lax.dynamic_slice(key_matrix, (0, start), (depth, half_width))
    half_weight, key_pre = together(half_weight, key_pre)
    weight_near = [swap(half_weight, "group", groups, k) for k in beside]

    prompt_key = norm_keys(key_pre, key_gain).astype(BF16)
    key_near = spread_near(prompt_key, responses)
    value_pieces = value_near + spread_far(value_near, responses)

    taken = turn_pass(columns, chips)
    both = together(*taken, *key_near)
    taken, key_near = both[:chips], both[chips:]
    key_pieces = key_near + spread_far(key_near, responses)
    taken[1:] = [swap(taken[p], "resp", responses, 2 * p) for p in range(1, chips)]

    query_grad, key_grad, value_grad, key_sums, far, value_sums, value_far = attend(
        resp_length, resp_query[0, 0], grad_out[0, 0], key_pieces, value_pieces,
        resp_key[0, 0], response_value[0, 0], head_dim,
    )
    key_sums, far, *both = together(key_sums, far, *taken, *weight_near)
    taken, weight_near = both[:chips], both[chips:]
    key_sums = total(chip_parts(pair_sum(key_sums, far, responses), responses, range(1, chips)))
    value_sums = pair_sum(value_sums, value_far, responses)
    weight_far = [swap(piece, "resp", responses, 1) for piece in weight_near]
    parts = [[1, chips - 1] if k in across else [chips] for k in range(groups)]
    mine, other = order_pass(taken, parts)
    count = len(weight_far)
    key_sums, value_sums, *both = together(
        key_sums, value_sums, *weight_far, *flat(mine), *flat(other)
    )
    weight_far, halves = both[:count], nested(both[count:], [len(counts) for counts in parts + parts])
    mine, other = halves[:groups], halves[groups:]
    _, pullback = jax.vjp(lambda values: norm_keys(values, key_gain), key_pre)
    key_pre_grad = pullback(key_sums)[0].astype(BF16)

    first = {k: swap(key_pre_grad, "group", groups, k) for k in across}
    grads = spread_near(key_pre_grad, responses)
    value_parts = chip_parts(value_sums, responses, (1,))
    value_parts[1], value_sums, *both = together(value_parts[1], value_sums, *grads, *first.values())
    grads, first = both[:chips], dict(zip(first, both[chips:]))
    some, every = jnp.concatenate(grads[1:], axis=0), jnp.concatenate(grads, axis=0)
    grad_hidden, *parts = hidden_pass(
        key_pre_grad, first, key_matrix, dict(zip(beside, weight_near)), dict(zip(beside, weight_far))
    )

    blocks = [[every]] + [None] * (groups - 1)
    for k in beside:
        blocks[k] = [swap(every, "group", groups, k)]
    for k in across:
        blocks[k] = [first[k], swap(some, "group", groups, k)]
    value_parts += chip_parts(value_sums, responses, range(2, chips))[1:]
    for k in across:
        *parts, blocks[k][-1] = together(*parts, blocks[k][-1])
    parts = [swap(part, "group", groups, k) for k, part in zip(across, parts)]
    order = [(0, 0)] + [(k, 0) for k in across] + [(k, 0) for k in beside] + [(k, 1) for k in across]
    other, *value_parts = together(weight_sum(other, blocks, order), *value_parts)
    value_sums = total(value_parts)
    grad_weight = weight_sum(mine, blocks, order) + swap(other, "resp", responses, 1)
    for k, part in zip(across, parts):
        start = (lax.axis_index("group") ^ k) * depth
        grad_hidden = lax.dynamic_update_slice(grad_hidden, part, (0, start))
    return (
        grad_hidden[None],
        grad_weight,
        value_sums.astype(BF16)[None],
        query_grad[None, None],
        key_grad[None, None],
        value_grad[None, None],
    )


def solution(mesh):
    return jax.shard_map(
        partial(shards, mesh.shape["group"], mesh.shape["resp"]),
        mesh=mesh,
        in_specs=(
            P("group", "resp", None),
            P("group", None),
            P(),
            P("group", "resp", None),
            P("group", "resp", None, None),
            P("group", "resp", None, None),
            P("group", "resp", None, None),
            P("group", "resp", None, None),
            P("group", "resp"),
        ),
        out_specs=(
            P("group", "resp", None),
            P(("group", "resp"), None),
            P("group", "resp", None),
            P("group", "resp", None, None),
            P("group", "resp", None, None),
            P("group", "resp", None, None),
        ),
        check_vma=False,
    )
```
